32 devices in a mesh: dp: 8 (over z, y), section: 4 (over x, core).
Axes of the slice: x: 2, y: 2, z: 4, core: 2. Of those that a mesh axis runs over, the one named last changes fastest.
Arguments:
- inputs: bfloat16 [8192, 768], P('dp'), may hold values from -8 to 8
- cotangent_first: bfloat16 [8192, 768], P('dp'), may hold values from -6 to 6
- cotangent_second: bfloat16 [8192, 768], P('dp'), may hold values from -6 to 6
- segment_ids: int32 [8192], P('dp'), may hold values from -1 to 5, as said below
- joint_projection: bfloat16 [1536, 2304], P('section'), may hold values from -0.21875 to 0.21875
- mixing_weight: bfloat16 [1536, 768], P('section'), may hold values from -0.875 to 0.875
- gated_weight: bfloat16 [1536, 6144], P('section'), may hold values from -0.21875 to 0.21875
- down_weight: bfloat16 [6144, 768], P('section'), may hold values from -0.109375 to 0.109375
- norm_gain: float32 [4, 768], P('section'), may hold values from 0.5 to 1.5
- norm_bias: float32 [4, 768], P('section'), may hold values from -1.75 to 1.75
Outputs:
- first_output: bfloat16 [8192, 768], P(('dp', 'section'))
- second_output: bfloat16 [8192, 768], P(('dp', 'section'))
- input_gradient: bfloat16 [8192, 768], P(('dp', 'section'))
- middle_gradient: bfloat16 [8192, 768], P(('dp', 'section'))
- joint_gradient: float32 [1536, 2304], P('section')
- mixing_gradient: float32 [1536, 768], P('section')
- gated_gradient: float32 [1536, 6144], P('section')
- down_gradient: float32 [6144, 768], P('section')
- gain_gradient: float32 [4, 768], P('section')
- bias_gradient: float32 [4, 768], P('section')
- magnitudes: float32 [2, 4], replicated
The draws below stay inside these ranges and needn't reach their ends.
Inputs may be any that keep to these rules, and one draw needn't show every extreme that they name: `segment_ids`: within each aligned block of 128 positions the numbers start at 0 and rise by one at each new sequence; every sequence is 20 positions or longer; positions after a block's last sequence hold -1.
All inputs are finite; a program needn't handle non-finite values.
Results may differ from the reference program's by a relative error of at most 0.028.
The reference program's roundings to bfloat16 on the way count: a program that leaves them out, or rounds other values in their place, can miss the bound.
Values may be sent and summed in bfloat16 or wider, within the bound.
A program may use at most 256 MiB of HBM per device.

```python
import math
import jax
import jax.numpy as jnp
from jax import lax

D = 768
HEADS = 12
FF = 3072
BLOCK = 128
LAYERS = 2
QKV = 2304
TOKENS = 8192


def draw_inputs(key, part):
    key = jax.random.fold_in(key, 7)
    rising = 0.5 + jnp.arange(TOKENS, dtype=jnp.float32) / TOKENS
    drawn = jax.random.normal(key, (TOKENS, D), jnp.float32) * rising[:, None]
    return jnp.clip(drawn, -8.0, 8.0).astype(jnp.bfloat16)


def draw_segment_ids(key, part):
    key = jax.random.fold_in(key, 13)
    blocks = TOKENS // BLOCK
    lengths = jax.random.randint(key, (blocks, 6), 20, BLOCK + 1)
    first_block = (jnp.arange(blocks) == 0)[:, None]
    lengths = jnp.where(first_block, 20, lengths)
    boundaries = jnp.cumsum(lengths, axis=1)
    positions = jnp.arange(BLOCK)
    valid_end = jnp.max(jnp.where(boundaries <= BLOCK, boundaries, 0), axis=1)
    numbers = jnp.sum((boundaries[:, None, :] <= positions[None, :, None]).astype(jnp.int32), axis=-1)
    numbers = jnp.where(positions[None, :] < valid_end[:, None], numbers, -1)
    return numbers.reshape(TOKENS).astype(jnp.int32)


def level_of(stream_key, dims, shards, least, top_value):
    factor_of = 1.0
    for axis_at, parts in shards:
        steps = jax.random.uniform(jax.random.fold_in(jax.random.fold_in(stream_key, 6), axis_at), (parts,), jnp.float32, least / len(shards), top_value / len(shards))
        factor_of = factor_of * jnp.repeat(jnp.exp(steps), dims[axis_at] // parts).reshape((-1,) + (1,) * (len(dims) - 1 - axis_at))
    return factor_of


def bell_draw(key, shape, scale, bound, shards=(), kind=jnp.bfloat16):
    result = jax.random.normal(key, shape, jnp.float32) * scale
    if len(shards) > 0:
        result = level_of(key, shape, shards, -0.22, 0.18) * result
    return jnp.clip(result, min=-bound, max=bound).astype(kind)


def setup_inputs(seed: int = 0) -> dict:
    streams_of = jax.random.split(jax.random.key(seed), 11)
    return {
        "inputs": draw_inputs(jax.random.fold_in(streams_of[10], 71), 0),
        "cotangent_first": bell_draw(streams_of[1], (TOKENS, D), 1.0, 6.0, ((0, 8),)),
        "cotangent_second": bell_draw(streams_of[2], (TOKENS, D), 1.0, 6.0, ((0, 8),)),
        "segment_ids": draw_segment_ids(jax.random.fold_in(streams_of[10], 71), 0),
        "joint_projection": bell_draw(streams_of[4], (LAYERS * D, QKV), D ** -0.5, 0.21875, ((0, 4),)),
        "mixing_weight": bell_draw(streams_of[5], (LAYERS * D, D), (D // 16) ** -0.5, 0.875, ((0, 4),)),
        "gated_weight": bell_draw(streams_of[6], (LAYERS * D, 2 * FF), D ** -0.5, 0.21875, ((0, 4),)),
        "down_weight": bell_draw(streams_of[7], (LAYERS * FF, D), FF ** -0.5, 0.109375, ((0, 4),)),
        "norm_gain": jnp.clip(1.0 + 0.1 * jax.random.normal(streams_of[8], (2 * LAYERS, D), jnp.float32), 0.5, 1.5),
        "norm_bias": bell_draw(streams_of[9], (2 * LAYERS, D), 0.3, 1.75, ((0, 4),), jnp.float32),
    }


EPSILON = 1e-05
MASKED = -1e+30
HIGHEST = lax.Precision.HIGHEST

@jax.custom_vjp
def low(v):
    return lax.optimization_barrier(v.astype(jnp.bfloat16)).astype(jnp.float32)

@jax.custom_vjp
def low_back(v):
    return v

def low_keep(v):
    return (low(v), None)

def low_pass(kept, grad):
    return (grad,)

def back_keep(v):
    return (v, None)

def back_low(kept, grad):
    return (low(grad),)
low.defvjp(low_keep, low_pass)
low_back.defvjp(back_keep, back_low)

def alibi_slopes(heads_count):
    closest = 1 << heads_count.bit_length() - 1
    first_slope = 2.0 ** (-8.0 / closest)
    slopes = [first_slope ** (power_index + 1) for power_index in range(closest)]
    if closest < heads_count:
        double_slope = 2.0 ** (-8.0 / (2 * closest))
        extra_slopes = [double_slope ** (power_index + 1) for power_index in range(2 * closest)]
        slopes = slopes + extra_slopes[0::2][:heads_count - closest]
    return jnp.array(slopes, jnp.float32)

def alibi_bias(heads_count):
    positions = jnp.arange(BLOCK)
    distance = jnp.abs(positions[:, None] - positions[None, :]).astype(jnp.float32)
    return -alibi_slopes(heads_count)[:, None, None] * distance

def normalize(summed_rows, gain_vector, bias_vector):
    center = summed_rows - lax.optimization_barrier(jnp.mean(summed_rows, axis=-1, keepdims=True))
    spread = lax.optimization_barrier(jnp.mean(center * center, axis=-1, keepdims=True))
    scaled = center * lax.rsqrt(spread + EPSILON)
    return scaled * gain_vector + bias_vector

def attention_layer(inputs, segments, joint_weight, mixing_matrix, gain_vector, bias_vector):
    total_rows = inputs.shape[0]
    blocks = total_rows // BLOCK
    head_size = D // HEADS
    joint_rows = low_back(low(jnp.dot(inputs, joint_weight, precision=HIGHEST)))
    split_heads = joint_rows.reshape(blocks, BLOCK, 3, HEADS, head_size)
    queries = split_heads[:, :, 0]
    keys_part = split_heads[:, :, 1]
    values_part = split_heads[:, :, 2]
    raw_scores = jnp.einsum('bqhd,bkhd->bhqk', queries, keys_part, precision=HIGHEST)
    scores = low_back(raw_scores * head_size ** (-0.5) + alibi_bias(HEADS)[None])
    segment_rows = segments.reshape(blocks, BLOCK)
    same_segment = segment_rows[:, None, :, None] == segment_rows[:, None, None, :]
    weights_soft = jax.nn.softmax(jnp.where(same_segment, scores, MASKED), axis=-1)
    mixed_rows = jnp.einsum('bhqk,bkhd->bqhd', low(weights_soft), values_part, precision=HIGHEST)
    mixed_rows = low_back(low(mixed_rows.reshape(total_rows, D)))
    branch = low_back(jnp.dot(mixed_rows, mixing_matrix, precision=HIGHEST))
    return (low(normalize(inputs + branch, gain_vector, bias_vector)), branch)

def feedforward_layer(inputs, gated_matrix, down_matrix, gain_vector, bias_vector):
    gate_up = low_back(jnp.dot(inputs, gated_matrix, precision=HIGHEST))
    gate_part = gate_up[:, :FF]
    up_part = gate_up[:, FF:]
    hidden = low(jax.nn.gelu(gate_part, approximate=False) * up_part)
    branch = low_back(jnp.dot(hidden, down_matrix, precision=HIGHEST))
    return (low(normalize(inputs + branch, gain_vector, bias_vector)), branch)

def reference(inputs, cotangent_first, cotangent_second, segment_ids, joint_projection, mixing_weight, gated_weight, down_weight, norm_gain, norm_bias):
    total_blocks = TOKENS // BLOCK
    group_blocks = math.gcd(total_blocks, 32)
    groups = total_blocks // group_blocks
    group_rows = group_blocks * BLOCK
    valid = (segment_ids >= 0).astype(jnp.float32)
    segment_groups = segment_ids.reshape(groups, group_rows)
    valid_groups = valid.reshape(groups, group_rows)

    def forward(start_rows, middle_rows, joint_all, mixing_all, gated_all, down_all, gain_all, bias_all):

        def one_group(totals, pieces):
            first_piece, middle_piece, segments, valid_rows = pieces
            section_in = low_back(first_piece)
            residual_terms = []
            branch_terms = []
            layer_outs = []
            for layer_index in range(LAYERS):
                attended, branch = attention_layer(section_in, segments, joint_all[layer_index * D:(layer_index + 1) * D], mixing_all[layer_index * D:(layer_index + 1) * D], gain_all[2 * layer_index], bias_all[2 * layer_index])
                residual_terms.append(jnp.sum(valid_rows * lax.optimization_barrier(jnp.sum(section_in * section_in, axis=-1))))
                branch_terms.append(jnp.sum(valid_rows * lax.optimization_barrier(jnp.sum(branch * branch, axis=-1))))
                attended = low_back(attended)
                fed_out, branch = feedforward_layer(attended, gated_all[layer_index * D:(layer_index + 1) * D], down_all[layer_index * FF:(layer_index + 1) * FF], gain_all[2 * layer_index + 1], bias_all[2 * layer_index + 1])
                residual_terms.append(jnp.sum(valid_rows * lax.optimization_barrier(jnp.sum(attended * attended, axis=-1))))
                branch_terms.append(jnp.sum(valid_rows * lax.optimization_barrier(jnp.sum(branch * branch, axis=-1))))
                if layer_index == 0:
                    section_in = low_back(fed_out + middle_piece)
                else:
                    section_in = low_back(fed_out)
                layer_outs.append(section_in)
            step_totals = jnp.stack([jnp.stack(residual_terms), jnp.stack(branch_terms)])
            return (totals + step_totals, (layer_outs[0], layer_outs[1]))
        totals_start = jnp.zeros((2, 2 * LAYERS), jnp.float32)
        totals, layer_rows = lax.scan(jax.checkpoint(one_group), totals_start, (start_rows.reshape(groups, group_rows, D), middle_rows.reshape(groups, group_rows, D), segment_groups, valid_groups))
        return (layer_rows[0].reshape(TOKENS, D), layer_rows[1].reshape(TOKENS, D), totals)
    primal_inputs = (inputs.astype(jnp.float32), jnp.zeros((TOKENS, D), jnp.float32), joint_projection.astype(jnp.float32), mixing_weight.astype(jnp.float32), gated_weight.astype(jnp.float32), down_weight.astype(jnp.float32), norm_gain.astype(jnp.float32), norm_bias.astype(jnp.float32))
    primal_outputs, pullback = jax.vjp(forward, *primal_inputs)
    first_rows, second_rows, totals = primal_outputs
    gradients = pullback((valid[:, None] * cotangent_first.astype(jnp.float32), valid[:, None] * cotangent_second.astype(jnp.float32), jnp.zeros_like(totals)))
    valid_count = jnp.sum(valid)
    magnitudes = jnp.sqrt(totals / (valid_count * D))
    return (first_rows.astype(jnp.bfloat16), second_rows.astype(jnp.bfloat16), gradients[0].astype(jnp.bfloat16), gradients[1].astype(jnp.bfloat16), gradients[2], gradients[3], gradients[4], gradients[5], gradients[6], gradients[7], magnitudes)
```

```python
import functools

import jax
import jax.numpy as jnp
from jax import lax
from jax.experimental import pallas as pl
from jax.experimental.pallas import tpu as pltpu
from jax.sharding import PartitionSpec as P

D = 768
HEADS = 12
HEAD = D // HEADS
FF = 3072
BLOCK = 128
HALF = D // 2
MICRO = 2

EPSILON = 1e-05
MASKED = -1e30
ROOT_HALF = 0.7071067811865476
ROOT_TWO_PI = 2.5066282746310002
SCALE = HEAD**-0.5

MESH = pl.DeviceIdType.MESH
PIECES = 32
PIECE = 384
SIDE = 112
RAIL = 160
WIDTH = 384
AHEAD = 4
LAG = 2


def reduce_kernel(
    lines, mine_ref, theirs_ref, out_ref,
    total, grown, landed, from_side, from_inner, from_low, from_high, from_root,
    load_sem, store_sem, core_send, core_recv, side_send, side_recv, inner_send, inner_recv,
    up_send, low_recv, high_recv, root_send, root_recv,
    line_send, line_recv, back_send, back_recv, low_send, high_send, rail_recv,
):
    dp, section = lax.axis_index("dp"), lax.axis_index("section")
    y, z = lax.rem(dp, 2), lax.div(dp, 2)
    half = lines // 2
    mid = half - 1
    partner = (dp, section + 1 - 2 * lax.rem(section, 2))
    across = (dp + 1 - 2 * y, section)
    below, above = (dp - 2, section), (dp + 2, section)
    lower = z < half
    depth = jnp.where(lower, z, lines - 1 - z)
    has_low, has_high = z > 0, z < lines - 1
    my_rows = pl.ds(pl.multiple_of(y * SIDE, 8), SIDE)
    other_rows = pl.ds(pl.multiple_of((1 - y) * SIDE, 8), SIDE)
    rail_rows = pl.ds(2 * SIDE, RAIL)
    last = PIECES - 1

    def remote(src, dst, send, recv, device):
        return pltpu.make_async_remote_copy(
            src_ref=src, dst_ref=dst, send_sem=send, recv_sem=recv, device_id=device, device_id_type=MESH
        )

    def arrived(dst, sem):
        pltpu.make_async_copy(dst, dst, sem).wait()

    barrier = pltpu.get_barrier_semaphore()
    pl.semaphore_signal(barrier, inc=1, device_id=partner, device_id_type=MESH)
    pl.semaphore_signal(barrier, inc=1, device_id=across, device_id_type=MESH)

    @pl.when(has_low)
    def _():
        pl.semaphore_signal(barrier, inc=1, device_id=below, device_id_type=MESH)

    @pl.when(has_high)
    def _():
        pl.semaphore_signal(barrier, inc=1, device_id=above, device_id_type=MESH)

    pl.semaphore_wait(barrier, 2 + has_low.astype(jnp.int32) + has_high.astype(jnp.int32))

    def to_partner(b):
        return remote(theirs_ref.at[b], landed.at[b], core_send.at[b], core_recv.at[b], partner)

    def load(b):
        return pltpu.make_async_copy(mine_ref.at[b], grown.at[b], load_sem.at[b])

    def store(b):
        return pltpu.make_async_copy(total.at[b], out_ref.at[b], store_sem.at[b])

    def start_all(b, carry):
        to_partner(b).start()
        load(b).start()
        return carry

    lax.fori_loop(0, AHEAD, start_all, 0)

    def add(dst, rows, b, *others):
        value = grown[b, rows].astype(jnp.float32)
        for other in others:
            value = value + other.astype(jnp.float32)
        dst[b, rows] = value.astype(jnp.bfloat16)

    def when(active, b):
        return pl.when(active & (b >= 0) & (b < PIECES))

    def root_of(b):
        odd = lax.rem(b, 2)
        return jnp.where(b < PIECES // 2, odd * (lines - 1), mid + odd)

    def step(i, carry):
        b1 = i - LAG * (1 + depth)

        @when(True, b1)
        def _():
            arrived(from_side.at[b1], side_recv.at[b1])

            @pl.when(depth == 0)
            def _():
                add(grown, my_rows, b1, from_side[b1])

            @pl.when(depth > 0)
            def _():
                arrived(from_inner.at[0, b1], inner_recv.at[0, b1])
                add(grown, my_rows, b1, from_side[b1], from_inner[0, b1])

            inward = (jnp.where(lower, dp + 2, dp - 2), section)
            slot = (depth == mid).astype(jnp.int32)
            remote(
                grown.at[b1, my_rows], from_inner.at[slot, b1], inner_send.at[b1], inner_recv.at[slot, b1], inward
            ).start()

        b2 = i - LAG * (2 + mid + mid - depth)

        @when(True, b2)
        def _():
            @pl.when(depth == mid)
            def _():
                arrived(from_inner.at[1, b2], inner_recv.at[1, b2])
                add(total, my_rows, b2, from_inner[1, b2])

            @pl.when(depth < mid)
            def _():
                arrived(total.at[b2, my_rows], line_recv.at[b2])

            @pl.when(depth > 0)
            def _():
                outward = (jnp.where(lower, dp - 2, dp + 2), section)
                remote(total.at[b2, my_rows], total.at[b2, my_rows], line_send.at[b2], line_recv.at[b2], outward).start()

            remote(total.at[b2, my_rows], total.at[b2, my_rows], back_send.at[b2], back_recv.at[b2], across).start()

        b3 = i - LAG * (3 + mid + mid - depth)

        @when(True, b3)
        def _():
            arrived(total.at[b3, other_rows], back_recv.at[b3])

        for early in (True, False):
            for odd in (0, 1):
                root = (odd * (lines - 1)) if early else mid + odd
                height = max(root, lines - 1 - root)
                distance = jnp.abs(z - root)

                def mine(b, root=root):
                    return (root_of(b) == root) & (lax.rem(b + 4 * PIECES, 2) == odd)

                hop = jnp.where(z < root, z, jnp.where(z > root, lines - 1 - z, height))
                c1 = i - LAG * hop

                @when((z != root) & (hop > 0) & mine(c1), c1)
                def _(root=root, c1=c1):
                    @pl.when(z < root)
                    def _():
                        arrived(from_low.at[c1], low_recv.at[c1])
                        add(grown, rail_rows, c1, from_low[c1])
                        remote(grown.at[c1, rail_rows], from_low.at[c1], up_send.at[c1], low_recv.at[c1], above).start()

                    @pl.when(z > root)
                    def _():
                        arrived(from_high.at[c1], high_recv.at[c1])
                        add(grown, rail_rows, c1, from_high[c1])
                        remote(grown.at[c1, rail_rows], from_high.at[c1], up_send.at[c1], high_recv.at[c1], below).start()

                @when((z == root) & mine(c1), c1)
                def _(root=root, c1=c1):
                    if root > 0:
                        arrived(from_low.at[c1], low_recv.at[c1])
                    if root < lines - 1:
                        arrived(from_high.at[c1], high_recv.at[c1])
                    parts = ([from_low[c1]] if root > 0 else []) + ([from_high[c1]] if root < lines - 1 else [])
                    add(grown, rail_rows, c1, *parts)
                    remote(grown.at[c1, rail_rows], from_root.at[c1], root_send.at[c1], root_recv.at[c1], across).start()

                c2 = i - LAG * (height + 1 + distance)

                @when(mine(c2), c2)
                def _(root=root, c2=c2):
                    @pl.when(z == root)
                    def _():
                        arrived(from_root.at[c2], root_recv.at[c2])
                        add(total, rail_rows, c2, from_root[c2])

                    @pl.when(z != root)
                    def _():
                        arrived(total.at[c2, rail_rows], rail_recv.at[c2])

                    @pl.when(has_low & (z <= root))
                    def _():
                        remote(total.at[c2, rail_rows], total.at[c2, rail_rows], low_send.at[c2], rail_recv.at[c2], below).start()

                    @pl.when(has_high & (z >= root))
                    def _():
                        remote(total.at[c2, rail_rows], total.at[c2, rail_rows], high_send.at[c2], rail_recv.at[c2], above).start()

        b4 = i - LAG * (2 * lines - 1)

        @when(True, b4)
        def _():
            store(b4).start()

        b0 = i

        @when(True, b0)
        def _():
            @pl.when(b0 + AHEAD < PIECES)
            def _():
                start_all(b0 + AHEAD, 0)

            load(b0).wait()
            to_partner(b0).wait_recv()
            grown[b0] = (grown[b0].astype(jnp.float32) + landed[b0].astype(jnp.float32)).astype(jnp.bfloat16)
            remote(grown.at[b0, other_rows], from_side.at[b0], side_send.at[b0], side_recv.at[b0], across).start()
            root = root_of(b0)

            @pl.when((z == 0) & (root != 0))
            def _():
                remote(grown.at[b0, rail_rows], from_low.at[b0], up_send.at[b0], low_recv.at[b0], above).start()

            @pl.when((z == lines - 1) & (root != lines - 1))
            def _():
                remote(grown.at[b0, rail_rows], from_high.at[b0], up_send.at[b0], high_recv.at[b0], below).start()

        return carry

    lax.fori_loop(0, PIECES + LAG * (2 * lines - 1), step, 0)

    def finish(b, carry):
        store(b).wait()
        to_partner(b).wait_send()
        root = root_of(b)
        pltpu.make_async_copy(grown.at[b, other_rows], grown.at[b, other_rows], side_send.at[b]).wait()
        pltpu.make_async_copy(grown.at[b, my_rows], grown.at[b, my_rows], inner_send.at[b]).wait()
        pltpu.make_async_copy(total.at[b, my_rows], total.at[b, my_rows], back_send.at[b]).wait()

        @pl.when(depth > 0)
        def _():
            pltpu.make_async_copy(total.at[b, my_rows], total.at[b, my_rows], line_send.at[b]).wait()

        @pl.when(z != root)
        def _():
            pltpu.make_async_copy(grown.at[b, rail_rows], grown.at[b, rail_rows], up_send.at[b]).wait()

        @pl.when(z == root)
        def _():
            pltpu.make_async_copy(grown.at[b, rail_rows], grown.at[b, rail_rows], root_send.at[b]).wait()

        @pl.when(has_low & (z <= root))
        def _():
            pltpu.make_async_copy(total.at[b, rail_rows], total.at[b, rail_rows], low_send.at[b]).wait()

        @pl.when(has_high & (z >= root))
        def _():
            pltpu.make_async_copy(total.at[b, rail_rows], total.at[b, rail_rows], high_send.at[b]).wait()

        return carry

    lax.fori_loop(0, PIECES, finish, 0)


def reduce_gradients(lines, mine, theirs):
    bf = jnp.bfloat16
    sems = lambda *s: pltpu.SemaphoreType.DMA(s or (PIECES,))
    return pl.pallas_call(
        functools.partial(reduce_kernel, lines),
        out_shape=jax.ShapeDtypeStruct((PIECES, PIECE, WIDTH), bf),
        in_specs=[pl.BlockSpec(memory_space=pl.ANY)] * 2,
        out_specs=pl.BlockSpec(memory_space=pl.ANY),
        scratch_shapes=[
            pltpu.VMEM((PIECES, PIECE, WIDTH), bf),
            pltpu.VMEM((PIECES, PIECE, WIDTH), bf),
            pltpu.VMEM((PIECES, PIECE, WIDTH), bf),
            pltpu.VMEM((PIECES, SIDE, WIDTH), bf),
            pltpu.VMEM((2, PIECES, SIDE, WIDTH), bf),
            pltpu.VMEM((PIECES, RAIL, WIDTH), bf),
            pltpu.VMEM((PIECES, RAIL, WIDTH), bf),
            pltpu.VMEM((PIECES, RAIL, WIDTH), bf),
            sems(), sems(),
            sems(), sems(),
            sems(), sems(),
            sems(), sems(2, PIECES),
            sems(), sems(), sems(),
            sems(), sems(),
            sems(), sems(),
            sems(), sems(),
            sems(), sems(), sems(),
        ],
        compiler_params=pltpu.CompilerParams(collective_id=1, has_side_effects=True, vmem_limit_bytes=60 * 2**20),
    )(mine, theirs)


def alibi_slopes():
    closest = 1 << HEADS.bit_length() - 1
    first_slope = 2.0 ** (-8.0 / closest)
    slopes = [first_slope ** (power_index + 1) for power_index in range(closest)]
    double_slope = 2.0 ** (-8.0 / (2 * closest))
    extra_slopes = [double_slope ** (power_index + 1) for power_index in range(2 * closest)]
    return slopes + extra_slopes[0::2][: HEADS - closest]


def alibi_bias():
    positions = jnp.arange(BLOCK)
    distance = jnp.abs(positions[:, None] - positions[None, :]).astype(jnp.float32)
    return -jnp.array(alibi_slopes(), jnp.float32)[:, None, None] * distance


def dot(a, b):
    return jnp.dot(a, b, preferred_element_type=jnp.float32)


def dot_right(a, b):
    return lax.dot_general(a, b, (((1,), (1,)), ((), ())), preferred_element_type=jnp.float32)


def dot_left(a, b):
    return lax.dot_general(a, b, (((0,), (0,)), ((), ())), preferred_element_type=jnp.float32)


def post_norm(inputs, branch, gain, bias):
    summed = inputs.astype(jnp.float32) + branch
    center = summed - jnp.mean(summed, axis=-1, keepdims=True)
    spread = jnp.mean(center * center, axis=-1, keepdims=True)
    inverse = lax.rsqrt(spread + EPSILON)
    scaled = center * inverse
    return ((scaled * gain + bias).astype(jnp.bfloat16), scaled, inverse)


def norm_back(upstream, scaled, inverse, gain):
    scaled_grad = upstream * gain
    gain_term = jnp.sum(upstream * scaled, axis=0)
    bias_term = jnp.sum(upstream, axis=0)
    through = inverse * (
        scaled_grad
        - jnp.mean(scaled_grad, axis=-1, keepdims=True)
        - scaled * jnp.mean(scaled_grad * scaled, axis=-1, keepdims=True)
    )
    return (through, gain_term, bias_term)


def squares(rows, valid):
    rows = rows.astype(jnp.float32)
    return jnp.sum(valid * jnp.sum(rows * rows, axis=-1))


def attend(rows, segments, joint, mixing, gain, bias):
    count = rows.shape[0] // BLOCK
    joint_rows = dot(rows, joint).astype(jnp.bfloat16).reshape(count, BLOCK, 3, HEADS, HEAD)
    queries, keys, values = joint_rows[:, :, 0], joint_rows[:, :, 1], joint_rows[:, :, 2]
    scores = jnp.einsum("bqhd,bkhd->bhqk", queries, keys, preferred_element_type=jnp.float32)
    scores = scores * SCALE + alibi_bias()[None]
    blocks = segments.reshape(count, BLOCK)
    same = blocks[:, None, :, None] == blocks[:, None, None, :]
    scores = jnp.where(same, scores, MASKED)
    exponents = jnp.exp(scores - jnp.max(scores, axis=-1, keepdims=True))
    probs = exponents / jnp.sum(exponents, axis=-1, keepdims=True)
    low = probs.astype(jnp.bfloat16)
    mixed = jnp.einsum("bhqk,bkhd->bqhd", low, values, preferred_element_type=jnp.float32)
    mixed = mixed.reshape(rows.shape[0], D).astype(jnp.bfloat16)
    branch = dot(mixed, mixing)
    out, scaled, inverse = post_norm(rows, branch, gain, bias)
    return out, branch, (queries, keys, values, probs, low, mixed, scaled, inverse)


def attend_back(upstream, kept, joint, mixing, gain):
    queries, keys, values, probs, low, mixed, scaled, inverse = kept
    through, gain_term, bias_term = norm_back(upstream, scaled, inverse, gain)
    branch_grad = through.astype(jnp.bfloat16)
    mixed_grad = dot_right(branch_grad, mixing).astype(jnp.bfloat16).reshape(queries.shape)
    probs_grad = jnp.einsum("bqhd,bkhd->bhqk", mixed_grad, values, preferred_element_type=jnp.float32)
    values_grad = jnp.einsum("bhqk,bqhd->bkhd", low, mixed_grad, preferred_element_type=jnp.float32)
    score_grad = probs * (probs_grad - jnp.sum(probs_grad * probs, axis=-1, keepdims=True))
    score_grad = score_grad.astype(jnp.bfloat16)
    queries_grad = SCALE * jnp.einsum("bhqk,bkhd->bqhd", score_grad, keys, preferred_element_type=jnp.float32)
    keys_grad = SCALE * jnp.einsum("bhqk,bqhd->bkhd", score_grad, queries, preferred_element_type=jnp.float32)
    joint_grad = jnp.stack([queries_grad, keys_grad, values_grad], axis=2)
    joint_grad = joint_grad.reshape(upstream.shape[0], 3 * D).astype(jnp.bfloat16)
    rows_grad = through + dot_right(joint_grad, joint)
    return rows_grad, (mixed, branch_grad, joint_grad), (gain_term, bias_term)


def feed(rows, gated, down, gain, bias):
    gate_up = dot(rows, gated)
    gate, up = gate_up[:, :FF], gate_up[:, FF:]
    normal = 0.5 * (1.0 + lax.erf(gate * ROOT_HALF))
    density = jnp.exp(-0.5 * gate * gate) / ROOT_TWO_PI
    active = gate * normal
    hidden = (active * up).astype(jnp.bfloat16)
    slope = up * (normal + gate * density)
    branch = dot(hidden, down)
    out, scaled, inverse = post_norm(rows, branch, gain, bias)
    return out, branch, (hidden, active, slope, scaled, inverse)


def feed_back(upstream, kept, gated, down, gain):
    hidden, active, slope, scaled, inverse = kept
    through, gain_term, bias_term = norm_back(upstream, scaled, inverse, gain)
    branch_grad = through.astype(jnp.bfloat16)
    hidden_grad = dot_right(branch_grad, down)
    both_grad = jnp.concatenate([hidden_grad * slope, hidden_grad * active], axis=-1).astype(jnp.bfloat16)
    rows_grad = through + dot_right(both_grad, gated)
    return rows_grad, (hidden, branch_grad, both_grad), (gain_term, bias_term)


def per_device(
    inputs, cotangent_first, cotangent_second, segment_ids,
    joint_projection, mixing_weight, gated_weight, down_weight, norm_gain, norm_bias,
):
    section = lax.axis_index("section")
    plane, core = section // 2, section % 2
    micro_rows = inputs.shape[0] // (2 * MICRO)
    lines = lax.axis_size("dp") // 2
    swap = [(0, 1), (1, 0), (2, 3), (3, 2)]
    forward = [(0, 2), (1, 3)]
    backward = [(2, 0), (3, 1)]

    def send(value, pairs):
        return lax.ppermute(value, "section", pairs)

    def whole(mine):
        other = send(mine, swap)
        return jnp.where(core == 0, jnp.concatenate([mine, other]), jnp.concatenate([other, mine]))

    joint, mixing, gated, down = [whole(w) for w in (joint_projection, mixing_weight, gated_weight, down_weight)]
    gains, biases = whole(norm_gain), whole(norm_bias)

    def micro(array, m):
        return lax.dynamic_slice_in_dim(array, (2 * m + core) * micro_rows, micro_rows, 0)

    segments = [micro(segment_ids, m) for m in range(MICRO)]
    valid = [(s >= 0).astype(jnp.float32) for s in segments]

    def layer(rows, m):
        attended, first_branch, first_kept = attend(rows, segments[m], joint, mixing, gains[0], biases[0])
        out, second_branch, second_kept = feed(attended, gated, down, gains[1], biases[1])
        stats = jnp.stack([
            jnp.stack([squares(rows, valid[m]), squares(attended, valid[m])]),
            jnp.stack([squares(first_branch, valid[m]), squares(second_branch, valid[m])]),
        ])
        return out, (rows, attended, first_kept, second_kept, stats)

    def layer_back(upstream, kept):
        rows, attended, first_kept, second_kept, _ = kept
        middle, second_terms, second_norm = feed_back(upstream, second_kept, gated, down, gains[1])
        middle = middle.astype(jnp.bfloat16).astype(jnp.float32)
        grad, first_terms, first_norm = attend_back(middle, first_kept, joint, mixing, gains[0])
        return grad, (first_terms, second_terms, first_norm, second_norm)

    starts = [micro(inputs, m) for m in range(MICRO)]
    early = [layer(starts[m], m)[0] for m in range(MICRO)]
    passed = [send(early[m], forward) for m in range(MICRO)]
    rows = [jnp.where(plane == 0, starts[m], passed[m]) for m in range(MICRO)]
    outs, kept = zip(*[layer(rows[m], m) for m in range(MICRO)])
    first_output = jnp.where(plane == 0, early[0], passed[1])
    second_output = jnp.where(plane == 0, send(outs[0], backward), outs[1])

    final = [valid[m][:, None] * micro(cotangent_second, m).astype(jnp.float32) for m in range(MICRO)]
    middle_add = [valid[m][:, None] * micro(cotangent_first, m).astype(jnp.float32) for m in range(MICRO)]
    early_back = [
        (layer_back(final[m], kept[m])[0] + middle_add[m]).astype(jnp.bfloat16) for m in range(MICRO)
    ]
    passed_back = [send(early_back[m], backward) for m in range(MICRO)]
    upstream = [jnp.where(plane == 0, passed_back[m].astype(jnp.float32), final[m]) for m in range(MICRO)]
    grads, terms = zip(*[layer_back(upstream[m], kept[m]) for m in range(MICRO)])
    grads = [g.astype(jnp.bfloat16) for g in grads]
    middle_gradient = jnp.where(plane == 0, passed_back[0], early_back[1])
    input_gradient = jnp.where(plane == 0, grads[0], send(grads[1], forward))

    def joined(get):
        return jnp.concatenate([get(m) for m in range(MICRO)])

    mixed = joined(lambda m: terms[m][0][0])
    first_branch = joined(lambda m: terms[m][0][1])
    joint_grad = joined(lambda m: terms[m][0][2])
    hidden = joined(lambda m: terms[m][1][0])
    second_branch = joined(lambda m: terms[m][1][1])
    both_grad = joined(lambda m: terms[m][1][2])
    first_rows = joined(lambda m: kept[m][0])
    second_rows = joined(lambda m: kept[m][1])
    weights = [
        dot_left(first_rows, joint_grad),
        dot_left(mixed, first_branch),
        dot_left(second_rows, both_grad),
        dot_left(hidden, second_branch),
    ]
    weights = [w.astype(jnp.bfloat16) for w in weights]

    def pieces(which):
        parts = []
        for w in weights:
            part = lax.dynamic_slice_in_dim(w, which * (w.shape[0] // 2), w.shape[0] // 2, 0)
            height, width = part.shape
            part = part.reshape(height // PIECE, PIECE, width // WIDTH, WIDTH).transpose(0, 2, 1, 3)
            parts.append(part.reshape(-1, PIECE, WIDTH))
        return jnp.concatenate(parts)

    reduced = reduce_gradients(lines, pieces(core), pieces(1 - core))
    results, at = [], 0
    for w in weights:
        height, width = w.shape[0] // 2, w.shape[1]
        count = height * width // (PIECE * WIDTH)
        part = reduced[at : at + count].reshape(height // PIECE, width // WIDTH, PIECE, WIDTH)
        results.append(part.transpose(0, 2, 1, 3).reshape(height, width).astype(jnp.float32))
        at += count

    norms = [
        jnp.stack([sum(terms[m][2 + k][0] for m in range(MICRO)), sum(terms[m][2 + k][1] for m in range(MICRO))])
        for k in range(2)
    ]
    own = jnp.where(core == 0, norms[0], norms[1]) + send(jnp.where(core == 0, norms[1], norms[0]), swap)
    gain_bias = lax.psum(own, "dp")

    stats = sum(kept[m][4] for m in range(MICRO))
    blank = jnp.zeros_like(stats)
    stats = jnp.where(plane == 0, jnp.concatenate([stats, blank], 1), jnp.concatenate([blank, stats], 1))
    count = jnp.where(plane == 0, sum(jnp.sum(v) for v in valid), 0.0)
    stats, count = lax.psum((stats, count), ("dp", "section"))
    magnitudes = jnp.sqrt(stats / (count * D))
    return (
        first_output, second_output, input_gradient, middle_gradient,
        results[0], results[1], results[2], results[3],
        gain_bias[:1], gain_bias[1:], magnitudes,
    )


def solution(mesh):
    tokens, rows = P("dp", None), P("section", None)
    return jax.shard_map(
        per_device,
        mesh=mesh,
        in_specs=(tokens, tokens, tokens, P("dp"), rows, rows, rows, rows, rows, rows),
        out_specs=(P(("dp", "section"), None),) * 4 + (rows,) * 6 + (P(),),
        check_vma=False,
    )
```

```python
import functools

import jax
import jax.numpy as jnp
from jax import lax
from jax.experimental import pallas as pl
from jax.experimental.pallas import tpu as pltpu
from jax.sharding import PartitionSpec as P

D = 768
HEADS = 12
HEAD = D // HEADS
FF = 3072
BLOCK = 128
HALF = D // 2
PAIRS = HEADS // 2
TOKENS = 512
MICRO = 2
ROWS = TOKENS // MICRO
CHUNK = 512
CHUNKS = FF // CHUNK
SMALL = 16
PIECES = 32
PIECE = 384
SIDE = 112
RAIL = 160
WIDTH = 384
AHEAD = 6
LAG = 2
TILES = 16
SLOTS = 8

EPSILON = 1e-05
FAR = 1e30
ROOT_HALF = 0.7071067811865476
ROOT_TWO_PI = 2.5066282746310002
SCALE = HEAD**-0.5

MESH = pl.DeviceIdType.MESH
BF = jnp.bfloat16
F32 = jnp.float32


def alibi_slopes():
    closest = 1 << HEADS.bit_length() - 1
    first_slope = 2.0 ** (-8.0 / closest)
    slopes = [first_slope ** (power_index + 1) for power_index in range(closest)]
    double_slope = 2.0 ** (-8.0 / (2 * closest))
    extra_slopes = [double_slope ** (power_index + 1) for power_index in range(2 * closest)]
    return slopes + extra_slopes[0::2][: HEADS - closest]


SLOPES = alibi_slopes()


def dot(a, b):
    return jnp.dot(a, b, preferred_element_type=F32)


def dot_right(a, b):
    return lax.dot_general(a, b, (((1,), (1,)), ((), ())), preferred_element_type=F32)


def dot_left(a, b):
    return lax.dot_general(a, b, (((0,), (0,)), ((), ())), preferred_element_type=F32)


def lane_mean(x):
    return jnp.sum(x, axis=-1, keepdims=True) * (1.0 / D)


def remote(src, dst, send, recv, device):
    return pltpu.make_async_remote_copy(
        src_ref=src, dst_ref=dst, send_sem=send, recv_sem=recv, device_id=device, device_id_type=MESH
    )


def settled(ref, sem):
    pltpu.make_async_copy(ref, ref, sem).wait()


def layer_kernel(
    inputs_ref, first_ref, second_ref, segments_ref, joint_ref, mixing_ref, gated_ref, down_ref, gain_ref, bias_ref,
    first_out, second_out, input_out, middle_out, mine_out, landed_out, small_out,
    joint_w, mixing_w, gated_w, down_w, norms,
    rows, attended, out, swapped, upstream, back,
    joint_rows, probs, mixed, hidden, active, slope, both_grad,
    branch_first, branch_second, scaled_first, scaled_second, spread, columns, total, small, mixed_grad,
    load_sem, local_sem, weight_send, weight_recv, norm_sem, norm_send, norm_recv,
    ahead_send, ahead_recv, behind_send, behind_recv, swap_send, swap_recv, out_sem,
    keep_sem, give_send, give_recv,
):
    dp, section = lax.axis_index("dp"), lax.axis_index("section")
    plane, core = lax.div(section, 2), lax.rem(section, 2)
    partner = (dp, section + 1 - 2 * core)
    peer = (dp, section + 2 - 4 * plane)

    barrier = pltpu.get_barrier_semaphore()
    pl.semaphore_signal(barrier, inc=1, device_id=partner, device_id_type=MESH)
    pl.semaphore_signal(barrier, inc=1, device_id=peer, device_id_type=MESH)
    pl.semaphore_wait(barrier, 2)

    mine = pl.ds(pl.multiple_of(core * HALF, HALF), HALF)
    theirs = pl.ds(pl.multiple_of((1 - core) * HALF, HALF), HALF)

    def micro_rows(m):
        return pl.ds(pl.multiple_of(m * ROWS, ROWS), ROWS)

    def token_loads():
        copies = []
        for m in range(2):
            there = pl.ds(pl.multiple_of((2 * m + core) * (TOKENS // 2), TOKENS // 2), TOKENS // 2)
            here = pl.ds(m * (TOKENS // 2), TOKENS // 2)
            copies.append(pltpu.make_async_copy(first_ref.at[there], back.at[here], load_sem.at[2 * m]))
            copies.append(pltpu.make_async_copy(second_ref.at[there], upstream.at[here], load_sem.at[2 * m + 1]))
        return copies

    def input_loads():
        copies = []
        for m in range(2):
            there = pl.ds(pl.multiple_of((2 * m + core) * (TOKENS // 2), TOKENS // 2), TOKENS // 2)
            here = pl.ds(m * (TOKENS // 2), TOKENS // 2)
            copies.append(pltpu.make_async_copy(inputs_ref.at[there], rows.at[here], load_sem.at[4 + m]))
        return copies

    def chunk(k):
        return pl.ds(pl.multiple_of(k * CHUNK, CHUNK), CHUNK)

    def upper(k):
        return pl.ds(pl.multiple_of(FF + k * CHUNK, CHUNK), CHUNK)

    def weight_copies(which):
        if which == 0:
            return [(joint_ref, joint_w.at[mine], joint_w.at[theirs], 0), (mixing_ref, mixing_w.at[mine], mixing_w.at[theirs], 1)]
        copies = []
        for k in range(CHUNKS):
            copies.append((gated_ref.at[:, chunk(k)], gated_w.at[mine, chunk(k)], gated_w.at[theirs, chunk(k)], 2 + 2 * k))
            copies.append((gated_ref.at[:, upper(k)], gated_w.at[mine, upper(k)], gated_w.at[theirs, upper(k)], 3 + 2 * k))
            if k % 2 == 1:
                j = k // 2
                part = pl.ds(j * CHUNK, CHUNK)
                here = pl.ds(pl.multiple_of(core * (FF // 2) + j * CHUNK, CHUNK), CHUNK)
                there = pl.ds(pl.multiple_of((1 - core) * (FF // 2) + j * CHUNK, CHUNK), CHUNK)
                copies.append((down_ref.at[part], down_w.at[here], down_w.at[there], 2 + 2 * CHUNKS + j))
        return copies

    def start_weights(which):
        for source, place, _, n in weight_copies(which):
            remote(source, place, weight_send.at[n], weight_recv.at[n], partner).start()
            pltpu.make_async_copy(source, place, local_sem.at[n]).start()

    def wait_weights(which):
        for source, place, other, n in weight_copies(which):
            pltpu.make_async_copy(source, place, local_sem.at[n]).wait()
            settled(other, weight_recv.at[n])

    def wait_weights_sent(which):
        for source, place, _, n in weight_copies(which):
            remote(source, place, weight_send.at[n], weight_recv.at[n], partner).wait_send()

    norm_copies = []
    for n, source in enumerate((gain_ref, bias_ref)):
        norm_copies.append((source, norms.at[n, core], norms.at[n, 1 - core], n))
    for source, place, _, n in norm_copies:
        remote(source, place, norm_send.at[n], norm_recv.at[n], partner).start()
        pltpu.make_async_copy(source, place, norm_sem.at[n]).start()
    start_weights(0)

    @pl.when(plane == 0)
    def _():
        for copy in input_loads():
            copy.start()

    @pl.when(plane == 1)
    def _():
        for copy in token_loads():
            copy.start()

    start_weights(1)

    first = lax.broadcasted_iota(jnp.int32, (BLOCK, BLOCK), 0)
    second = lax.broadcasted_iota(jnp.int32, (BLOCK, BLOCK), 1)
    distance = jnp.abs(first - second).astype(F32)
    half_blocks = TOKENS // (2 * BLOCK)
    for b in range(TOKENS // BLOCK):
        at = (2 * (b // half_blocks) + core) * half_blocks + b % half_blocks
        across = jnp.broadcast_to(segments_ref[pl.ds(at, 1), :].astype(F32), (BLOCK, BLOCK))
        down = across.T
        spread[b] = jnp.where(across == down, distance, FAR)
        columns[pl.ds(b * BLOCK, BLOCK), :] = jnp.where(down >= 0.0, 1.0, 0.0)
    small[...] = jnp.zeros_like(small)
    small[8:9, :BLOCK] = jnp.sum(columns[...], axis=0, keepdims=True)

    lane = lax.broadcasted_iota(jnp.int32, (1, BLOCK), 1)
    low_lanes = jnp.where(lane < HEAD, 1.0, 0.0).astype(BF)
    high_lanes = jnp.where(lane < HEAD, 0.0, 1.0).astype(BF)

    def stacked(x):
        return jnp.concatenate([x * low_lanes, x * high_lanes], axis=0)

    def beside(x):
        return jnp.concatenate([x[:BLOCK], x[BLOCK:]], axis=1)

    for source, place, other, n in norm_copies:
        pltpu.make_async_copy(source, place, norm_sem.at[n]).wait()
        settled(other, norm_recv.at[n])

    def add_small(row, value):
        small[row : row + 1, :] += value

    def keep_column(r, at, value):
        columns[r] = jnp.where(lane == at, value, columns[r])

    def column(value):
        return jnp.sum(value, axis=0, keepdims=True)

    def post_norm(r, source, branch, kind, scaled_ref, result_ref):
        before = source[r].astype(F32)
        ok = columns[r, :1]
        add_small(4 + kind, column(ok * (before * before)))
        add_small(6 + kind, column(ok * (branch * branch)))
        summed = before + branch
        center = summed - lane_mean(summed)
        inverse = lax.rsqrt(lane_mean(center * center) + EPSILON)
        scaled = center * inverse
        scaled_ref[r] = scaled
        keep_column(r, 1 + kind, inverse)
        result_ref[r] = (scaled * norms[0, kind] + norms[1, kind]).astype(BF)

    def norm_back(r, grad, kind, scaled_ref):
        scaled = scaled_ref[r]
        add_small(2 * kind, column(grad * scaled))
        add_small(2 * kind + 1, column(grad))
        inner = grad * norms[0, kind]
        return columns[r, 1 + kind : 2 + kind] * (inner - lane_mean(inner) - scaled * lane_mean(inner * scaled))

    def attend(m):
        r = micro_rows(m)
        joint_rows[r] = dot(rows[r], joint_w[...]).astype(BF)
        for j in range(ROWS // BLOCK):
            b = m * (ROWS // BLOCK) + j
            at = pl.ds(pl.multiple_of(b * BLOCK, BLOCK), BLOCK)
            far = spread[b]
            for p in range(PAIRS):
                lanes = pl.ds(p * BLOCK, BLOCK)
                queries = joint_rows[at, lanes]
                keys = joint_rows[at, pl.ds(D + p * BLOCK, BLOCK)]
                values = joint_rows[at, pl.ds(2 * D + p * BLOCK, BLOCK)]
                raw = dot_right(stacked(queries), keys)
                parts = []
                for e in range(2):
                    scores = raw[e * BLOCK : (e + 1) * BLOCK] * SCALE - SLOPES[2 * p + e] * far
                    weights = jnp.exp(scores - jnp.max(scores, axis=-1, keepdims=True))
                    parts.append(weights / jnp.sum(weights, axis=-1, keepdims=True))
                soft = jnp.concatenate(parts, axis=0)
                probs[b * PAIRS + p] = soft
                mixed[at, lanes] = dot(beside(soft.astype(BF)), stacked(values)).astype(BF)
        branch = dot(mixed[r], mixing_w[...])
        post_norm(r, rows, branch, 0, scaled_first, attended)

    def feed(m):
        r = micro_rows(m)
        total[...] = jnp.zeros_like(total)

        def body(k, carry):
            gate = dot(attended[r], gated_w[:, chunk(k)])
            up = dot(attended[r], gated_w[:, upper(k)])
            normal = 0.5 + 0.5 * lax.erf(gate * ROOT_HALF)
            density = jnp.exp(-0.5 * gate * gate) * (1.0 / ROOT_TWO_PI)
            gelu = gate * normal
            low = (gelu * up).astype(BF)
            hidden[r, chunk(k)] = low
            active[r, chunk(k)] = gelu
            slope[r, chunk(k)] = up * (normal + gate * density)
            total[...] += dot(low, down_w[chunk(k)])
            return carry

        lax.fori_loop(0, CHUNKS, body, 0)
        post_norm(r, attended, total[...], 1, scaled_second, out)

    def feed_back(m, grad):
        r = micro_rows(m)
        through = norm_back(r, grad, 1, scaled_second)
        branch_second[r] = through.astype(BF)
        total[...] = through

        def body(k, carry):
            hidden_grad = dot_right(branch_second[r], down_w[chunk(k)])
            gate_grad = (hidden_grad * slope[r, chunk(k)]).astype(BF)
            up_grad = (hidden_grad * active[r, chunk(k)]).astype(BF)
            both_grad[r, chunk(k)] = gate_grad
            both_grad[r, upper(k)] = up_grad
            total[...] += dot_right(gate_grad, gated_w[:, chunk(k)]) + dot_right(up_grad, gated_w[:, upper(k)])
            return carry

        lax.fori_loop(0, CHUNKS, body, 0)

    def attend_back(m, grad):
        r = micro_rows(m)
        through = norm_back(r, grad, 0, scaled_first)
        branch_first[r] = through.astype(BF)
        total[...] = through
        mixed_grad[...] = dot_right(branch_first[r], mixing_w[...]).astype(BF)
        for j in range(ROWS // BLOCK):
            b = m * (ROWS // BLOCK) + j
            at = pl.ds(pl.multiple_of(b * BLOCK, BLOCK), BLOCK)
            for p in range(PAIRS):
                lanes = pl.ds(p * BLOCK, BLOCK)
                key_lanes, value_lanes = pl.ds(D + p * BLOCK, BLOCK), pl.ds(2 * D + p * BLOCK, BLOCK)
                queries, keys, values = joint_rows[at, lanes], joint_rows[at, key_lanes], joint_rows[at, value_lanes]
                above = stacked(mixed_grad[j * BLOCK : (j + 1) * BLOCK, p * BLOCK : (p + 1) * BLOCK])
                soft = probs[b * PAIRS + p]
                probs_grad = dot_right(above, values)
                joint_rows[at, value_lanes] = dot_left(soft.astype(BF), above).astype(BF)
                score_grad = soft * (probs_grad - jnp.sum(probs_grad * soft, axis=-1, keepdims=True))
                score_grad = score_grad.astype(BF)
                joint_rows[at, lanes] = (SCALE * dot(beside(score_grad), stacked(keys))).astype(BF)
                joint_rows[at, key_lanes] = (SCALE * dot_left(score_grad, stacked(queries))).astype(BF)
        total[...] += dot_right(joint_rows[r], joint_w[...])

    def ahead(m):
        r = micro_rows(m)
        return remote(out.at[r], rows.at[r], ahead_send.at[m], ahead_recv.at[m], peer)

    def behind(m):
        r = micro_rows(m)
        return remote(back.at[r], upstream.at[r], behind_send.at[m], behind_recv.at[m], peer)

    front, rear = pl.ds(0, TOKENS // 2), pl.ds(TOKENS // 2, TOKENS // 2)

    with jax.named_scope("first_weights"):
        wait_weights(0)

    @pl.when(plane == 0)
    def _():
        for copy in input_loads():
            copy.wait()

    def forward_step(step, carry):
        feeding = jnp.where(plane == 0, lax.div(step, MICRO), lax.rem(step, 2))
        m = jnp.where(plane == 0, lax.rem(step, MICRO), lax.div(step, 2))

        @pl.when(feeding == 0)
        def _():
            @pl.when(plane == 1)
            def _():
                with jax.named_scope("rows_wait"):
                    ahead(m).wait_recv()

            with jax.named_scope("attend"):
                attend(m)

        @pl.when(feeding == 1)
        def _():
            @pl.when(m == 0)
            def _():
                with jax.named_scope("weights"):
                    wait_weights(1)

            with jax.named_scope("feed"):
                feed(m)

            @pl.when(plane == 0)
            def _():
                ahead(m).start()

        return carry

    lax.fori_loop(0, 2 * MICRO, forward_step, 0)

    @pl.when(plane == 1)
    def _():
        remote(out.at[front], swapped, swap_send, swap_recv, peer).start()

    @pl.when(plane == 1)
    def _():
        for copy in token_loads():
            copy.wait()

    def backward_step(m, carry):
        r = micro_rows(m)

        @pl.when(plane == 0)
        def _():
            with jax.named_scope("grad_wait"):
                behind(m).wait_recv()

        @pl.when(plane == 1)
        def _():
            upstream[r] = (columns[r, :1] * upstream[r].astype(F32)).astype(BF)

        with jax.named_scope("feed_back"):
            feed_back(m, upstream[r].astype(F32))
        with jax.named_scope("attend_back"):
            attend_back(m, total[...].astype(BF).astype(F32))

        @pl.when(plane == 0)
        def _():
            back[r] = total[...].astype(BF)

        @pl.when(plane == 1)
        def _():
            back[r] = (total[...] + columns[r, :1] * back[r].astype(F32)).astype(BF)
            behind(m).start()

        return carry

    lax.fori_loop(0, MICRO, backward_step, 0)

    @pl.when(plane == 0)
    def _():
        remote(back.at[rear], swapped, swap_send, swap_recv, peer).start()

    def keep(tile, a, b, piece):
        source = gated_w.at[pl.ds(pl.multiple_of(a * PIECE, PIECE), PIECE), pl.ds(pl.multiple_of(lax.rem(tile, SLOTS) * D + b * WIDTH, WIDTH), WIDTH)]
        return pltpu.make_async_copy(source, mine_out.at[piece], keep_sem.at[piece])

    def give(tile, a, b, piece):
        source = gated_w.at[pl.ds(pl.multiple_of(a * PIECE, PIECE), PIECE), pl.ds(pl.multiple_of(lax.rem(tile, SLOTS) * D + b * WIDTH, WIDTH), WIDTH)]
        return remote(source, landed_out.at[piece], give_send.at[piece], give_recv.at[piece], partner)

    def wide(k):
        return pl.ds(pl.multiple_of(k * D, D), D)

    def finish_tile(tile):
        for b in range(2):
            @pl.when(tile < 4)
            def _(b=b):
                for a in range(2):
                    piece = lax.rem(tile, 2) * 4 + 2 * a + b

                    @pl.when(lax.div(tile, 2) == core)
                    def _(a=a, piece=piece):
                        keep(tile, a, b, piece).wait()

                    @pl.when(lax.div(tile, 2) != core)
                    def _(a=a, piece=piece):
                        give(tile, a, b, piece).wait_send()

            @pl.when(tile >= 4)
            def _(b=b):
                piece = 8 + (tile - 4) * 2 + b
                keep(tile, core, b, piece).wait()
                give(tile, 1 - core, b, piece).wait_send()

    def launch_tile(tile, value):
        @pl.when(tile >= SLOTS)
        def _():
            finish_tile(tile - SLOTS)

        gated_w[:, wide(lax.rem(tile, SLOTS))] = value.astype(BF)
        for b in range(2):
            @pl.when(tile < 4)
            def _(b=b):
                for a in range(2):
                    piece = lax.rem(tile, 2) * 4 + 2 * a + b

                    @pl.when(lax.div(tile, 2) == core)
                    def _(a=a, piece=piece):
                        keep(tile, a, b, piece).start()

                    @pl.when(lax.div(tile, 2) != core)
                    def _(a=a, piece=piece):
                        give(tile, a, b, piece).start()

            @pl.when(tile >= 4)
            def _(b=b):
                piece = 8 + (tile - 4) * 2 + b
                keep(tile, core, b, piece).start()
                give(tile, 1 - core, b, piece).start()

    def down_tile(k, carry):
        launch_tile(k, dot_left(hidden[:, wide(k)], branch_second[...]))
        return carry

    def gated_tile(k, carry):
        launch_tile(4 + k, dot_left(attended[...], both_grad[:, wide(k)]))
        return carry

    def joint_tile(k, carry):
        launch_tile(12 + k, dot_left(rows[...], joint_rows[:, wide(k)]))
        return carry

    with jax.named_scope("down_gradient"):
        lax.fori_loop(0, 4, down_tile, 0)
    with jax.named_scope("gated_gradient"):
        lax.fori_loop(0, 8, gated_tile, 0)
    with jax.named_scope("joint_gradient"):
        lax.fori_loop(0, 3, joint_tile, 0)
    launch_tile(jnp.int32(15), dot_left(mixed[...], branch_first[...]))

    def drain(tile, carry):
        finish_tile(tile)
        return carry

    lax.fori_loop(TILES - SLOTS, TILES, drain, 0)

    remote(out.at[front], swapped, swap_send, swap_recv, peer).wait_recv()

    def writes(which):
        pairs = [
            [(out.at[front], first_out), (swapped, second_out), (back.at[front], input_out), (upstream.at[front], middle_out)],
            [(rows.at[rear], first_out), (out.at[rear], second_out), (swapped, input_out), (back.at[rear], middle_out)],
        ][which]
        return [pltpu.make_async_copy(a, b, out_sem.at[n]) for n, (a, b) in enumerate(pairs)]

    for which in range(2):
        @pl.when(plane == which)
        def _(which=which):
            for copy in writes(which):
                copy.start()

    small_copy = pltpu.make_async_copy(small, small_out, out_sem.at[4])
    small_copy.start()
    small_copy.wait()
    for which in range(2):
        @pl.when(plane == which)
        def _(which=which):
            for copy in writes(which):
                copy.wait()

    remote(out.at[front], swapped, swap_send, swap_recv, peer).wait_send()
    for m in range(MICRO):
        @pl.when(plane == 0)
        def _(m=m):
            ahead(m).wait_send()

        @pl.when(plane == 1)
        def _(m=m):
            behind(m).wait_send()

    for n, (source, place, _, _) in enumerate(norm_copies):
        remote(source, place, norm_send.at[n], norm_recv.at[n], partner).wait_send()
    wait_weights_sent(0)
    wait_weights_sent(1)
    for piece in range(PIECES):
        settled(landed_out.at[piece], give_recv.at[piece])


def run_layer(inputs, first, second, segments, joint, mixing, gated, down, gain, bias):
    sems = lambda *s: pltpu.SemaphoreType.DMA(s)
    half = TOKENS // 2
    copies = 2 + 2 * CHUNKS + CHUNKS // 2
    any_spec, vmem = pl.BlockSpec(memory_space=pl.ANY), pl.BlockSpec(memory_space=pltpu.VMEM)
    rows_out = jax.ShapeDtypeStruct((half, D), BF)
    pieces = jax.ShapeDtypeStruct((PIECES, PIECE, WIDTH), BF)
    tokens = pltpu.VMEM((TOKENS, D), BF)
    return pl.pallas_call(
        layer_kernel,
        out_shape=[rows_out] * 4 + [pieces, pieces, jax.ShapeDtypeStruct((SMALL, D), F32)],
        in_specs=[any_spec] * 3 + [vmem] + [any_spec] * 6,
        out_specs=[any_spec] * 7,
        scratch_shapes=[
            pltpu.VMEM((D, 3 * D), BF), pltpu.VMEM((D, D), BF), pltpu.VMEM((D, 2 * FF), BF), pltpu.VMEM((FF, D), BF),
            pltpu.VMEM((2, 2, 1, D), F32),
            tokens, tokens, tokens, pltpu.VMEM((half, D), BF), tokens, tokens,
            pltpu.VMEM((TOKENS, 3 * D), BF),
            pltpu.VMEM((TOKENS // BLOCK * PAIRS, 2 * BLOCK, BLOCK), F32),
            tokens, pltpu.VMEM((TOKENS, FF), BF), pltpu.VMEM((TOKENS, FF), F32), pltpu.VMEM((TOKENS, FF), F32),
            pltpu.VMEM((TOKENS, 2 * FF), BF),
            tokens, tokens, pltpu.VMEM((TOKENS, D), F32), pltpu.VMEM((TOKENS, D), F32),
            pltpu.VMEM((TOKENS // BLOCK, BLOCK, BLOCK), F32), pltpu.VMEM((TOKENS, BLOCK), F32),
            pltpu.VMEM((ROWS, D), F32), pltpu.VMEM((SMALL, D), F32),
            pltpu.VMEM((ROWS, D), BF),
            sems(6), sems(copies), sems(copies), sems(copies), sems(2), sems(2), sems(2),
            sems(MICRO), sems(MICRO), sems(MICRO), sems(MICRO), pltpu.SemaphoreType.DMA, pltpu.SemaphoreType.DMA, sems(5),
            sems(PIECES), sems(PIECES), sems(PIECES),
        ],
        compiler_params=pltpu.CompilerParams(collective_id=2, has_side_effects=True, vmem_limit_bytes=62 * 2**20),
    )(inputs, first, second, segments, joint, mixing, gated, down, gain, bias)


def reduce_kernel(
    lines, mine_ref, landed_ref, small_ref, out_ref, small_out, other_out,
    total, grown, small, small_in, from_side, from_inner, from_low, from_high, from_root,
    load_sem, other_sem, store_sem, small_send, small_recv, small_load, side_send, side_recv, inner_send, inner_recv,
    up_send, low_recv, high_recv, root_send, root_recv,
    line_send, line_recv, back_send, back_recv, low_send, high_send, rail_recv,
):
    dp, section = lax.axis_index("dp"), lax.axis_index("section")
    y, z = lax.rem(dp, 2), lax.div(dp, 2)
    half = lines // 2
    mid = half - 1
    partner = (dp, section + 1 - 2 * lax.rem(section, 2))
    across = (dp + 1 - 2 * y, section)
    peer = (dp, lax.rem(section + 2, 4))
    below, above = (dp - 2, section), (dp + 2, section)
    lower = z < half
    depth = jnp.where(lower, z, lines - 1 - z)
    has_low, has_high = z > 0, z < lines - 1
    my_rows = pl.ds(pl.multiple_of(y * SIDE, 8), SIDE)
    other_rows = pl.ds(pl.multiple_of((1 - y) * SIDE, 8), SIDE)
    rail_rows = pl.ds(2 * SIDE, RAIL)
    last = PIECES - 1

    barrier = pltpu.get_barrier_semaphore()
    pl.semaphore_signal(barrier, inc=1, device_id=partner, device_id_type=MESH)
    pl.semaphore_signal(barrier, inc=1, device_id=across, device_id_type=MESH)
    pl.semaphore_signal(barrier, inc=1, device_id=peer, device_id_type=MESH)

    @pl.when(has_low)
    def _():
        pl.semaphore_signal(barrier, inc=1, device_id=below, device_id_type=MESH)

    @pl.when(has_high)
    def _():
        pl.semaphore_signal(barrier, inc=1, device_id=above, device_id_type=MESH)

    pl.semaphore_wait(barrier, 3 + has_low.astype(jnp.int32) + has_high.astype(jnp.int32))

    def load(b):
        return pltpu.make_async_copy(mine_ref.at[b], grown.at[b], load_sem.at[b])

    def load_other(b):
        return pltpu.make_async_copy(landed_ref.at[b], total.at[b], other_sem.at[b])

    def store(b):
        return pltpu.make_async_copy(total.at[b], out_ref.at[b], store_sem.at[b])

    def start_all(b, carry):
        load_other(b).start()
        load(b).start()
        return carry

    lax.fori_loop(0, AHEAD, start_all, 0)

    def add(dst, rows, b, *others):
        value = grown[b, rows].astype(jnp.float32)
        for other in others:
            value = value + other.astype(jnp.float32)
        dst[b, rows] = value.astype(jnp.bfloat16)

    def when(active, b):
        return pl.when(active & (b >= 0) & (b < PIECES))

    def root_of(b):
        odd = lax.rem(b, 2)
        return jnp.where(b < PIECES // 2, odd * (lines - 1), mid + odd)

    inward = (jnp.where(lower, dp + 2, dp - 2), section)
    outward = (jnp.where(lower, dp - 2, dp + 2), section)

    def small_copy(n, device, into=None):
        into = n if into is None else into
        return remote(small.at[n], small_in.at[into], small_send.at[n], small_recv.at[into], device)

    def small_sum(n, source, arrival):
        settled(small_in.at[arrival], small_recv.at[arrival])
        small[n] = small[source] + small_in[arrival]

    def small_steps(i):
        @pl.when(i == 2)
        def _():
            small_copy(0, partner).start()

        @pl.when(i == 4)
        def _():
            small_sum(1, 0, 0)
            small_copy(1, across).start()

        @pl.when(i == 6 + 2 * depth)
        def _():
            small_sum(2, 1, 1)

            @pl.when(depth > 0)
            def _():
                small_sum(3, 2, 2)

            @pl.when(depth == 0)
            def _():
                small[3] = small[2]

            slot = jnp.where(depth == mid, 3, 2)
            remote(small.at[3], small_in.at[slot], small_send.at[2], small_recv.at[slot], inward).start()

        @pl.when(i == 8 + 2 * (2 * mid - depth))
        def _():
            @pl.when(depth == mid)
            def _():
                small_sum(4, 3, 3)

            @pl.when(depth < mid)
            def _():
                settled(small.at[4], small_recv.at[4])

            @pl.when(depth > 0)
            def _():
                remote(small.at[4], small.at[4], small_send.at[3], small_recv.at[4], outward).start()

            remote(small.at[4], small_in.at[4], small_send.at[4], small_recv.at[5], peer).start()

    def small_finish():
        settled(small_in.at[4], small_recv.at[5])
        settled(small.at[0], small_send.at[0])
        settled(small.at[1], small_send.at[1])
        settled(small.at[3], small_send.at[2])
        settled(small.at[4], small_send.at[4])

        @pl.when(depth > 0)
        def _():
            settled(small.at[4], small_send.at[3])

        for n, (source, place) in enumerate(((small.at[4], small_out), (small_in.at[4], other_out))):
            copy = pltpu.make_async_copy(source, place, small_load.at[n])
            copy.start()
            copy.wait()

    first_small = pltpu.make_async_copy(small_ref, small.at[0], small_load.at[2])
    first_small.start()
    first_small.wait()

    def step(i, carry):
        small_steps(i)

        b1 = i - LAG * (1 + depth)

        @when(True, b1)
        def _():
            settled(from_side.at[b1], side_recv.at[b1])

            @pl.when(depth == 0)
            def _():
                add(grown, my_rows, b1, from_side[b1])

            @pl.when(depth > 0)
            def _():
                settled(from_inner.at[0, b1], inner_recv.at[0, b1])
                add(grown, my_rows, b1, from_side[b1], from_inner[0, b1])

            slot = (depth == mid).astype(jnp.int32)
            remote(
                grown.at[b1, my_rows], from_inner.at[slot, b1], inner_send.at[b1], inner_recv.at[slot, b1], inward
            ).start()

        b2 = i - LAG * (2 + mid + mid - depth)

        @when(True, b2)
        def _():
            @pl.when(depth == mid)
            def _():
                settled(from_inner.at[1, b2], inner_recv.at[1, b2])
                add(total, my_rows, b2, from_inner[1, b2])

            @pl.when(depth < mid)
            def _():
                settled(total.at[b2, my_rows], line_recv.at[b2])

            @pl.when(depth > 0)
            def _():
                remote(total.at[b2, my_rows], total.at[b2, my_rows], line_send.at[b2], line_recv.at[b2], outward).start()

            remote(total.at[b2, my_rows], total.at[b2, my_rows], back_send.at[b2], back_recv.at[b2], across).start()

        b3 = i - LAG * (3 + mid + mid - depth)

        @when(True, b3)
        def _():
            settled(total.at[b3, other_rows], back_recv.at[b3])

        for early in (True, False):
            for odd in (0, 1):
                root = (odd * (lines - 1)) if early else mid + odd
                height = max(root, lines - 1 - root)
                distance = jnp.abs(z - root)

                def mine(b, root=root):
                    return (root_of(b) == root) & (lax.rem(b + 4 * PIECES, 2) == odd)

                hop = jnp.where(z < root, z, jnp.where(z > root, lines - 1 - z, height))
                c1 = i - LAG * hop

                @when((z != root) & (hop > 0) & mine(c1), c1)
                def _(root=root, c1=c1):
                    @pl.when(z < root)
                    def _():
                        settled(from_low.at[c1], low_recv.at[c1])
                        add(grown, rail_rows, c1, from_low[c1])
                        remote(grown.at[c1, rail_rows], from_low.at[c1], up_send.at[c1], low_recv.at[c1], above).start()

                    @pl.when(z > root)
                    def _():
                        settled(from_high.at[c1], high_recv.at[c1])
                        add(grown, rail_rows, c1, from_high[c1])
                        remote(grown.at[c1, rail_rows], from_high.at[c1], up_send.at[c1], high_recv.at[c1], below).start()

                @when((z == root) & mine(c1), c1)
                def _(root=root, c1=c1):
                    if root > 0:
                        settled(from_low.at[c1], low_recv.at[c1])
                    if root < lines - 1:
                        settled(from_high.at[c1], high_recv.at[c1])
                    parts = ([from_low[c1]] if root > 0 else []) + ([from_high[c1]] if root < lines - 1 else [])
                    add(grown, rail_rows, c1, *parts)
                    remote(grown.at[c1, rail_rows], from_root.at[c1], root_send.at[c1], root_recv.at[c1], across).start()

                c2 = i - LAG * (height + 1 + distance)

                @when(mine(c2), c2)
                def _(root=root, c2=c2):
                    @pl.when(z == root)
                    def _():
                        settled(from_root.at[c2], root_recv.at[c2])
                        add(total, rail_rows, c2, from_root[c2])

                    @pl.when(z != root)
                    def _():
                        settled(total.at[c2, rail_rows], rail_recv.at[c2])

                    @pl.when(has_low & (z <= root))
                    def _():
                        remote(total.at[c2, rail_rows], total.at[c2, rail_rows], low_send.at[c2], rail_recv.at[c2], below).start()

                    @pl.when(has_high & (z >= root))
                    def _():
                        remote(total.at[c2, rail_rows], total.at[c2, rail_rows], high_send.at[c2], rail_recv.at[c2], above).start()

        b4 = i - LAG * (2 * lines - 1)

        @when(True, b4)
        def _():
            store(b4).start()

        b0 = i

        @when(True, b0)
        def _():
            @pl.when(b0 + AHEAD < PIECES)
            def _():
                start_all(b0 + AHEAD, 0)

            load(b0).wait()
            load_other(b0).wait()
            grown[b0] = (grown[b0].astype(jnp.float32) + total[b0].astype(jnp.float32)).astype(jnp.bfloat16)
            remote(grown.at[b0, other_rows], from_side.at[b0], side_send.at[b0], side_recv.at[b0], across).start()
            root = root_of(b0)

            @pl.when((z == 0) & (root != 0))
            def _():
                remote(grown.at[b0, rail_rows], from_low.at[b0], up_send.at[b0], low_recv.at[b0], above).start()

            @pl.when((z == lines - 1) & (root != lines - 1))
            def _():
                remote(grown.at[b0, rail_rows], from_high.at[b0], up_send.at[b0], high_recv.at[b0], below).start()

        return carry

    lax.fori_loop(0, PIECES + LAG * (2 * lines - 1), step, 0)

    small_finish()

    def finish(b, carry):
        store(b).wait()
        root = root_of(b)
        pltpu.make_async_copy(grown.at[b, other_rows], grown.at[b, other_rows], side_send.at[b]).wait()
        pltpu.make_async_copy(grown.at[b, my_rows], grown.at[b, my_rows], inner_send.at[b]).wait()
        pltpu.make_async_copy(total.at[b, my_rows], total.at[b, my_rows], back_send.at[b]).wait()

        @pl.when(depth > 0)
        def _():
            pltpu.make_async_copy(total.at[b, my_rows], total.at[b, my_rows], line_send.at[b]).wait()

        @pl.when(z != root)
        def _():
            pltpu.make_async_copy(grown.at[b, rail_rows], grown.at[b, rail_rows], up_send.at[b]).wait()

        @pl.when(z == root)
        def _():
            pltpu.make_async_copy(grown.at[b, rail_rows], grown.at[b, rail_rows], root_send.at[b]).wait()

        @pl.when(has_low & (z <= root))
        def _():
            pltpu.make_async_copy(total.at[b, rail_rows], total.at[b, rail_rows], low_send.at[b]).wait()

        @pl.when(has_high & (z >= root))
        def _():
            pltpu.make_async_copy(total.at[b, rail_rows], total.at[b, rail_rows], high_send.at[b]).wait()

        return carry

    lax.fori_loop(0, PIECES, finish, 0)


def reduce_gradients(lines, mine, landed, small):
    sems = lambda *s: pltpu.SemaphoreType.DMA(s or (PIECES,))
    any_spec = pl.BlockSpec(memory_space=pl.ANY)
    block = jax.ShapeDtypeStruct((SMALL, D), F32)
    return pl.pallas_call(
        functools.partial(reduce_kernel, lines),
        out_shape=[jax.ShapeDtypeStruct((PIECES, PIECE, WIDTH), BF), block, block],
        in_specs=[any_spec] * 3,
        out_specs=[any_spec] * 3,
        scratch_shapes=[
            pltpu.VMEM((PIECES, PIECE, WIDTH), BF), pltpu.VMEM((PIECES, PIECE, WIDTH), BF),
            pltpu.VMEM((5, SMALL, D), F32), pltpu.VMEM((5, SMALL, D), F32),
            pltpu.VMEM((PIECES, SIDE, WIDTH), BF), pltpu.VMEM((2, PIECES, SIDE, WIDTH), BF),
            pltpu.VMEM((PIECES, RAIL, WIDTH), BF), pltpu.VMEM((PIECES, RAIL, WIDTH), BF),
            pltpu.VMEM((PIECES, RAIL, WIDTH), BF),
            sems(), sems(), sems(), sems(5), sems(6), sems(3), sems(), sems(), sems(), sems(2, PIECES),
            sems(), sems(), sems(), sems(), sems(), sems(), sems(), sems(), sems(), sems(), sems(), sems(),
        ],
        compiler_params=pltpu.CompilerParams(collective_id=1, has_side_effects=True, vmem_limit_bytes=60 * 2**20),
    )(mine, landed, small)


def place_kernel(pieces_ref, joint_out, mixing_out, gated_out, down_out, held, wide, load_sem, store_sem):
    def place(piece):
        if piece < 8:
            return down_out.at[pl.ds(piece // 2 * PIECE, PIECE), pl.ds(piece % 2 * WIDTH, WIDTH)]
        if piece < 24:
            return gated_out.at[:, pl.ds((piece - 8) * WIDTH, WIDTH)]
        if piece < 30:
            return joint_out.at[:, pl.ds((piece - 24) * WIDTH, WIDTH)]
        return mixing_out.at[:, pl.ds((piece - 30) * WIDTH, WIDTH)]

    loads = [pltpu.make_async_copy(pieces_ref.at[p], held.at[p], load_sem.at[p]) for p in range(PIECES)]
    stores = [pltpu.make_async_copy(wide.at[p % 4], place(p), store_sem.at[p % 4]) for p in range(PIECES)]
    for load in loads:
        load.start()
    for p in range(PIECES):
        loads[p].wait()
        if p >= 4:
            stores[p - 4].wait()
        wide[p % 4] = held[p].astype(F32)
        stores[p].start()
    for p in range(PIECES - 4, PIECES):
        stores[p].wait()


def place_gradients(pieces):
    any_spec = pl.BlockSpec(memory_space=pl.ANY)
    shapes = ((HALF, 3 * D), (HALF, D), (HALF, 2 * FF), (FF // 2, D))
    return pl.pallas_call(
        place_kernel,
        out_shape=[jax.ShapeDtypeStruct(s, F32) for s in shapes],
        in_specs=[any_spec],
        out_specs=[any_spec] * 4,
        scratch_shapes=[
            pltpu.VMEM((PIECES, PIECE, WIDTH), BF), pltpu.VMEM((4, PIECE, WIDTH), F32),
            pltpu.SemaphoreType.DMA((PIECES,)), pltpu.SemaphoreType.DMA((4,)),
        ],
        compiler_params=pltpu.CompilerParams(vmem_limit_bytes=40 * 2**20),
    )(pieces)


def per_device(
    inputs, cotangent_first, cotangent_second, segment_ids,
    joint_projection, mixing_weight, gated_weight, down_weight, norm_gain, norm_bias,
):
    section = lax.axis_index("section")
    plane, core = section // 2, section % 2
    segments = segment_ids.reshape(-1, BLOCK)
    first, second, input_gradient, middle, mine, landed, small = run_layer(
        inputs, cotangent_first, cotangent_second, segments,
        joint_projection, mixing_weight, gated_weight, down_weight, norm_gain, norm_bias,
    )
    pieces, small, other = reduce_gradients(lax.axis_size("dp") // 2, mine, landed, small)
    joint, mixing, gated, down = place_gradients(pieces)
    norms = lax.dynamic_slice_in_dim(small, 2 * core, 2, 0)
    own, across = jnp.sum(small[4:8], axis=1).reshape(2, 2), jnp.sum(other[4:8], axis=1).reshape(2, 2)
    squares = jnp.where(plane == 0, jnp.concatenate([own, across], 1), jnp.concatenate([across, own], 1))
    magnitudes = jnp.sqrt(squares / (small[8, 0] * D))
    return (
        first, second, input_gradient, middle, joint, mixing, gated, down, norms[:1], norms[1:], magnitudes,
    )


def solution(mesh):
    tokens, rows = P("dp", None), P("section", None)
    return jax.shard_map(
        per_device,
        mesh=mesh,
        in_specs=(tokens, tokens, tokens, P("dp"), rows, rows, rows, rows, rows, rows),
        out_specs=(P(("dp", "section"), None),) * 4 + (rows,) * 6 + (P(),),
        check_vma=False,
    )
```

```python
import functools

import jax
import jax.numpy as jnp
from jax import lax
from jax.experimental import pallas as pl
from jax.experimental.pallas import tpu as pltpu
from jax.sharding import PartitionSpec as P

D = 768
HEADS = 12
HEAD = D // HEADS
FF = 3072
BLOCK = 128
HALF = D // 2
PAIRS = HEADS // 2
TOKENS = 512
MICRO = 2
ROWS = TOKENS // MICRO
CHUNK = 1024
PART = 512
CHUNKS = FF // CHUNK
SMALL = 16
PIECES = 32
PIECE = 384
SIDE = 112
RAIL = 160
WIDTH = 384
AHEAD = 6
LAG = 2
RING = 16
TILES = 16
SLOTS = 8

EPSILON = 1e-05
FAR = 1e30
ROOT_HALF = 0.7071067811865476
ROOT_TWO_PI = 2.5066282746310002
SCALE = HEAD**-0.5

MESH = pl.DeviceIdType.MESH
BF = jnp.bfloat16
F32 = jnp.float32


def alibi_slopes():
    closest = 1 << HEADS.bit_length() - 1
    first_slope = 2.0 ** (-8.0 / closest)
    slopes = [first_slope ** (power_index + 1) for power_index in range(closest)]
    double_slope = 2.0 ** (-8.0 / (2 * closest))
    extra_slopes = [double_slope ** (power_index + 1) for power_index in range(2 * closest)]
    return slopes + extra_slopes[0::2][: HEADS - closest]


SLOPES = alibi_slopes()


def dot(a, b):
    return jnp.dot(a, b, preferred_element_type=F32)


def dot_right(a, b):
    return lax.dot_general(a, b, (((1,), (1,)), ((), ())), preferred_element_type=F32)


def dot_left(a, b):
    return lax.dot_general(a, b, (((0,), (0,)), ((), ())), preferred_element_type=F32)


def lane_mean(x):
    return jnp.sum(x, axis=-1, keepdims=True) * (1.0 / D)


def remote(src, dst, send, recv, device):
    return pltpu.make_async_remote_copy(
        src_ref=src, dst_ref=dst, send_sem=send, recv_sem=recv, device_id=device, device_id_type=MESH
    )


def settled(ref, sem):
    pltpu.make_async_copy(ref, ref, sem).wait()


def layer_kernel(
    lines,
    inputs_ref, first_ref, second_ref, segments_ref, joint_ref, mixing_ref, gated_ref, down_ref, gain_ref, bias_ref,
    first_out, second_out, input_out, middle_out, mine_out, landed_out, pieces_out, small_out, other_out,
    joint_w, mixing_w, gated_w, down_w, norms,
    rows, attended, out, swapped, upstream, back,
    joint_rows, probs, mixed, hidden, active, slope, both_grad,
    branch_first, branch_second, scaled_first, scaled_second, spread, columns,
    total, small, small_in, mixed_grad, staged,
    load_sem, local_sem, weight_send, weight_recv, norm_sem, norm_send, norm_recv,
    ahead_send, ahead_recv, behind_send, behind_recv, swap_send, swap_recv, out_sem,
    keep_sem, give_send, give_recv, ready_sem,
    own_sem, other_sem, store_sem, small_send, small_recv, side_send, side_recv, inner_send, inner_recv,
    up_send, low_recv, high_recv, root_send, root_recv, line_send, line_recv, back_send, back_recv,
    low_send, high_send, rail_recv,
):
    dp, section = lax.axis_index("dp"), lax.axis_index("section")
    plane, core = lax.div(section, 2), lax.rem(section, 2)
    partner = (dp, section + 1 - 2 * core)
    peer = (dp, section + 2 - 4 * plane)

    y, z = lax.rem(dp, 2), lax.div(dp, 2)
    across, below, above = (dp + 1 - 2 * y, section), (dp - 2, section), (dp + 2, section)
    has_low, has_high = z > 0, z < lines - 1
    near = 1 + has_low.astype(jnp.int32) + has_high.astype(jnp.int32)

    def signal_near(semaphore):
        pl.semaphore_signal(semaphore, inc=1, device_id=across, device_id_type=MESH)

        @pl.when(has_low)
        def _():
            pl.semaphore_signal(semaphore, inc=1, device_id=below, device_id_type=MESH)

        @pl.when(has_high)
        def _():
            pl.semaphore_signal(semaphore, inc=1, device_id=above, device_id_type=MESH)

    barrier = pltpu.get_barrier_semaphore()
    pl.semaphore_signal(barrier, inc=1, device_id=partner, device_id_type=MESH)
    pl.semaphore_signal(barrier, inc=1, device_id=peer, device_id_type=MESH)
    signal_near(barrier)
    pl.semaphore_wait(barrier, 2 + near)

    mine = pl.ds(pl.multiple_of(core * HALF, HALF), HALF)
    theirs = pl.ds(pl.multiple_of((1 - core) * HALF, HALF), HALF)

    def micro_rows(m):
        return pl.ds(pl.multiple_of(m * ROWS, ROWS), ROWS)

    def token_loads():
        copies = []
        for m in range(2):
            there = pl.ds(pl.multiple_of((2 * m + core) * (TOKENS // 2), TOKENS // 2), TOKENS // 2)
            here = pl.ds(m * (TOKENS // 2), TOKENS // 2)
            copies.append(pltpu.make_async_copy(first_ref.at[there], back.at[here], load_sem.at[2 * m]))
            copies.append(pltpu.make_async_copy(second_ref.at[there], upstream.at[here], load_sem.at[2 * m + 1]))
        return copies

    def input_loads():
        copies = []
        for m in range(2):
            there = pl.ds(pl.multiple_of((2 * m + core) * (TOKENS // 2), TOKENS // 2), TOKENS // 2)
            here = pl.ds(m * (TOKENS // 2), TOKENS // 2)
            copies.append(pltpu.make_async_copy(inputs_ref.at[there], rows.at[here], load_sem.at[4 + m]))
        return copies

    def chunk(k):
        return pl.ds(pl.multiple_of(k * CHUNK, CHUNK), CHUNK)

    def upper(k):
        return pl.ds(pl.multiple_of(FF + k * CHUNK, CHUNK), CHUNK)

    def weight_copies(which):
        if which == 0:
            return [(joint_ref, joint_w.at[mine], joint_w.at[theirs], 0), (mixing_ref, mixing_w.at[mine], mixing_w.at[theirs], 1)]
        copies = []
        for k in range(CHUNKS):
            for n, columns_at in enumerate((chunk(k), upper(k))):
                copies.append((gated_ref.at[:, columns_at], gated_w.at[mine, columns_at], gated_w.at[theirs, columns_at], 2 + 2 * k + n))
            here = pl.ds(pl.multiple_of(core * (FF // 2) + k * PART, PART), PART)
            there = pl.ds(pl.multiple_of((1 - core) * (FF // 2) + k * PART, PART), PART)
            copies.append((down_ref.at[pl.ds(k * PART, PART)], down_w.at[here], down_w.at[there], 2 + 2 * CHUNKS + k))
        return copies

    def start_weights(which):
        for source, place, _, n in weight_copies(which):
            remote(source, place, weight_send.at[n], weight_recv.at[n], partner).start()
            pltpu.make_async_copy(source, place, local_sem.at[n]).start()

    def wait_weights(which):
        for source, place, other, n in weight_copies(which):
            pltpu.make_async_copy(source, place, local_sem.at[n]).wait()
            settled(other, weight_recv.at[n])

    def wait_chunk(k):
        for source, place, other, n in weight_copies(1)[3 * k : 3 * k + 2]:
            pltpu.make_async_copy(source, place, local_sem.at[n]).wait()
            settled(other, weight_recv.at[n])
        for part in (2 * k, 2 * k + 1):
            source, _, _, n = weight_copies(1)[3 * (part % CHUNKS) + 2]
            place = down_w.at[pl.ds(part * PART, PART)]

            @pl.when(core == part // CHUNKS)
            def _():
                pltpu.make_async_copy(source, place, local_sem.at[n]).wait()

            @pl.when(core != part // CHUNKS)
            def _():
                settled(place, weight_recv.at[n])

    def wait_weights_sent(which):
        for source, place, _, n in weight_copies(which):
            remote(source, place, weight_send.at[n], weight_recv.at[n], partner).wait_send()

    norm_copies = []
    for n, source in enumerate((gain_ref, bias_ref)):
        norm_copies.append((source, norms.at[n, core], norms.at[n, 1 - core], n))
    for source, place, _, n in norm_copies:
        remote(source, place, norm_send.at[n], norm_recv.at[n], partner).start()
        pltpu.make_async_copy(source, place, norm_sem.at[n]).start()
    start_weights(0)

    @pl.when(plane == 0)
    def _():
        for copy in input_loads():
            copy.start()

    @pl.when(plane == 1)
    def _():
        for copy in token_loads():
            copy.start()

    start_weights(1)

    first = lax.broadcasted_iota(jnp.int32, (BLOCK, BLOCK), 0)
    second = lax.broadcasted_iota(jnp.int32, (BLOCK, BLOCK), 1)
    distance = jnp.abs(first - second).astype(F32)
    half_blocks = TOKENS // (2 * BLOCK)
    for b in range(TOKENS // BLOCK):
        at = (2 * (b // half_blocks) + core) * half_blocks + b % half_blocks
        along = jnp.broadcast_to(segments_ref[pl.ds(at, 1), :].astype(F32), (BLOCK, BLOCK))
        down = along.T
        spread[b] = jnp.where(along == down, distance, FAR)
        columns[pl.ds(b * BLOCK, BLOCK), :] = jnp.where(down >= 0.0, 1.0, 0.0)
    small[0] = jnp.zeros_like(small[0])
    small[0, 8:9, :BLOCK] = jnp.sum(columns[...], axis=0, keepdims=True)

    lane = lax.broadcasted_iota(jnp.int32, (1, BLOCK), 1)
    low_lanes = jnp.where(lane < HEAD, 1.0, 0.0).astype(BF)
    high_lanes = jnp.where(lane < HEAD, 0.0, 1.0).astype(BF)

    def stacked(x):
        return jnp.concatenate([x * low_lanes, x * high_lanes], axis=0)

    def beside(x):
        return jnp.concatenate([x[:BLOCK], x[BLOCK:]], axis=1)

    for source, place, other, n in norm_copies:
        pltpu.make_async_copy(source, place, norm_sem.at[n]).wait()
        settled(other, norm_recv.at[n])

    def add_small(row, value):
        small[0, row : row + 1, :] += value

    def keep_column(r, at, value):
        columns[r] = jnp.where(lane == at, value, columns[r])

    def column(value):
        return jnp.sum(value, axis=0, keepdims=True)

    def post_norm(r, source, branch, kind, scaled_ref, result_ref):
        before = source[r].astype(F32)
        ok = columns[r, :1]
        add_small(4 + kind, column(ok * (before * before)))
        add_small(6 + kind, column(ok * (branch * branch)))
        summed = before + branch
        center = summed - lane_mean(summed)
        inverse = lax.rsqrt(lane_mean(center * center) + EPSILON)
        scaled = center * inverse
        scaled_ref[r] = scaled
        keep_column(r, 1 + kind, inverse)
        result_ref[r] = (scaled * norms[0, kind] + norms[1, kind]).astype(BF)

    def norm_back(r, grad, kind, scaled_ref):
        scaled = scaled_ref[r]
        add_small(2 * kind, column(grad * scaled))
        add_small(2 * kind + 1, column(grad))
        inner = grad * norms[0, kind]
        return columns[r, 1 + kind : 2 + kind] * (inner - lane_mean(inner) - scaled * lane_mean(inner * scaled))

    def in_step(units):
        units = list(units)
        while units:
            units = [u for u in units if next(u, units) is not units]

    def attend(m):
        r = micro_rows(m)
        joint_rows[r] = dot(rows[r], joint_w[...]).astype(BF)
        for j in range(ROWS // BLOCK):
            b = m * (ROWS // BLOCK) + j
            at = pl.ds(pl.multiple_of(b * BLOCK, BLOCK), BLOCK)
            far = spread[b]

            def pair(p, b=b, at=at, far=far):
                queries, keys, values = [joint_rows[at, pl.ds(n * D + p * BLOCK, BLOCK)] for n in range(3)]
                raw = dot_right(stacked(queries), keys)
                yield
                parts = []
                for e in range(2):
                    scores = raw[e * BLOCK : (e + 1) * BLOCK] * SCALE - SLOPES[2 * p + e] * far
                    weights = jnp.exp(scores - jnp.max(scores, axis=-1, keepdims=True))
                    parts.append(weights * (1.0 / jnp.sum(weights, axis=-1, keepdims=True)))
                soft = jnp.concatenate(parts, axis=0)
                probs[b * PAIRS + p] = soft
                yield
                mixed[at, pl.ds(p * BLOCK, BLOCK)] = dot(beside(soft.astype(BF)), stacked(values)).astype(BF)

            in_step([pair(p) for p in range(PAIRS)])
        branch = dot(mixed[r], mixing_w[...])
        post_norm(r, rows, branch, 0, scaled_first, attended)

    def feed(m):
        r = micro_rows(m)
        for k in range(CHUNKS):
            @pl.when(m == 0)
            def _(k=k):
                wait_chunk(k)

        branch = 0.0
        for k in range(CHUNKS):
            gate = dot(attended[r], gated_w[:, chunk(k)])
            up = dot(attended[r], gated_w[:, upper(k)])
            normal = 0.5 + 0.5 * lax.erf(gate * ROOT_HALF)
            density = jnp.exp(-0.5 * gate * gate) * (1.0 / ROOT_TWO_PI)
            gelu = gate * normal
            low = (gelu * up).astype(BF)
            hidden[r, chunk(k)] = low
            active[r, chunk(k)] = gelu.astype(BF)
            slope[r, chunk(k)] = (up * (normal + gate * density)).astype(BF)
            branch += dot(low, down_w[chunk(k)])
        total[...] = branch
        post_norm(r, attended, total[...], 1, scaled_second, out)

    def feed_back(m, grad):
        r = micro_rows(m)
        through = norm_back(r, grad, 1, scaled_second)
        branch_second[r] = through.astype(BF)
        for k in range(CHUNKS):
            hidden_grad = dot_right(branch_second[r], down_w[chunk(k)])
            gate_grad = (hidden_grad * slope[r, chunk(k)].astype(F32)).astype(BF)
            up_grad = (hidden_grad * active[r, chunk(k)].astype(F32)).astype(BF)
            both_grad[r, chunk(k)] = gate_grad
            both_grad[r, upper(k)] = up_grad
            through += dot_right(gate_grad, gated_w[:, chunk(k)]) + dot_right(up_grad, gated_w[:, upper(k)])
        total[...] = through

    def attend_back(m, grad):
        r = micro_rows(m)
        through = norm_back(r, grad, 0, scaled_first)
        branch_first[r] = through.astype(BF)
        total[...] = through
        mixed_grad[...] = dot_right(branch_first[r], mixing_w[...]).astype(BF)
        for j in range(ROWS // BLOCK):
            b = m * (ROWS // BLOCK) + j
            at = pl.ds(pl.multiple_of(b * BLOCK, BLOCK), BLOCK)

            def pair(p, b=b, j=j, at=at):
                lanes = [pl.ds(n * D + p * BLOCK, BLOCK) for n in range(3)]
                queries, keys, values = [joint_rows[at, n] for n in lanes]
                above = stacked(mixed_grad[j * BLOCK : (j + 1) * BLOCK, p * BLOCK : (p + 1) * BLOCK])
                soft = probs[b * PAIRS + p]
                probs_grad = dot_right(above, values)
                yield
                values_grad = dot_left(soft.astype(BF), above)
                score_grad = soft * (probs_grad - jnp.sum(probs_grad * soft, axis=-1, keepdims=True))
                score_grad = score_grad.astype(BF)
                yield
                queries_grad = SCALE * dot(beside(score_grad), stacked(keys))
                keys_grad = SCALE * dot_left(score_grad, stacked(queries))
                yield
                for n, grad_part in zip(lanes, (queries_grad, keys_grad, values_grad)):
                    joint_rows[at, n] = grad_part.astype(BF)

            in_step([pair(p) for p in range(PAIRS)])
        total[...] += dot_right(joint_rows[r], joint_w[...])

    def ahead(m):
        r = micro_rows(m)
        return remote(out.at[r], rows.at[r], ahead_send.at[m], ahead_recv.at[m], peer)

    def behind(m):
        r = micro_rows(m)
        return remote(back.at[r], upstream.at[r], behind_send.at[m], behind_recv.at[m], peer)

    front, rear = pl.ds(0, TOKENS // 2), pl.ds(TOKENS // 2, TOKENS // 2)

    wait_weights(0)

    @pl.when(plane == 0)
    def _():
        for copy in input_loads():
            copy.wait()

    def forward_step(step, carry):
        feeding = jnp.where(plane == 0, lax.div(step, MICRO), lax.rem(step, 2))
        m = jnp.where(plane == 0, lax.rem(step, MICRO), lax.div(step, 2))

        @pl.when(feeding == 0)
        def _():
            @pl.when(plane == 1)
            def _():
                ahead(m).wait_recv()

            attend(m)

        @pl.when(feeding == 1)
        def _():
            feed(m)

            @pl.when(plane == 0)
            def _():
                ahead(m).start()

        return carry

    lax.fori_loop(0, 2 * MICRO, forward_step, 0)

    @pl.when(plane == 1)
    def _():
        remote(out.at[front], swapped, swap_send, swap_recv, peer).start()

    @pl.when(plane == 1)
    def _():
        for copy in token_loads():
            copy.wait()

    def backward_step(m, carry):
        r = micro_rows(m)

        @pl.when(plane == 0)
        def _():
            behind(m).wait_recv()

        @pl.when(plane == 1)
        def _():
            upstream[r] = (columns[r, :1] * upstream[r].astype(F32)).astype(BF)

        feed_back(m, upstream[r].astype(F32))

        @pl.when((plane == 1) | (m < MICRO - 1))
        def _():
            attend_back(m, total[...].astype(BF).astype(F32))

            @pl.when(plane == 0)
            def _():
                back[r] = total[...].astype(BF)

            @pl.when(plane == 1)
            def _():
                back[r] = (total[...] + columns[r, :1] * back[r].astype(F32)).astype(BF)
                behind(m).start()

        return carry

    lax.fori_loop(0, MICRO, backward_step, 0)

    def last_attend_back():
        attend_back(MICRO - 1, total[...].astype(BF).astype(F32))
        back[pl.ds((MICRO - 1) * ROWS, ROWS)] = total[...].astype(BF)
        remote(back.at[rear], swapped, swap_send, swap_recv, peer).start()

    def staged_part(tile, a, b):
        return staged.at[lax.rem(tile, 2), pl.ds(pl.multiple_of(a * PIECE, PIECE), PIECE), pl.ds(b * WIDTH, WIDTH)]

    def keep(tile, a, b, piece):
        return pltpu.make_async_copy(staged_part(tile, a, b), mine_out.at[piece], keep_sem.at[piece])

    def give(tile, a, b, piece):
        return remote(staged_part(tile, a, b), landed_out.at[piece], give_send.at[piece], give_recv.at[piece], partner)

    def wide(k):
        return pl.ds(pl.multiple_of(k * D, D), D)

    def finish_tile(tile):
        for b in range(2):
            @pl.when(tile < 4)
            def _(b=b):
                for a in range(2):
                    piece = lax.rem(tile, 2) * 4 + 2 * a + b

                    @pl.when(lax.div(tile, 2) == core)
                    def _(a=a, piece=piece):
                        keep(tile, a, b, piece).wait()

                    @pl.when(lax.div(tile, 2) != core)
                    def _(a=a, piece=piece):
                        give(tile, a, b, piece).wait_send()

            @pl.when(tile >= 4)
            def _(b=b):
                piece = 8 + (tile - 4) * 2 + b
                keep(tile, core, b, piece).wait()
                give(tile, 1 - core, b, piece).wait_send()

    def launch_tile(tile, value):
        @pl.when(tile >= 2)
        def _():
            finish_tile(tile - 2)

        staged[lax.rem(tile, 2)] = value.astype(BF)
        for b in range(2):
            @pl.when(tile < 4)
            def _(b=b):
                for a in range(2):
                    piece = lax.rem(tile, 2) * 4 + 2 * a + b

                    @pl.when(lax.div(tile, 2) == core)
                    def _(a=a, piece=piece):
                        keep(tile, a, b, piece).start()

                    @pl.when(lax.div(tile, 2) != core)
                    def _(a=a, piece=piece):
                        give(tile, a, b, piece).start()

            @pl.when(tile >= 4)
            def _(b=b):
                piece = 8 + (tile - 4) * 2 + b
                keep(tile, core, b, piece).start()
                give(tile, 1 - core, b, piece).start()

    def down_tile(k, carry):
        launch_tile(k, dot_left(hidden[:, wide(k)], branch_second[...]))
        return carry

    def gated_tile(k, carry):
        launch_tile(4 + k, dot_left(attended[...], both_grad[:, wide(k)]))
        return carry

    def task(i):
        @pl.when(i < 6)
        def _():
            gated_tile(2 + i, 0)

        @pl.when((i == 6) & (plane == 0))
        def _():
            last_attend_back()

        @pl.when((i >= 7) & (i < 10))
        def _():
            launch_tile(5 + i, dot_left(rows[...], joint_rows[:, wide(i - 7)]))

        @pl.when(i == 10)
        def _():
            launch_tile(jnp.int32(TILES - 1), dot_left(mixed[...], branch_first[...]))

        @pl.when((i >= 11) & (i < 13))
        def _():
            finish_tile(TILES - 13 + i)

    lax.fori_loop(0, 4, down_tile, 0)
    lax.fori_loop(0, 2, gated_tile, 0)

    half = lines // 2
    mid = half - 1
    lower = z < half
    depth = jnp.where(lower, z, lines - 1 - z)
    inward = (jnp.where(lower, dp + 2, dp - 2), section)
    outward = (jnp.where(lower, dp - 2, dp + 2), section)
    my_side, other_side = y * SIDE, (1 - y) * SIDE
    pause = max(0, LAG * (2 * lines - 1) - (RING - 2))

    def window(ref, row, column, height):
        return ref.at[pl.ds(pl.multiple_of(row, 16), height), pl.ds(pl.multiple_of(column * WIDTH, WIDTH), WIDTH)]

    def slot(b):
        return lax.rem(b, RING)

    def grown(b, row=0, height=PIECE):
        return window(gated_w, row, slot(b), height)

    def sums(b, row=0, height=PIECE):
        return window(gated_w, PIECE + row, slot(b), height)

    def landed(b):
        return window(down_w, lax.rem(b, 8) * PIECE, 0, PIECE)

    def from_side(b):
        return window(down_w, lax.div(slot(b), 2) * PIECE + lax.rem(b, 2) * SIDE, 1, SIDE)

    def from_inner(n, b):
        return window(active, (2 * n + lax.div(slot(b), 8)) * SIDE, lax.rem(b, 8), SIDE)

    def from_low(b):
        return window(slope, lax.div(slot(b), 8) * RAIL, lax.rem(b, 8), RAIL)

    def from_high(b):
        return window(hidden, lax.div(slot(b), 8) * RAIL, lax.rem(b, 8), RAIL)

    def from_root(b):
        return window(slope, 2 * RAIL, lax.rem(lax.div(b, 2), 8), RAIL)

    def load_own(b):
        return pltpu.make_async_copy(mine_out.at[b], grown(b), own_sem.at[b])

    def load_other(b):
        return pltpu.make_async_copy(landed_out.at[b], landed(b), other_sem.at[b])

    def store(b):
        return pltpu.make_async_copy(sums(b), pieces_out.at[b], store_sem.at[b])

    def root_of(b):
        odd = lax.rem(b, 2)
        return jnp.where(b < PIECES // 2, odd * (lines - 1), mid + odd)

    def release_grown(b):
        root = root_of(b)
        settled(grown(b, other_side, SIDE), side_send.at[b])
        settled(grown(b, my_side, SIDE), inner_send.at[b])

        @pl.when(z != root)
        def _():
            settled(grown(b, 2 * SIDE, RAIL), up_send.at[b])

        @pl.when(z == root)
        def _():
            settled(grown(b, 2 * SIDE, RAIL), root_send.at[b])

    def release_sums(b):
        root = root_of(b)
        store(b).wait()
        settled(sums(b, my_side, SIDE), back_send.at[b])

        @pl.when(depth > 0)
        def _():
            settled(sums(b, my_side, SIDE), line_send.at[b])

        @pl.when(has_low & (z <= root))
        def _():
            settled(sums(b, 2 * SIDE, RAIL), low_send.at[b])

        @pl.when(has_high & (z >= root))
        def _():
            settled(sums(b, 2 * SIDE, RAIL), high_send.at[b])

    def load(b):
        @pl.when(b >= RING)
        def _():
            release_grown(b - RING)

        settled(landed_out.at[b], give_recv.at[b])
        load_own(b).start()
        load_other(b).start()

    def add(into, first, *others):
        value = first[...].astype(F32)
        for other in others:
            value = value + other[...].astype(F32)
        into[...] = value.astype(BF)

    def piece_at(j):
        if pause == 0:
            return j
        return jnp.where(j < RING, j, jnp.where(j < RING + pause, -1, j - pause))

    def when(active_now, b):
        return pl.when(active_now & (b >= 0) & (b < PIECES))

    def small_sum(n, source, arrival):
        settled(small_in.at[arrival], small_recv.at[arrival])
        small[n] = small[source] + small_in[arrival]

    def small_step(i):
        @pl.when(i == 14)
        def _():
            remote(small.at[0], small_in.at[0], small_send.at[0], small_recv.at[0], partner).start()

        @pl.when(i == 16)
        def _():
            small_sum(1, 0, 0)
            remote(small.at[1], small_in.at[1], small_send.at[1], small_recv.at[1], across).start()

        @pl.when(i == 18 + 2 * depth)
        def _():
            small_sum(2, 1, 1)

            @pl.when(depth > 0)
            def _():
                small_sum(3, 2, 2)

            @pl.when(depth == 0)
            def _():
                small[3] = small[2]

            into = jnp.where(depth == mid, 3, 2)
            remote(small.at[3], small_in.at[into], small_send.at[2], small_recv.at[into], inward).start()

        @pl.when(i == 20 + 2 * (2 * mid - depth))
        def _():
            @pl.when(depth == mid)
            def _():
                small_sum(4, 3, 3)

            @pl.when(depth < mid)
            def _():
                settled(small.at[4], small_recv.at[4])

            @pl.when(depth > 0)
            def _():
                remote(small.at[4], small.at[4], small_send.at[3], small_recv.at[4], outward).start()

            remote(small.at[4], small_in.at[4], small_send.at[4], small_recv.at[5], peer).start()

    def small_finish():
        settled(small_in.at[4], small_recv.at[5])
        settled(small.at[0], small_send.at[0])
        settled(small.at[1], small_send.at[1])
        settled(small.at[3], small_send.at[2])
        settled(small.at[4], small_send.at[4])

        @pl.when(depth > 0)
        def _():
            settled(small.at[4], small_send.at[3])

    def step(i, carry):
        small_step(i)

        b1 = piece_at(i - LAG * (1 + depth))

        @when(True, b1)
        def _():
            settled(from_side(b1), side_recv.at[b1])

            @pl.when(depth == 0)
            def _():
                add(grown(b1, my_side, SIDE), grown(b1, my_side, SIDE), from_side(b1))

            @pl.when(depth > 0)
            def _():
                settled(from_inner(0, b1), inner_recv.at[0, b1])
                add(grown(b1, my_side, SIDE), grown(b1, my_side, SIDE), from_side(b1), from_inner(0, b1))

            into = (depth == mid).astype(jnp.int32)
            remote(grown(b1, my_side, SIDE), from_inner(into, b1), inner_send.at[b1], inner_recv.at[into, b1], inward).start()

        b2 = piece_at(i - LAG * (2 + mid + mid - depth))

        @when(True, b2)
        def _():
            @pl.when(depth == mid)
            def _():
                settled(from_inner(1, b2), inner_recv.at[1, b2])
                add(sums(b2, my_side, SIDE), grown(b2, my_side, SIDE), from_inner(1, b2))

            @pl.when(depth < mid)
            def _():
                settled(sums(b2, my_side, SIDE), line_recv.at[b2])

            part = sums(b2, my_side, SIDE)

            @pl.when(depth > 0)
            def _():
                remote(part, part, line_send.at[b2], line_recv.at[b2], outward).start()

            remote(part, part, back_send.at[b2], back_recv.at[b2], across).start()

        b3 = piece_at(i - LAG * (3 + mid + mid - depth))

        @when(True, b3)
        def _():
            settled(sums(b3, other_side, SIDE), back_recv.at[b3])

        for early in (True, False):
            for odd in (0, 1):
                root = (odd * (lines - 1)) if early else mid + odd
                height = max(root, lines - 1 - root)
                distance = jnp.abs(z - root)

                def matches(b, root=root, odd=odd):
                    return (root_of(b) == root) & (lax.rem(b + 2 * PIECES, 2) == odd)

                hop = jnp.where(z < root, z, jnp.where(z > root, lines - 1 - z, height))
                c1 = piece_at(i - LAG * hop)

                @when((z != root) & (hop > 0) & matches(c1), c1)
                def _(root=root, c1=c1):
                    part = grown(c1, 2 * SIDE, RAIL)

                    @pl.when(z < root)
                    def _():
                        settled(from_low(c1), low_recv.at[c1])
                        add(part, part, from_low(c1))
                        remote(part, from_low(c1), up_send.at[c1], low_recv.at[c1], above).start()

                    @pl.when(z > root)
                    def _():
                        settled(from_high(c1), high_recv.at[c1])
                        add(part, part, from_high(c1))
                        remote(part, from_high(c1), up_send.at[c1], high_recv.at[c1], below).start()

                @when((z == root) & matches(c1), c1)
                def _(root=root, c1=c1):
                    part = grown(c1, 2 * SIDE, RAIL)
                    others = []
                    if root > 0:
                        settled(from_low(c1), low_recv.at[c1])
                        others.append(from_low(c1))
                    if root < lines - 1:
                        settled(from_high(c1), high_recv.at[c1])
                        others.append(from_high(c1))
                    add(part, part, *others)
                    remote(part, from_root(c1), root_send.at[c1], root_recv.at[c1], across).start()

                c2 = piece_at(i - LAG * (height + 1 + distance))

                @when(matches(c2), c2)
                def _(root=root, c2=c2):
                    part = sums(c2, 2 * SIDE, RAIL)

                    @pl.when(z == root)
                    def _():
                        settled(from_root(c2), root_recv.at[c2])
                        add(part, grown(c2, 2 * SIDE, RAIL), from_root(c2))

                    @pl.when(z != root)
                    def _():
                        settled(part, rail_recv.at[c2])

                    @pl.when(has_low & (z <= root))
                    def _():
                        remote(part, part, low_send.at[c2], rail_recv.at[c2], below).start()

                    @pl.when(has_high & (z >= root))
                    def _():
                        remote(part, part, high_send.at[c2], rail_recv.at[c2], above).start()

        b4 = piece_at(i - LAG * (2 * lines - 1))

        @when(True, b4)
        def _():
            store(b4).start()

        b5 = piece_at(i + AHEAD)

        @when(i > 0, b5)
        def _():
            load(b5)

        b0 = piece_at(i)

        @when(True, b0)
        def _():
            @pl.when(b0 >= RING)
            def _():
                release_sums(b0 - RING)

            load_own(b0).wait()
            load_other(b0).wait()
            add(grown(b0), grown(b0), landed(b0))
            remote(grown(b0, other_side, SIDE), from_side(b0), side_send.at[b0], side_recv.at[b0], across).start()
            part, root = grown(b0, 2 * SIDE, RAIL), root_of(b0)

            @pl.when((z == 0) & (root != 0))
            def _():
                remote(part, from_low(b0), up_send.at[b0], low_recv.at[b0], above).start()

            @pl.when((z == lines - 1) & (root != lines - 1))
            def _():
                remote(part, from_high(b0), up_send.at[b0], high_recv.at[b0], below).start()

        task(i)
        return carry

    signal_near(ready_sem)

    def first_load(b, carry):
        load(b)
        return carry

    lax.fori_loop(0, AHEAD + 1, first_load, 0)
    pl.semaphore_wait(ready_sem, near)
    lax.fori_loop(0, PIECES + pause + LAG * (2 * lines - 1), step, 0)
    small_finish()

    def release_last(b, carry):
        release_grown(b)
        release_sums(b)
        return carry

    lax.fori_loop(PIECES - RING, PIECES, release_last, 0)

    remote(out.at[front], swapped, swap_send, swap_recv, peer).wait_recv()

    def writes(which):
        pairs = [
            [(out.at[front], first_out), (swapped, second_out), (back.at[front], input_out), (upstream.at[front], middle_out)],
            [(rows.at[rear], first_out), (out.at[rear], second_out), (swapped, input_out), (back.at[rear], middle_out)],
        ][which]
        return [pltpu.make_async_copy(a, b, out_sem.at[n]) for n, (a, b) in enumerate(pairs)]

    for which in range(2):
        @pl.when(plane == which)
        def _(which=which):
            for copy in writes(which):
                copy.start()

    for n, (source, target) in enumerate(((small.at[4], small_out), (small_in.at[4], other_out))):
        small_copy = pltpu.make_async_copy(source, target, out_sem.at[4 + n])
        small_copy.start()
        small_copy.wait()

    for which in range(2):
        @pl.when(plane == which)
        def _(which=which):
            for copy in writes(which):
                copy.wait()

    remote(out.at[front], swapped, swap_send, swap_recv, peer).wait_send()
    for m in range(MICRO):
        @pl.when(plane == 0)
        def _(m=m):
            ahead(m).wait_send()

        @pl.when(plane == 1)
        def _(m=m):
            behind(m).wait_send()

    for n, (source, place, _, _) in enumerate(norm_copies):
        remote(source, place, norm_send.at[n], norm_recv.at[n], partner).wait_send()
    wait_weights_sent(0)
    wait_weights_sent(1)


def run_layer(lines, inputs, first, second, segments, joint, mixing, gated, down, gain, bias):
    sems = lambda *s: pltpu.SemaphoreType.DMA(s)
    half = TOKENS // 2
    copies = 2 + 3 * CHUNKS
    any_spec, vmem = pl.BlockSpec(memory_space=pl.ANY), pl.BlockSpec(memory_space=pltpu.VMEM)
    rows_out = jax.ShapeDtypeStruct((half, D), BF)
    pieces = jax.ShapeDtypeStruct((PIECES, PIECE, WIDTH), BF)
    block = jax.ShapeDtypeStruct((SMALL, D), F32)
    tokens, hiddens = pltpu.VMEM((TOKENS, D), BF), pltpu.VMEM((TOKENS, FF), BF)
    return pl.pallas_call(
        functools.partial(layer_kernel, lines),
        out_shape=[rows_out] * 4 + [pieces] * 3 + [block] * 2,
        in_specs=[any_spec] * 3 + [vmem] + [any_spec] * 6,
        out_specs=[any_spec] * 9,
        scratch_shapes=[
            pltpu.VMEM((D, 3 * D), BF), pltpu.VMEM((D, D), BF), pltpu.VMEM((D, 2 * FF), BF), pltpu.VMEM((FF, D), BF),
            pltpu.VMEM((2, 2, 1, D), F32),
            tokens, tokens, tokens, pltpu.VMEM((half, D), BF), tokens, tokens,
            pltpu.VMEM((TOKENS, 3 * D), BF),
            pltpu.VMEM((TOKENS // BLOCK * PAIRS, 2 * BLOCK, BLOCK), F32),
            tokens, hiddens, hiddens, hiddens, pltpu.VMEM((TOKENS, 2 * FF), BF),
            tokens, tokens, pltpu.VMEM((TOKENS, D), F32), pltpu.VMEM((TOKENS, D), F32),
            pltpu.VMEM((TOKENS // BLOCK, BLOCK, BLOCK), F32), pltpu.VMEM((TOKENS, BLOCK), F32),
            pltpu.VMEM((ROWS, D), F32), pltpu.VMEM((5, SMALL, D), F32), pltpu.VMEM((5, SMALL, D), F32),
            pltpu.VMEM((ROWS, D), BF), pltpu.VMEM((2, D, D), BF),
            sems(6), sems(copies), sems(copies), sems(copies), sems(2), sems(2), sems(2),
            sems(MICRO), sems(MICRO), sems(MICRO), sems(MICRO), pltpu.SemaphoreType.DMA, pltpu.SemaphoreType.DMA, sems(6),
            sems(PIECES), sems(PIECES), sems(PIECES), pltpu.SemaphoreType.REGULAR,
            sems(PIECES), sems(PIECES), sems(PIECES), sems(5), sems(6), sems(PIECES), sems(PIECES), sems(PIECES), sems(2, PIECES),
            sems(PIECES), sems(PIECES), sems(PIECES), sems(PIECES), sems(PIECES), sems(PIECES), sems(PIECES),
            sems(PIECES), sems(PIECES), sems(PIECES), sems(PIECES), sems(PIECES),
        ],
        compiler_params=pltpu.CompilerParams(collective_id=2, has_side_effects=True, vmem_limit_bytes=62 * 2**20),
    )(inputs, first, second, segments, joint, mixing, gated, down, gain, bias)


def place_kernel(
    pieces_ref, small_ref, other_ref, first_ref, second_ref, input_ref, middle_ref,
    first_out, second_out, input_out, middle_out, joint_out, mixing_out, gated_out, down_out, gain_out, bias_out, stats_out,
    held, wide, passed, load_sem, store_sem, pass_sem,
):
    section = lax.axis_index("section")
    plane, core = lax.div(section, 2), lax.rem(section, 2)
    loads = [pltpu.make_async_copy(pieces_ref.at[p], held.at[p], load_sem.at[p]) for p in range(PIECES)]
    for load in loads:
        load.start()
    pairs = ((first_ref, first_out), (second_ref, second_out), (input_ref, input_out), (middle_ref, middle_out))
    takes = [pltpu.make_async_copy(a, passed.at[n], pass_sem.at[n]) for n, (a, _) in enumerate(pairs)]
    passes = [pltpu.make_async_copy(passed.at[n], b, pass_sem.at[4 + n]) for n, (_, b) in enumerate(pairs)]
    for copy in takes:
        copy.start()

    def place(piece):
        if piece < 8:
            return down_out.at[pl.ds(piece // 2 * PIECE, PIECE), pl.ds(piece % 2 * WIDTH, WIDTH)]
        if piece < 24:
            return gated_out.at[:, pl.ds((piece - 8) * WIDTH, WIDTH)]
        if piece < 30:
            return joint_out.at[:, pl.ds((piece - 24) * WIDTH, WIDTH)]
        return mixing_out.at[:, pl.ds((piece - 30) * WIDTH, WIDTH)]

    stores = [pltpu.make_async_copy(wide.at[p % SLOTS], place(p), store_sem.at[p % SLOTS]) for p in range(PIECES)]
    for p in range(PIECES):
        loads[p].wait()
        if p >= SLOTS:
            stores[p - SLOTS].wait()
        wide[p % SLOTS] = held[p].astype(F32)
        stores[p].start()

    for take, copy in zip(takes, passes):
        take.wait()
        copy.start()

    gain_out[...] = small_ref[pl.ds(2 * core, 1), :]
    bias_out[...] = small_ref[pl.ds(2 * core + 1, 1), :]
    count = small_ref[8:9, :1] * D
    row = lax.broadcasted_iota(jnp.int32, (2, 4), 0)
    lane = lax.broadcasted_iota(jnp.int32, (2, 4), 1)
    stats = jnp.zeros((2, 4), F32)
    for n in range(4):
        for at, source in ((2 * plane, small_ref), (2 - 2 * plane, other_ref)):
            value = jnp.sum(source[4 + n : 5 + n, :], axis=1, keepdims=True) / count
            stats = jnp.where((row == n // 2) & (lane == at + n % 2), jnp.sqrt(value), stats)
    stats_out[...] = stats
    for p in range(PIECES - SLOTS, PIECES):
        stores[p].wait()
    for copy in passes:
        copy.wait()


def place_results(pieces, small, other, *rows):
    any_spec, vmem = pl.BlockSpec(memory_space=pl.ANY), pl.BlockSpec(memory_space=pltpu.VMEM)
    shapes = ((HALF, 3 * D), (HALF, D), (HALF, 2 * FF), (FF // 2, D), (1, D), (1, D), (2, 4))
    return pl.pallas_call(
        place_kernel,
        out_shape=[jax.ShapeDtypeStruct(r.shape, BF) for r in rows] + [jax.ShapeDtypeStruct(s, F32) for s in shapes],
        in_specs=[any_spec, vmem, vmem] + [any_spec] * 4,
        out_specs=[any_spec] * 8 + [vmem] * 3,
        scratch_shapes=[
            pltpu.VMEM((PIECES, PIECE, WIDTH), BF), pltpu.VMEM((SLOTS, PIECE, WIDTH), F32),
            pltpu.VMEM((4,) + rows[0].shape, BF),
            pltpu.SemaphoreType.DMA((PIECES,)), pltpu.SemaphoreType.DMA((SLOTS,)), pltpu.SemaphoreType.DMA((8,)),
        ],
        compiler_params=pltpu.CompilerParams(vmem_limit_bytes=61 * 2**20),
    )(pieces, small, other, *rows)


def per_device(
    inputs, cotangent_first, cotangent_second, segment_ids,
    joint_projection, mixing_weight, gated_weight, down_weight, norm_gain, norm_bias,
):
    segments = segment_ids.reshape(-1, BLOCK)
    *rows, _, _, pieces, small, other = run_layer(
        lax.axis_size("dp") // 2, inputs, cotangent_first, cotangent_second, segments,
        joint_projection, mixing_weight, gated_weight, down_weight, norm_gain, norm_bias,
    )
    return tuple(place_results(pieces, small, other, *rows))


def solution(mesh):
    tokens, rows = P("dp", None), P("section", None)
    return jax.shard_map(
        per_device,
        mesh=mesh,
        in_specs=(tokens, tokens, tokens, P("dp"), rows, rows, rows, rows, rows, rows),
        out_specs=(P(("dp", "section"), None),) * 4 + (rows,) * 6 + (P(),),
        check_vma=False,
    )
```

```python
import functools

import jax
import jax.numpy as jnp
from jax import lax
from jax.experimental import pallas as pl
from jax.experimental.pallas import tpu as pltpu
from jax.sharding import PartitionSpec as P

D = 768
HEADS = 12
HEAD = D // HEADS
FF = 3072
BLOCK = 128
HALF = D // 2
PAIRS = HEADS // 2
TOKENS = 512
MICRO = 2
ROWS = TOKENS // MICRO
CHUNK = 1024
PART = 512
CHUNKS = FF // CHUNK
SMALL = 16
PIECES = 32
PIECE = 384
SIDE = 128
RAIL = 128
WIDTH = 384
AHEAD = 3
LAG = 2
RING = 16
BLOCKS = ROWS // BLOCK
TILES = 16
SLOTS = 8

EPSILON = 1e-05
FAR = 1e30
ROOT_HALF = 0.7071067811865476
ROOT_TWO_PI = 2.5066282746310002
SCALE = HEAD**-0.5

MESH = pl.DeviceIdType.MESH
BF = jnp.bfloat16
F32 = jnp.float32


def alibi_slopes():
    closest = 1 << HEADS.bit_length() - 1
    first_slope = 2.0 ** (-8.0 / closest)
    slopes = [first_slope ** (power_index + 1) for power_index in range(closest)]
    double_slope = 2.0 ** (-8.0 / (2 * closest))
    extra_slopes = [double_slope ** (power_index + 1) for power_index in range(2 * closest)]
    return slopes + extra_slopes[0::2][: HEADS - closest]


SLOPES = alibi_slopes()


def dot(a, b):
    return jnp.dot(a, b, preferred_element_type=F32)


def dot_right(a, b):
    return lax.dot_general(a, b, (((1,), (1,)), ((), ())), preferred_element_type=F32)


def dot_left(a, b):
    return lax.dot_general(a, b, (((0,), (0,)), ((), ())), preferred_element_type=F32)


def lane_mean(x):
    return jnp.sum(x, axis=-1, keepdims=True) * (1.0 / D)


def remote(src, dst, send, recv, device):
    return pltpu.make_async_remote_copy(
        src_ref=src, dst_ref=dst, send_sem=send, recv_sem=recv, device_id=device, device_id_type=MESH
    )


def settled(ref, sem):
    pltpu.make_async_copy(ref, ref, sem).wait()


def layer_kernel(
    lines,
    inputs_ref, first_ref, second_ref, segments_ref, joint_ref, mixing_ref, gated_ref, down_ref, gain_ref, bias_ref,
    first_out, second_out, input_out, middle_out, mine_out, landed_out, pieces_out, small_out, other_out,
    joint_w, mixing_w, gated_w, down_w, norms,
    rows, attended, out, swapped, upstream, back,
    joint_rows, probs, mixed, hidden, active, slope, both_grad,
    branch_first, branch_second, scaled_first, scaled_second, spread, columns,
    total, small, small_in, mixed_grad, staged, high,
    load_sem, local_sem, weight_send, weight_recv, norm_sem, norm_send, norm_recv,
    ahead_send, ahead_recv, behind_send, behind_recv, swap_send, swap_recv, out_sem,
    keep_sem, give_send, give_recv, ready_sem,
    own_sem, other_sem, store_sem, small_send, small_recv, side_send, side_recv, inner_send, inner_recv,
    up_send, low_recv, high_recv, root_recv, line_send, back_send, back_recv, low_send, high_send,
):
    dp, section = lax.axis_index("dp"), lax.axis_index("section")
    plane, core = lax.div(section, 2), lax.rem(section, 2)
    partner = (dp, section + 1 - 2 * core)
    peer = (dp, section + 2 - 4 * plane)

    y, z = lax.rem(dp, 2), lax.div(dp, 2)
    across, below, above = (dp + 1 - 2 * y, section), (dp - 2, section), (dp + 2, section)
    has_low, has_high = z > 0, z < lines - 1
    near = 1 + has_low.astype(jnp.int32) + has_high.astype(jnp.int32)

    def signal_near(semaphore):
        pl.semaphore_signal(semaphore, inc=1, device_id=across, device_id_type=MESH)

        @pl.when(has_low)
        def _():
            pl.semaphore_signal(semaphore, inc=1, device_id=below, device_id_type=MESH)

        @pl.when(has_high)
        def _():
            pl.semaphore_signal(semaphore, inc=1, device_id=above, device_id_type=MESH)

    barrier = pltpu.get_barrier_semaphore()
    pl.semaphore_signal(barrier, inc=1, device_id=partner, device_id_type=MESH)
    pl.semaphore_signal(barrier, inc=1, device_id=peer, device_id_type=MESH)
    signal_near(barrier)
    pl.semaphore_wait(barrier, 2 + near)

    mine = pl.ds(pl.multiple_of(core * HALF, HALF), HALF)
    theirs = pl.ds(pl.multiple_of((1 - core) * HALF, HALF), HALF)

    def micro_rows(m):
        return pl.ds(pl.multiple_of(m * ROWS, ROWS), ROWS)

    def token_loads():
        copies = []
        for m in range(2):
            there = pl.ds(pl.multiple_of((2 * m + core) * (TOKENS // 2), TOKENS // 2), TOKENS // 2)
            here = pl.ds(m * (TOKENS // 2), TOKENS // 2)
            copies.append(pltpu.make_async_copy(first_ref.at[there], back.at[here], load_sem.at[2 * m]))
            copies.append(pltpu.make_async_copy(second_ref.at[there], upstream.at[here], load_sem.at[2 * m + 1]))
        return copies

    def input_loads():
        copies = []
        for m in range(2):
            there = pl.ds(pl.multiple_of((2 * m + core) * (TOKENS // 2), TOKENS // 2), TOKENS // 2)
            here = pl.ds(m * (TOKENS // 2), TOKENS // 2)
            copies.append(pltpu.make_async_copy(inputs_ref.at[there], rows.at[here], load_sem.at[4 + m]))
        return copies

    def chunk(k):
        return pl.ds(pl.multiple_of(k * CHUNK, CHUNK), CHUNK)

    def upper(k):
        return pl.ds(pl.multiple_of(FF + k * CHUNK, CHUNK), CHUNK)

    def weight_copies(which):
        if which == 0:
            return [(joint_ref, joint_w.at[mine], joint_w.at[theirs], 0), (mixing_ref, mixing_w.at[mine], mixing_w.at[theirs], 1)]
        copies = []
        for k in range(CHUNKS):
            for n, columns_at in enumerate((chunk(k), upper(k))):
                copies.append((gated_ref.at[:, columns_at], gated_w.at[mine, columns_at], gated_w.at[theirs, columns_at], 2 + 2 * k + n))
            here = pl.ds(pl.multiple_of(core * (FF // 2) + k * PART, PART), PART)
            there = pl.ds(pl.multiple_of((1 - core) * (FF // 2) + k * PART, PART), PART)
            copies.append((down_ref.at[pl.ds(k * PART, PART)], down_w.at[here], down_w.at[there], 2 + 2 * CHUNKS + k))
        return copies

    def start_weights(which):
        for source, place, _, n in weight_copies(which):
            remote(source, place, weight_send.at[n], weight_recv.at[n], partner).start()
            pltpu.make_async_copy(source, place, local_sem.at[n]).start()

    def wait_weights(which):
        for source, place, other, n in weight_copies(which):
            pltpu.make_async_copy(source, place, local_sem.at[n]).wait()
            settled(other, weight_recv.at[n])

    def wait_chunk(k):
        for source, place, other, n in weight_copies(1)[3 * k : 3 * k + 2]:
            pltpu.make_async_copy(source, place, local_sem.at[n]).wait()
            settled(other, weight_recv.at[n])
        for part in (2 * k, 2 * k + 1):
            source, _, _, n = weight_copies(1)[3 * (part % CHUNKS) + 2]
            place = down_w.at[pl.ds(part * PART, PART)]

            @pl.when(core == part // CHUNKS)
            def _():
                pltpu.make_async_copy(source, place, local_sem.at[n]).wait()

            @pl.when(core != part // CHUNKS)
            def _():
                settled(place, weight_recv.at[n])

    def wait_weights_sent(which):
        for source, place, _, n in weight_copies(which):
            remote(source, place, weight_send.at[n], weight_recv.at[n], partner).wait_send()

    norm_copies = []
    for n, source in enumerate((gain_ref, bias_ref)):
        norm_copies.append((source, norms.at[n, core], norms.at[n, 1 - core], n))
    for source, place, _, n in norm_copies:
        remote(source, place, norm_send.at[n], norm_recv.at[n], partner).start()
        pltpu.make_async_copy(source, place, norm_sem.at[n]).start()
    start_weights(0)

    @pl.when(plane == 0)
    def _():
        for copy in input_loads():
            copy.start()

    @pl.when(plane == 1)
    def _():
        for copy in token_loads():
            copy.start()

    start_weights(1)

    first = lax.broadcasted_iota(jnp.int32, (BLOCK, BLOCK), 0)
    second = lax.broadcasted_iota(jnp.int32, (BLOCK, BLOCK), 1)
    distance = jnp.abs(first - second).astype(F32)
    half_blocks = TOKENS // (2 * BLOCK)
    for b in range(TOKENS // BLOCK):
        at = (2 * (b // half_blocks) + core) * half_blocks + b % half_blocks
        along = jnp.broadcast_to(segments_ref[pl.ds(at, 1), :].astype(F32), (BLOCK, BLOCK))
        down = along.T
        spread[b] = jnp.where(along == down, distance, FAR)
        columns[pl.ds(b * BLOCK, BLOCK), :] = jnp.where(down >= 0.0, 1.0, 0.0)
    small[0] = jnp.zeros_like(small[0])
    small[0, 8:9, :BLOCK] = jnp.sum(columns[...], axis=0, keepdims=True)

    lane = lax.broadcasted_iota(jnp.int32, (1, BLOCK), 1)
    low_lanes = jnp.where(lane < HEAD, 1.0, 0.0).astype(BF)
    high_lanes = jnp.where(lane < HEAD, 0.0, 1.0).astype(BF)

    def stacked(x):
        return jnp.concatenate([x * low_lanes, x * high_lanes], axis=0)

    def beside(x):
        return jnp.concatenate([x[:BLOCK], x[BLOCK:]], axis=1)

    for source, place, other, n in norm_copies:
        pltpu.make_async_copy(source, place, norm_sem.at[n]).wait()
        settled(other, norm_recv.at[n])

    def add_small(row, value):
        small[0, row : row + 1, :] += value

    def keep_column(r, at, value):
        columns[r] = jnp.where(lane == at, value, columns[r])

    def column(value):
        return jnp.sum(value, axis=0, keepdims=True)

    def post_norm(r, source, branch, kind, scaled_ref, result_ref):
        before = source[r].astype(F32)
        ok = columns[r, :1]
        add_small(4 + kind, column(ok * (before * before)))
        add_small(6 + kind, column(ok * (branch * branch)))
        summed = before + branch
        center = summed - lane_mean(summed)
        inverse = lax.rsqrt(lane_mean(center * center) + EPSILON)
        scaled = center * inverse
        scaled_ref[r] = scaled
        keep_column(r, 1 + kind, inverse)
        result_ref[r] = (scaled * norms[0, kind] + norms[1, kind]).astype(BF)

    def norm_back(r, grad, kind, scaled_ref):
        scaled = scaled_ref[r]
        add_small(2 * kind, column(grad * scaled))
        add_small(2 * kind + 1, column(grad))
        inner = grad * norms[0, kind]
        return columns[r, 1 + kind : 2 + kind] * (inner - lane_mean(inner) - scaled * lane_mean(inner * scaled))

    def in_step(units):
        units = list(units)
        while units:
            units = [u for u in units if next(u, units) is not units]

    def block_rows(b):
        return pl.ds(pl.multiple_of(b * BLOCK, BLOCK), BLOCK)

    def ahead(b):
        r = block_rows(b)
        return remote(out.at[r], rows.at[r], ahead_send.at[b], ahead_recv.at[b], peer)

    def behind(b):
        r = block_rows(b)
        return remote(back.at[r], upstream.at[r], behind_send.at[b], behind_recv.at[b], peer)

    front, rear = pl.ds(0, TOKENS // 2), pl.ds(TOKENS // 2, TOKENS // 2)

    def attend(m):
        r = micro_rows(m)
        for j in range(BLOCKS):
            b = m * BLOCKS + j

            @pl.when(plane == 1)
            def _(b=b):
                ahead(b).wait_recv()

            at = block_rows(b)
            joint_rows[at] = dot(rows[at], joint_w[...]).astype(BF)
            far = spread[b]

            def pair(p, b=b, at=at, far=far):
                queries, keys, values = [joint_rows[at, pl.ds(n * D + p * BLOCK, BLOCK)] for n in range(3)]
                raw = dot_right(stacked(queries), keys)
                yield
                parts = []
                for e in range(2):
                    scores = raw[e * BLOCK : (e + 1) * BLOCK] * SCALE - SLOPES[2 * p + e] * far
                    weights = jnp.exp(scores - jnp.max(scores, axis=-1, keepdims=True))
                    parts.append(weights * (1.0 / jnp.sum(weights, axis=-1, keepdims=True)))
                soft = jnp.concatenate(parts, axis=0)
                probs[b * PAIRS + p] = soft
                yield
                mixed[at, pl.ds(p * BLOCK, BLOCK)] = dot(beside(soft.astype(BF)), stacked(values)).astype(BF)

            in_step([pair(p) for p in range(PAIRS)])
        branch = dot(mixed[r], mixing_w[...])
        post_norm(r, rows, branch, 0, scaled_first, attended)

    def feed(m, arriving):
        r = micro_rows(m)
        branch = 0.0
        for k in range(CHUNKS):
            if arriving:
                wait_chunk(k)
            gate = dot(attended[r], gated_w[:, chunk(k)])
            up = dot(attended[r], gated_w[:, upper(k)])
            normal = 0.5 + 0.5 * lax.erf(gate * ROOT_HALF)
            density = jnp.exp(-0.5 * gate * gate) * (1.0 / ROOT_TWO_PI)
            gelu = gate * normal
            low = (gelu * up).astype(BF)
            hidden[r, chunk(k)] = low
            active[r, chunk(k)] = gelu.astype(BF)
            slope[r, chunk(k)] = (up * (normal + gate * density)).astype(BF)
            if arriving:
                total[...] = dot(low, down_w[chunk(k)]) + (total[...] if k else 0.0)
            else:
                branch += dot(low, down_w[chunk(k)])
        if not arriving:
            total[...] = branch
        post_norm(r, attended, total[...], 1, scaled_second, out)

    def feed_back(m, grad):
        r = micro_rows(m)
        through = norm_back(r, grad, 1, scaled_second)
        branch_second[r] = through.astype(BF)
        for k in range(CHUNKS):
            hidden_grad = dot_right(branch_second[r], down_w[chunk(k)])
            gate_grad = (hidden_grad * slope[r, chunk(k)].astype(F32)).astype(BF)
            up_grad = (hidden_grad * active[r, chunk(k)].astype(F32)).astype(BF)
            both_grad[r, chunk(k)] = gate_grad
            both_grad[r, upper(k)] = up_grad
            through += dot_right(gate_grad, gated_w[:, chunk(k)]) + dot_right(up_grad, gated_w[:, upper(k)])
        total[...] = through

    def attend_back(m, grad):
        r = micro_rows(m)
        through = norm_back(r, grad, 0, scaled_first)
        branch_first[r] = through.astype(BF)
        total[...] = through
        mixed_grad[...] = dot_right(branch_first[r], mixing_w[...]).astype(BF)
        for j in range(BLOCKS):
            b = m * BLOCKS + j
            at = block_rows(b)

            def pair(p, b=b, j=j, at=at):
                lanes = [pl.ds(n * D + p * BLOCK, BLOCK) for n in range(3)]
                queries, keys, values = [joint_rows[at, n] for n in lanes]
                above = stacked(mixed_grad[j * BLOCK : (j + 1) * BLOCK, p * BLOCK : (p + 1) * BLOCK])
                soft = probs[b * PAIRS + p]
                probs_grad = dot_right(above, values)
                yield
                values_grad = dot_left(soft.astype(BF), above)
                score_grad = soft * (probs_grad - jnp.sum(probs_grad * soft, axis=-1, keepdims=True))
                score_grad = score_grad.astype(BF)
                yield
                queries_grad = SCALE * dot(beside(score_grad), stacked(keys))
                keys_grad = SCALE * dot_left(score_grad, stacked(queries))
                yield
                for n, grad_part in zip(lanes, (queries_grad, keys_grad, values_grad)):
                    joint_rows[at, n] = grad_part.astype(BF)

            in_step([pair(p) for p in range(PAIRS)])
            grad_rows = total[j * BLOCK : (j + 1) * BLOCK, :] + dot_right(joint_rows[at], joint_w[...])

            @pl.when(plane == 0)
            def _(at=at, grad_rows=grad_rows):
                back[at] = grad_rows.astype(BF)

            @pl.when(plane == 1)
            def _(b=b, at=at, grad_rows=grad_rows):
                back[at] = (grad_rows + columns[at, :1] * back[at].astype(F32)).astype(BF)
                behind(b).start()


    wait_weights(0)

    @pl.when(plane == 0)
    def _():
        for copy in input_loads():
            copy.wait()

    def forward_step(step, carry):
        feeding = jnp.where(plane == 0, lax.div(step, MICRO), lax.rem(step, 2))
        m = jnp.where(plane == 0, lax.rem(step, MICRO), lax.div(step, 2))

        @pl.when(feeding == 0)
        def _():
            attend(m)

        @pl.when(feeding == 1)
        def _():
            @pl.when(m == 0)
            def _():
                feed(0, True)

            @pl.when(m > 0)
            def _():
                feed(m, False)

            @pl.when(plane == 0)
            def _():
                for j in range(BLOCKS):
                    ahead(m * BLOCKS + j).start()

        return carry

    lax.fori_loop(0, 2 * MICRO, forward_step, 0)

    @pl.when(plane == 1)
    def _():
        remote(out.at[front], swapped, swap_send, swap_recv, peer).start()

    @pl.when(plane == 1)
    def _():
        for copy in token_loads():
            copy.wait()

    def backward_step(m, carry):
        r = micro_rows(m)

        @pl.when(plane == 0)
        def _():
            for j in range(BLOCKS):
                behind(m * BLOCKS + j).wait_recv()

        @pl.when(plane == 1)
        def _():
            upstream[r] = (columns[r, :1] * upstream[r].astype(F32)).astype(BF)

        feed_back(m, upstream[r].astype(F32))

        @pl.when((plane == 1) | (m < MICRO - 1))
        def _():
            attend_back(m, total[...].astype(BF).astype(F32))

        return carry

    lax.fori_loop(0, MICRO, backward_step, 0)

    def last_attend_back():
        attend_back(MICRO - 1, total[...].astype(BF).astype(F32))
        remote(back.at[rear], swapped, swap_send, swap_recv, peer).start()

    def pairs(n, height):
        tile = tile_of(n)
        row = jnp.where(tile < 4, lax.rem(tile, 2) * D, tile * PIECE)
        return pl.ds(pl.multiple_of(row, PIECE), height)

    def half_tile(n, which):
        return staged.at[lax.rem(n, 2), pl.ds(pl.multiple_of(which * PIECE, PIECE), PIECE)]

    def keep(n, source, height):
        return pltpu.make_async_copy(source, mine_out.at[pairs(n, height)], keep_sem.at[lax.rem(n, 2)])

    def give(n, source, height):
        unit = jnp.where(n < 4, lax.rem(tile_of(n), 2), n - 2)
        return remote(source, landed_out.at[pairs(n, height)], give_send.at[lax.rem(n, 2)], give_recv.at[unit], partner)

    def wide(k):
        return pl.ds(pl.multiple_of(k * D, D), D)

    def tile_of(n):
        return n + (n == 1).astype(jnp.int32) - (n == 2).astype(jnp.int32)

    def each_part(n, kept, given):
        tile = tile_of(n)

        @pl.when((tile < 4) & (lax.div(tile, 2) == core))
        def _():
            kept(keep(n, staged.at[lax.rem(n, 2)], D))

        @pl.when((tile < 4) & (lax.div(tile, 2) != core))
        def _():
            given(give(n, staged.at[lax.rem(n, 2)], D))

        @pl.when(tile >= 4)
        def _():
            kept(keep(n, half_tile(n, core), PIECE))
            given(give(n, half_tile(n, 1 - core), PIECE))

    def finish(n):
        each_part(n, lambda copy: copy.wait(), lambda copy: copy.wait_send())

    def launch(n, value):
        staged[lax.rem(n, 2)] = value.astype(BF)
        each_part(n, lambda copy: copy.start(), lambda copy: copy.start())

    def down_tile(n):
        launch(n, dot_left(hidden[:, wide(tile_of(n))], branch_second[...]))

    def task(i):
        n = i + 3

        @pl.when(i == 0)
        def _():
            down_tile(n)
            finish(n - 1)

        @pl.when((i > 0) & (i < 9))
        def _():
            launch(n, dot_left(attended[...], both_grad[:, wide(n - 4)]))
            finish(n - 1)

        @pl.when((i == 9) & (plane == 0))
        def _():
            last_attend_back()

        @pl.when((i >= 10) & (i < 13))
        def _():
            launch(n - 1, dot_left(rows[...], joint_rows[:, wide(n - 13)]))
            finish(n - 2)

        @pl.when(i == 13)
        def _():
            launch(n - 1, dot_left(mixed[...], branch_first[...]))
            finish(n - 2)

        @pl.when(i == 14)
        def _():
            finish(n - 2)

    signal_near(ready_sem)
    down_first = [jnp.int32(n) for n in range(3)]
    down_tile(down_first[0])
    down_tile(down_first[1])
    finish(down_first[0])
    down_tile(down_first[2])
    finish(down_first[1])
    half = lines // 2
    mid = half - 1
    lower = z < half
    depth = jnp.where(lower, z, lines - 1 - z)
    inward = (jnp.where(lower, dp + 2, dp - 2), section)
    outward = (jnp.where(lower, dp - 2, dp + 2), section)
    my_side, other_side = y * SIDE, (1 - y) * SIDE
    pause = max(0, LAG * (2 * lines - 1) - (RING - 2))

    def window(ref, row, column, height):
        return ref.at[pl.ds(pl.multiple_of(row, 16), height), pl.ds(pl.multiple_of(column * WIDTH, WIDTH), WIDTH)]

    def slot(b):
        return lax.rem(b, RING)

    def grown(b, row=0, height=PIECE):
        return window(gated_w, row, slot(b), height)

    def sums(b, row=0, height=PIECE):
        return window(gated_w, PIECE + row, slot(b), height)

    def landed(b):
        return window(down_w, lax.rem(b, 8) * PIECE, 0, PIECE)

    def from_side(b):
        return window(down_w, lax.div(slot(b), 2) * PIECE + lax.rem(b, 2) * SIDE, 1, SIDE)

    def from_inner(n, b):
        return window(active, (2 * n + lax.div(slot(b), 8)) * SIDE, lax.rem(b, 8), SIDE)

    def from_low(b):
        return window(slope, lax.div(slot(b), 8) * RAIL, lax.rem(b, 8), RAIL)

    def from_high(b):
        return high.at[slot(b)]

    def from_root(b):
        return window(slope, 2 * RAIL, lax.rem(lax.div(b, 2), 8), RAIL)

    def from_pair(ref, b):
        row = pl.multiple_of(lax.div(b, 2) * PIECE, PIECE)
        return ref.at[pl.ds(row, PIECE), pl.ds(pl.multiple_of(lax.rem(b, 2) * WIDTH, WIDTH), WIDTH)]

    def load_own(b):
        return pltpu.make_async_copy(from_pair(mine_out, b), grown(b), own_sem.at[lax.rem(b, AHEAD + 1)])

    def load_other(b):
        return pltpu.make_async_copy(from_pair(landed_out, b), landed(b), other_sem.at[lax.rem(b, AHEAD + 1)])

    def store(b):
        return pltpu.make_async_copy(sums(b), pieces_out.at[b], store_sem.at[slot(b)])

    def root_of(b):
        odd = lax.rem(b, 2)
        return jnp.where(b < PIECES // 2, odd * (lines - 1), mid + odd)

    def release_grown(b):
        root = root_of(b)
        settled(grown(b, other_side, SIDE), side_send.at[slot(b)])
        settled(grown(b, my_side, SIDE), inner_send.at[slot(b)])

        @pl.when(z != root)
        def _():
            settled(grown(b, 2 * SIDE, RAIL), up_send.at[slot(b)])

        @pl.when(z == root)
        def _():
            settled(grown(b, 2 * SIDE, RAIL), up_send.at[slot(b)])

    def release_sums(b):
        root = root_of(b)
        store(b).wait()
        settled(sums(b, my_side, SIDE), back_send.at[slot(b)])

        @pl.when(depth > 0)
        def _():
            settled(sums(b, my_side, SIDE), line_send.at[slot(b)])

        @pl.when(has_low & (z <= root))
        def _():
            settled(sums(b, 2 * SIDE, RAIL), low_send.at[slot(b)])

        @pl.when(has_high & (z >= root))
        def _():
            settled(sums(b, 2 * SIDE, RAIL), high_send.at[slot(b)])

    def load(b):
        @pl.when(b >= RING)
        def _():
            release_grown(b - RING)

        @pl.when((b < 8) & (lax.rem(b, 4) == 0))
        def _():
            settled(landed_out.at[pl.ds(0, D)], give_recv.at[lax.div(b, 4)])

        @pl.when((b >= 8) & (lax.rem(b, 2) == 0))
        def _():
            settled(landed_out.at[pl.ds(0, PIECE)], give_recv.at[lax.div(b, 2) - 2])

        load_own(b).start()
        load_other(b).start()

    def add(into, first, *others):
        value = first[...].astype(F32)
        for other in others:
            value = value + other[...].astype(F32)
        into[...] = value.astype(BF)

    def piece_at(j):
        if pause == 0:
            return j
        return jnp.where(j < RING, j, jnp.where(j < RING + pause, -1, j - pause))

    def when(active_now, b):
        return pl.when(active_now & (b >= 0) & (b < PIECES))

    def small_sum(n, source, arrival):
        settled(small_in.at[arrival], small_recv.at[arrival])
        small[n] = small[source] + small_in[arrival]

    def small_step(i):
        @pl.when(i == 14)
        def _():
            remote(small.at[0], small_in.at[0], small_send.at[0], small_recv.at[0], partner).start()

        @pl.when(i == 16)
        def _():
            small_sum(1, 0, 0)
            remote(small.at[1], small_in.at[1], small_send.at[1], small_recv.at[1], across).start()

        @pl.when(i == 18 + 2 * depth)
        def _():
            small_sum(2, 1, 1)

            @pl.when(depth > 0)
            def _():
                small_sum(3, 2, 2)

            @pl.when(depth == 0)
            def _():
                small[3] = small[2]

            into = jnp.where(depth == mid, 3, 2)
            remote(small.at[3], small_in.at[into], small_send.at[2], small_recv.at[into], inward).start()

        @pl.when(i == 20 + 2 * (2 * mid - depth))
        def _():
            @pl.when(depth == mid)
            def _():
                small_sum(4, 3, 3)

            @pl.when(depth < mid)
            def _():
                settled(small.at[4], small_recv.at[4])

            @pl.when(depth > 0)
            def _():
                remote(small.at[4], small.at[4], small_send.at[3], small_recv.at[4], outward).start()

            remote(small.at[4], small_in.at[4], small_send.at[4], small_recv.at[5], peer).start()

    def small_finish():
        settled(small_in.at[4], small_recv.at[5])
        settled(small.at[0], small_send.at[0])
        settled(small.at[1], small_send.at[1])
        settled(small.at[3], small_send.at[2])
        settled(small.at[4], small_send.at[4])

        @pl.when(depth > 0)
        def _():
            settled(small.at[4], small_send.at[3])

    def step(i, carry):
        small_step(i)

        b1 = piece_at(i - LAG * (1 + depth))

        @when(True, b1)
        def _():
            settled(from_side(b1), side_recv.at[slot(b1)])

            @pl.when(depth == 0)
            def _():
                add(grown(b1, my_side, SIDE), grown(b1, my_side, SIDE), from_side(b1))

            @pl.when(depth > 0)
            def _():
                settled(from_inner(0, b1), inner_recv.at[0, slot(b1)])
                add(grown(b1, my_side, SIDE), grown(b1, my_side, SIDE), from_side(b1), from_inner(0, b1))

            into = (depth == mid).astype(jnp.int32)
            remote(grown(b1, my_side, SIDE), from_inner(into, b1), inner_send.at[slot(b1)], inner_recv.at[into, slot(b1)], inward).start()

        b2 = piece_at(i - LAG * (2 + mid + mid - depth))

        @when(True, b2)
        def _():
            @pl.when(depth == mid)
            def _():
                settled(from_inner(1, b2), inner_recv.at[1, slot(b2)])
                add(sums(b2, my_side, SIDE), grown(b2, my_side, SIDE), from_inner(1, b2))

            @pl.when(depth < mid)
            def _():
                settled(sums(b2, my_side, SIDE), inner_recv.at[1, slot(b2)])

            part = sums(b2, my_side, SIDE)

            @pl.when(depth > 0)
            def _():
                remote(part, part, line_send.at[slot(b2)], inner_recv.at[1, slot(b2)], outward).start()

            remote(part, part, back_send.at[slot(b2)], back_recv.at[slot(b2)], across).start()

        b3 = piece_at(i - LAG * (3 + mid + mid - depth))

        @when(True, b3)
        def _():
            settled(sums(b3, other_side, SIDE), back_recv.at[slot(b3)])

        for early in (True, False):
            for odd in (0, 1):
                root = (odd * (lines - 1)) if early else mid + odd
                height = max(root, lines - 1 - root)
                distance = jnp.abs(z - root)

                def matches(b, root=root, odd=odd):
                    return (root_of(b) == root) & (lax.rem(b + 2 * PIECES, 2) == odd)

                hop = jnp.where(z < root, z, jnp.where(z > root, lines - 1 - z, height))
                c1 = piece_at(i - LAG * hop)

                @when((z != root) & (hop > 0) & matches(c1), c1)
                def _(root=root, c1=c1):
                    part = grown(c1, 2 * SIDE, RAIL)

                    @pl.when(z < root)
                    def _():
                        settled(from_low(c1), low_recv.at[slot(c1)])
                        add(part, part, from_low(c1))
                        remote(part, from_low(c1), up_send.at[slot(c1)], low_recv.at[slot(c1)], above).start()

                    @pl.when(z > root)
                    def _():
                        settled(from_high(c1), high_recv.at[slot(c1)])
                        add(part, part, from_high(c1))
                        remote(part, from_high(c1), up_send.at[slot(c1)], high_recv.at[slot(c1)], below).start()

                @when((z == root) & matches(c1), c1)
                def _(root=root, c1=c1):
                    part = grown(c1, 2 * SIDE, RAIL)
                    others = []
                    if root > 0:
                        settled(from_low(c1), low_recv.at[slot(c1)])
                        others.append(from_low(c1))
                    if root < lines - 1:
                        settled(from_high(c1), high_recv.at[slot(c1)])
                        others.append(from_high(c1))
                    add(part, part, *others)
                    remote(part, from_root(c1), up_send.at[slot(c1)], root_recv.at[slot(c1)], across).start()

                c2 = piece_at(i - LAG * (height + 1 + distance))

                @when(matches(c2), c2)
                def _(root=root, c2=c2):
                    part = sums(c2, 2 * SIDE, RAIL)

                    @pl.when(z == root)
                    def _():
                        settled(from_root(c2), root_recv.at[slot(c2)])
                        add(part, grown(c2, 2 * SIDE, RAIL), from_root(c2))

                    @pl.when(z != root)
                    def _():
                        settled(part, root_recv.at[slot(c2)])

                    @pl.when(has_low & (z <= root))
                    def _():
                        remote(part, part, low_send.at[slot(c2)], root_recv.at[slot(c2)], below).start()

                    @pl.when(has_high & (z >= root))
                    def _():
                        remote(part, part, high_send.at[slot(c2)], root_recv.at[slot(c2)], above).start()

        b4 = piece_at(i - LAG * (2 * lines - 1))

        @when(True, b4)
        def _():
            store(b4).start()

        b0 = piece_at(i)

        @when(True, b0)
        def _():
            @pl.when(b0 >= RING)
            def _():
                release_sums(b0 - RING)

            load_own(b0).wait()
            load_other(b0).wait()
            add(grown(b0), grown(b0), landed(b0))
            remote(grown(b0, other_side, SIDE), from_side(b0), side_send.at[slot(b0)], side_recv.at[slot(b0)], across).start()
            part, root = grown(b0, 2 * SIDE, RAIL), root_of(b0)

            @pl.when((z == 0) & (root != 0))
            def _():
                remote(part, from_low(b0), up_send.at[slot(b0)], low_recv.at[slot(b0)], above).start()

            @pl.when((z == lines - 1) & (root != lines - 1))
            def _():
                remote(part, from_high(b0), up_send.at[slot(b0)], high_recv.at[slot(b0)], below).start()

        task(i)
        b5 = piece_at(i + AHEAD)

        @when(i > 0, b5)
        def _():
            load(b5)

        return carry

    def first_load(b, carry):
        load(b)
        return carry

    lax.fori_loop(0, AHEAD + 1, first_load, 0)
    pl.semaphore_wait(ready_sem, near)
    lax.fori_loop(0, PIECES + pause + LAG * (2 * lines - 1), step, 0)
    small_finish()

    def release_last(b, carry):
        release_grown(b)
        release_sums(b)
        return carry

    lax.fori_loop(PIECES - RING, PIECES, release_last, 0)

    remote(out.at[front], swapped, swap_send, swap_recv, peer).wait_recv()

    def writes(which):
        pairs = [
            [(out.at[front], first_out), (swapped, second_out), (back.at[front], input_out), (upstream.at[front], middle_out)],
            [(rows.at[rear], first_out), (out.at[rear], second_out), (swapped, input_out), (back.at[rear], middle_out)],
        ][which]
        return [pltpu.make_async_copy(a, b, out_sem.at[n]) for n, (a, b) in enumerate(pairs)]

    for which in range(2):
        @pl.when(plane == which)
        def _(which=which):
            for copy in writes(which):
                copy.start()

    for n, (source, target) in enumerate(((small.at[4], small_out), (small_in.at[4], other_out))):
        small_copy = pltpu.make_async_copy(source, target, out_sem.at[4 + n])
        small_copy.start()
        small_copy.wait()

    for which in range(2):
        @pl.when(plane == which)
        def _(which=which):
            for copy in writes(which):
                copy.wait()

    remote(out.at[front], swapped, swap_send, swap_recv, peer).wait_send()
    for b in range(TOKENS // BLOCK):
        @pl.when(plane == 0)
        def _(b=b):
            ahead(b).wait_send()

        @pl.when(plane == 1)
        def _(b=b):
            behind(b).wait_send()

    for n, (source, place, _, _) in enumerate(norm_copies):
        remote(source, place, norm_send.at[n], norm_recv.at[n], partner).wait_send()
    wait_weights_sent(0)
    wait_weights_sent(1)


def run_layer(lines, inputs, first, second, segments, joint, mixing, gated, down, gain, bias):
    sems = lambda *s: pltpu.SemaphoreType.DMA(s)
    half = TOKENS // 2
    copies = 2 + 3 * CHUNKS
    ring = sems(RING)
    any_spec, vmem = pl.BlockSpec(memory_space=pl.ANY), pl.BlockSpec(memory_space=pltpu.VMEM)
    rows_out = jax.ShapeDtypeStruct((half, D), BF)
    pieces = jax.ShapeDtypeStruct((PIECES, PIECE, WIDTH), BF)
    paired = jax.ShapeDtypeStruct((PIECES // 2 * PIECE, 2 * WIDTH), BF)
    block = jax.ShapeDtypeStruct((SMALL, D), F32)
    tokens, hiddens = pltpu.VMEM((TOKENS, D), BF), pltpu.VMEM((TOKENS, FF), BF)
    return pl.pallas_call(
        functools.partial(layer_kernel, lines),
        out_shape=[rows_out] * 4 + [paired] * 2 + [pieces] + [block] * 2,
        in_specs=[any_spec] * 3 + [vmem] + [any_spec] * 6,
        out_specs=[any_spec] * 9,
        scratch_shapes=[
            pltpu.VMEM((D, 3 * D), BF), pltpu.VMEM((D, D), BF), pltpu.VMEM((D, 2 * FF), BF), pltpu.VMEM((FF, D), BF),
            pltpu.VMEM((2, 2, 1, D), F32),
            tokens, tokens, tokens, pltpu.VMEM((half, D), BF), tokens, tokens,
            pltpu.VMEM((TOKENS, 3 * D), BF),
            pltpu.VMEM((TOKENS // BLOCK * PAIRS, 2 * BLOCK, BLOCK), F32),
            tokens, hiddens, hiddens, hiddens, pltpu.VMEM((TOKENS, 2 * FF), BF),
            tokens, tokens, pltpu.VMEM((TOKENS, D), F32), pltpu.VMEM((TOKENS, D), F32),
            pltpu.VMEM((TOKENS // BLOCK, BLOCK, BLOCK), F32), pltpu.VMEM((TOKENS, BLOCK), F32),
            pltpu.VMEM((ROWS, D), F32), pltpu.VMEM((5, SMALL, D), F32), pltpu.VMEM((5, SMALL, D), F32),
            pltpu.VMEM((ROWS, D), BF), pltpu.VMEM((2, D, D), BF), pltpu.VMEM((RING, RAIL, WIDTH), BF),
            sems(6), sems(copies), sems(copies), sems(copies), sems(2), sems(2), sems(2),
            sems(4), sems(4), sems(4), sems(4), pltpu.SemaphoreType.DMA, pltpu.SemaphoreType.DMA, sems(6),
            sems(2), sems(2), sems(TILES - 2), pltpu.SemaphoreType.REGULAR,
            sems(AHEAD + 1), sems(AHEAD + 1), ring, sems(5), sems(6), ring, ring, ring, sems(2, RING),
            ring, ring, ring, ring, ring, ring, ring, ring, ring,
        ],
        compiler_params=pltpu.CompilerParams(collective_id=2, has_side_effects=True, vmem_limit_bytes=62 * 2**20),
    )(inputs, first, second, segments, joint, mixing, gated, down, gain, bias)


def place_kernel(
    pieces_ref, small_ref, other_ref, first_ref, second_ref, input_ref, middle_ref,
    first_out, second_out, input_out, middle_out, joint_out, mixing_out, gated_out, down_out, gain_out, bias_out, stats_out,
    held, wide, passed, load_sem, store_sem, pass_sem,
):
    section = lax.axis_index("section")
    plane, core = lax.div(section, 2), lax.rem(section, 2)
    loads = [pltpu.make_async_copy(pieces_ref.at[p], held.at[p], load_sem.at[p]) for p in range(PIECES)]
    for load in loads:
        load.start()
    pairs = ((first_ref, first_out), (second_ref, second_out), (input_ref, input_out), (middle_ref, middle_out))
    takes = [pltpu.make_async_copy(a, passed.at[n], pass_sem.at[n]) for n, (a, _) in enumerate(pairs)]
    passes = [pltpu.make_async_copy(passed.at[n], b, pass_sem.at[4 + n]) for n, (_, b) in enumerate(pairs)]
    for copy in takes:
        copy.start()

    def place(piece):
        if piece < 8:
            return down_out.at[pl.ds(piece // 2 * PIECE, PIECE), pl.ds(piece % 2 * WIDTH, WIDTH)]
        if piece < 24:
            return gated_out.at[:, pl.ds((piece - 8) * WIDTH, WIDTH)]
        if piece < 30:
            return joint_out.at[:, pl.ds((piece - 24) * WIDTH, WIDTH)]
        return mixing_out.at[:, pl.ds((piece - 30) * WIDTH, WIDTH)]

    stores = [pltpu.make_async_copy(wide.at[p % SLOTS], place(p), store_sem.at[p % SLOTS]) for p in range(PIECES)]
    for p in range(PIECES):
        loads[p].wait()
        if p >= SLOTS:
            stores[p - SLOTS].wait()
        wide[p % SLOTS] = held[p].astype(F32)
        stores[p].start()

    for take, copy in zip(takes, passes):
        take.wait()
        copy.start()

    gain_out[...] = small_ref[pl.ds(2 * core, 1), :]
    bias_out[...] = small_ref[pl.ds(2 * core + 1, 1), :]
    count = small_ref[8:9, :1] * D
    row = lax.broadcasted_iota(jnp.int32, (2, 4), 0)
    lane = lax.broadcasted_iota(jnp.int32, (2, 4), 1)
    stats = jnp.zeros((2, 4), F32)
    for n in range(4):
        for at, source in ((2 * plane, small_ref), (2 - 2 * plane, other_ref)):
            value = jnp.sum(source[4 + n : 5 + n, :], axis=1, keepdims=True) / count
            stats = jnp.where((row == n // 2) & (lane == at + n % 2), jnp.sqrt(value), stats)
    stats_out[...] = stats
    for p in range(PIECES - SLOTS, PIECES):
        stores[p].wait()
    for copy in passes:
        copy.wait()


def place_results(pieces, small, other, *rows):
    any_spec, vmem = pl.BlockSpec(memory_space=pl.ANY), pl.BlockSpec(memory_space=pltpu.VMEM)
    shapes = ((HALF, 3 * D), (HALF, D), (HALF, 2 * FF), (FF // 2, D), (1, D), (1, D), (2, 4))
    return pl.pallas_call(
        place_kernel,
        out_shape=[jax.ShapeDtypeStruct(r.shape, BF) for r in rows] + [jax.ShapeDtypeStruct(s, F32) for s in shapes],
        in_specs=[any_spec, vmem, vmem] + [any_spec] * 4,
        out_specs=[any_spec] * 8 + [vmem] * 3,
        scratch_shapes=[
            pltpu.VMEM((PIECES, PIECE, WIDTH), BF), pltpu.VMEM((SLOTS, PIECE, WIDTH), F32),
            pltpu.VMEM((4,) + rows[0].shape, BF),
            pltpu.SemaphoreType.DMA((PIECES,)), pltpu.SemaphoreType.DMA((SLOTS,)), pltpu.SemaphoreType.DMA((8,)),
        ],
        compiler_params=pltpu.CompilerParams(vmem_limit_bytes=61 * 2**20),
    )(pieces, small, other, *rows)


def per_device(
    inputs, cotangent_first, cotangent_second, segment_ids,
    joint_projection, mixing_weight, gated_weight, down_weight, norm_gain, norm_bias,
):
    segments = segment_ids.reshape(-1, BLOCK)
    *rows, _, _, pieces, small, other = run_layer(
        lax.axis_size("dp") // 2, inputs, cotangent_first, cotangent_second, segments,
        joint_projection, mixing_weight, gated_weight, down_weight, norm_gain, norm_bias,
    )
    return tuple(place_results(pieces, small, other, *rows))


def solution(mesh):
    tokens, rows = P("dp", None), P("section", None)
    return jax.shard_map(
        per_device,
        mesh=mesh,
        in_specs=(tokens, tokens, tokens, P("dp"), rows, rows, rows, rows, rows, rows),
        out_specs=(P(("dp", "section"), None),) * 4 + (rows,) * 6 + (P(),),
        check_vma=False,
    )
```

```python
import functools

import jax
import jax.numpy as jnp
from jax import lax
from jax.experimental import pallas as pl
from jax.experimental.pallas import tpu as pltpu
from jax.sharding import PartitionSpec as P

D = 768
HEADS = 12
HEAD = D // HEADS
FF = 3072
BLOCK = 128
HALF = D // 2
PAIRS = HEADS // 2
TOKENS = 512
MICRO = 2
ROWS = TOKENS // MICRO
CHUNK = 1024
PART = 512
CHUNKS = FF // CHUNK
SMALL = 16
PIECES = 32
PIECE = 384
SIDE = 128
RAIL = 128
WIDTH = 384
AHEAD = 3
LAG = 2
RING = 16
BLOCKS = ROWS // BLOCK
TILES = 16
SLOTS = 8

EPSILON = 1e-05
FAR = 1e30
ROOT_HALF = 0.7071067811865476
ROOT_TWO_PI = 2.5066282746310002
SCALE = HEAD**-0.5

MESH = pl.DeviceIdType.MESH
BF = jnp.bfloat16
F32 = jnp.float32


def alibi_slopes():
    closest = 1 << HEADS.bit_length() - 1
    first_slope = 2.0 ** (-8.0 / closest)
    slopes = [first_slope ** (power_index + 1) for power_index in range(closest)]
    double_slope = 2.0 ** (-8.0 / (2 * closest))
    extra_slopes = [double_slope ** (power_index + 1) for power_index in range(2 * closest)]
    return slopes + extra_slopes[0::2][: HEADS - closest]


SLOPES = alibi_slopes()


def dot(a, b):
    return jnp.dot(a, b, preferred_element_type=F32)


def dot_right(a, b):
    return lax.dot_general(a, b, (((1,), (1,)), ((), ())), preferred_element_type=F32)


def dot_left(a, b):
    return lax.dot_general(a, b, (((0,), (0,)), ((), ())), preferred_element_type=F32)


def lane_mean(x):
    return jnp.sum(x, axis=-1, keepdims=True) * (1.0 / D)


def remote(src, dst, send, recv, device):
    return pltpu.make_async_remote_copy(
        src_ref=src, dst_ref=dst, send_sem=send, recv_sem=recv, device_id=device, device_id_type=MESH
    )


def settled(ref, sem):
    pltpu.make_async_copy(ref, ref, sem).wait()


def layer_kernel(
    lines,
    inputs_ref, first_ref, second_ref, segments_ref, joint_ref, mixing_ref, gated_ref, down_ref, gain_ref, bias_ref,
    first_out, second_out, input_out, middle_out, mine_out, landed_out, pieces_out, small_out, other_out,
    joint_w, mixing_w, gated_w, down_w, norms,
    rows, attended, out, swapped, upstream, back,
    joint_rows, probs, mixed, hidden, active, slope, both_grad,
    branch_first, branch_second, scaled_first, scaled_second, spread, columns,
    total, small, small_in, mixed_grad, staged, high,
    load_sem, local_sem, weight_send, weight_recv, norm_sem, norm_send, norm_recv,
    ahead_send, ahead_recv, behind_send, behind_recv, swap_send, swap_recv, out_sem,
    keep_sem, give_send, give_recv, ready_sem,
    own_sem, other_sem, store_sem, small_send, small_recv, side_send, side_recv, inner_send, inner_recv,
    up_send, low_recv, high_recv, root_recv, line_send, back_send, back_recv, low_send, high_send,
):
    dp, section = lax.axis_index("dp"), lax.axis_index("section")
    plane, core = lax.div(section, 2), lax.rem(section, 2)
    partner = (dp, section + 1 - 2 * core)
    peer = (dp, section + 2 - 4 * plane)

    y, z = lax.rem(dp, 2), lax.div(dp, 2)
    across, below, above = (dp + 1 - 2 * y, section), (dp - 2, section), (dp + 2, section)
    has_low, has_high = z > 0, z < lines - 1
    near = 1 + has_low.astype(jnp.int32) + has_high.astype(jnp.int32)

    def signal_near(semaphore):
        pl.semaphore_signal(semaphore, inc=1, device_id=across, device_id_type=MESH)

        @pl.when(has_low)
        def _():
            pl.semaphore_signal(semaphore, inc=1, device_id=below, device_id_type=MESH)

        @pl.when(has_high)
        def _():
            pl.semaphore_signal(semaphore, inc=1, device_id=above, device_id_type=MESH)

    barrier = pltpu.get_barrier_semaphore()
    pl.semaphore_signal(barrier, inc=1, device_id=partner, device_id_type=MESH)
    pl.semaphore_signal(barrier, inc=1, device_id=peer, device_id_type=MESH)
    signal_near(barrier)
    pl.semaphore_wait(barrier, 2 + near)

    mine = pl.ds(pl.multiple_of(core * HALF, HALF), HALF)
    theirs = pl.ds(pl.multiple_of((1 - core) * HALF, HALF), HALF)

    def micro_rows(m):
        return pl.ds(pl.multiple_of(m * ROWS, ROWS), ROWS)

    def token_loads():
        copies = []
        for m in range(2):
            there = pl.ds(pl.multiple_of((2 * m + core) * (TOKENS // 2), TOKENS // 2), TOKENS // 2)
            here = pl.ds(m * (TOKENS // 2), TOKENS // 2)
            copies.append(pltpu.make_async_copy(first_ref.at[there], back.at[here], load_sem.at[2 * m]))
            copies.append(pltpu.make_async_copy(second_ref.at[there], upstream.at[here], load_sem.at[2 * m + 1]))
        return copies

    def input_loads():
        copies = []
        for m in range(2):
            there = pl.ds(pl.multiple_of((2 * m + core) * (TOKENS // 2), TOKENS // 2), TOKENS // 2)
            here = pl.ds(m * (TOKENS // 2), TOKENS // 2)
            copies.append(pltpu.make_async_copy(inputs_ref.at[there], rows.at[here], load_sem.at[4 + m]))
        return copies

    def chunk(k):
        return pl.ds(pl.multiple_of(k * CHUNK, CHUNK), CHUNK)

    def upper(k):
        return pl.ds(pl.multiple_of(FF + k * CHUNK, CHUNK), CHUNK)

    def weight_copies(which):
        if which == 0:
            return [(joint_ref, joint_w.at[mine], joint_w.at[theirs], 0), (mixing_ref, mixing_w.at[mine], mixing_w.at[theirs], 1)]
        copies = []
        for k in range(CHUNKS):
            for n, columns_at in enumerate((chunk(k), upper(k))):
                copies.append((gated_ref.at[:, columns_at], gated_w.at[mine, columns_at], gated_w.at[theirs, columns_at], 2 + 2 * k + n))
            here = pl.ds(pl.multiple_of(core * (FF // 2) + k * PART, PART), PART)
            there = pl.ds(pl.multiple_of((1 - core) * (FF // 2) + k * PART, PART), PART)
            copies.append((down_ref.at[pl.ds(k * PART, PART)], down_w.at[here], down_w.at[there], 2 + 2 * CHUNKS + k))
        return copies

    def start_weights(which):
        for source, place, _, n in weight_copies(which):
            remote(source, place, weight_send.at[n], weight_recv.at[n], partner).start()
            pltpu.make_async_copy(source, place, local_sem.at[n]).start()

    def wait_weights(which):
        for source, place, other, n in weight_copies(which):
            pltpu.make_async_copy(source, place, local_sem.at[n]).wait()
            settled(other, weight_recv.at[n])

    def wait_chunk(k):
        for source, place, other, n in weight_copies(1)[3 * k : 3 * k + 2]:
            pltpu.make_async_copy(source, place, local_sem.at[n]).wait()
            settled(other, weight_recv.at[n])
        for part in (2 * k, 2 * k + 1):
            source, _, _, n = weight_copies(1)[3 * (part % CHUNKS) + 2]
            place = down_w.at[pl.ds(part * PART, PART)]

            @pl.when(core == part // CHUNKS)
            def _():
                pltpu.make_async_copy(source, place, local_sem.at[n]).wait()

            @pl.when(core != part // CHUNKS)
            def _():
                settled(place, weight_recv.at[n])

    def wait_weights_sent(which):
        for source, place, _, n in weight_copies(which):
            remote(source, place, weight_send.at[n], weight_recv.at[n], partner).wait_send()

    norm_copies = []
    for n, source in enumerate((gain_ref, bias_ref)):
        norm_copies.append((source, norms.at[n, core], norms.at[n, 1 - core], n))
    for source, place, _, n in norm_copies:
        remote(source, place, norm_send.at[n], norm_recv.at[n], partner).start()
        pltpu.make_async_copy(source, place, norm_sem.at[n]).start()
    start_weights(0)

    @pl.when(plane == 0)
    def _():
        for copy in input_loads():
            copy.start()

    @pl.when(plane == 1)
    def _():
        for copy in token_loads():
            copy.start()

    start_weights(1)

    first = lax.broadcasted_iota(jnp.int32, (BLOCK, BLOCK), 0)
    second = lax.broadcasted_iota(jnp.int32, (BLOCK, BLOCK), 1)
    distance = jnp.abs(first - second).astype(F32)
    half_blocks = TOKENS // (2 * BLOCK)
    for b in range(TOKENS // BLOCK):
        at = (2 * (b // half_blocks) + core) * half_blocks + b % half_blocks
        along = jnp.broadcast_to(segments_ref[pl.ds(at, 1), :].astype(F32), (BLOCK, BLOCK))
        down = along.T
        spread[b] = jnp.where(along == down, distance, FAR)
        columns[pl.ds(b * BLOCK, BLOCK), :] = jnp.where(down >= 0.0, 1.0, 0.0)
    small[0] = jnp.zeros_like(small[0])
    small[0, 8:9, :BLOCK] = jnp.sum(columns[...], axis=0, keepdims=True)

    lane = lax.broadcasted_iota(jnp.int32, (1, BLOCK), 1)
    low_lanes = jnp.where(lane < HEAD, 1.0, 0.0).astype(BF)
    high_lanes = jnp.where(lane < HEAD, 0.0, 1.0).astype(BF)

    def stacked(x):
        return jnp.concatenate([x * low_lanes, x * high_lanes], axis=0)

    def beside(x):
        return jnp.concatenate([x[:BLOCK], x[BLOCK:]], axis=1)

    for source, place, other, n in norm_copies:
        pltpu.make_async_copy(source, place, norm_sem.at[n]).wait()
        settled(other, norm_recv.at[n])

    def add_small(row, value):
        small[0, row : row + 1, :] += value

    def keep_column(r, at, value):
        columns[r] = jnp.where(lane == at, value, columns[r])

    def column(value):
        return jnp.sum(value, axis=0, keepdims=True)

    def post_norm(r, source, branch, kind, scaled_ref, result_ref):
        before = source[r].astype(F32)
        ok = columns[r, :1]
        add_small(4 + kind, column(ok * (before * before)))
        add_small(6 + kind, column(ok * (branch * branch)))
        summed = before + branch
        center = summed - lane_mean(summed)
        inverse = lax.rsqrt(lane_mean(center * center) + EPSILON)
        scaled = center * inverse
        scaled_ref[r] = scaled
        keep_column(r, 1 + kind, inverse)
        result_ref[r] = (scaled * norms[0, kind] + norms[1, kind]).astype(BF)

    def norm_back(r, grad, kind, scaled_ref):
        scaled = scaled_ref[r]
        add_small(2 * kind, column(grad * scaled))
        add_small(2 * kind + 1, column(grad))
        inner = grad * norms[0, kind]
        return columns[r, 1 + kind : 2 + kind] * (inner - lane_mean(inner) - scaled * lane_mean(inner * scaled))

    def in_step(units):
        units = list(units)
        while units:
            units = [u for u in units if next(u, units) is not units]

    def block_rows(b):
        return pl.ds(pl.multiple_of(b * BLOCK, BLOCK), BLOCK)

    def ahead(b):
        r = block_rows(b)
        return remote(out.at[r], rows.at[r], ahead_send.at[b], ahead_recv.at[b], peer)

    def behind(b):
        r = block_rows(b)
        return remote(back.at[r], upstream.at[r], behind_send.at[b], behind_recv.at[b], peer)

    front, rear = pl.ds(0, TOKENS // 2), pl.ds(TOKENS // 2, TOKENS // 2)

    def attend(m):
        r = micro_rows(m)
        for j in range(BLOCKS):
            b = m * BLOCKS + j

            @pl.when(plane == 1)
            def _(b=b):
                ahead(b).wait_recv()

            at = block_rows(b)
            joint_rows[at] = dot(rows[at], joint_w[...]).astype(BF)
            far = spread[b]

            def pair(p, b=b, at=at, far=far):
                queries, keys, values = [joint_rows[at, pl.ds(n * D + p * BLOCK, BLOCK)] for n in range(3)]
                raw = dot_right(stacked(queries), keys)
                yield
                parts = []
                for e in range(2):
                    scores = raw[e * BLOCK : (e + 1) * BLOCK] * SCALE - SLOPES[2 * p + e] * far
                    weights = jnp.exp(scores - jnp.max(scores, axis=-1, keepdims=True))
                    parts.append(weights * (1.0 / jnp.sum(weights, axis=-1, keepdims=True)))
                soft = jnp.concatenate(parts, axis=0)
                probs[b * PAIRS + p] = soft
                yield
                mixed[at, pl.ds(p * BLOCK, BLOCK)] = dot(beside(soft.astype(BF)), stacked(values)).astype(BF)

            in_step([pair(p) for p in range(PAIRS)])
        branch = dot(mixed[r], mixing_w[...])
        post_norm(r, rows, branch, 0, scaled_first, attended)

    def feed(m, arriving):
        r = micro_rows(m)
        branch = 0.0
        for k in range(CHUNKS):
            if arriving:
                wait_chunk(k)
            gate = dot(attended[r], gated_w[:, chunk(k)])
            up = dot(attended[r], gated_w[:, upper(k)])
            normal = 0.5 + 0.5 * lax.erf(gate * ROOT_HALF)
            density = jnp.exp(-0.5 * gate * gate) * (1.0 / ROOT_TWO_PI)
            gelu = gate * normal
            low = (gelu * up).astype(BF)
            hidden[r, chunk(k)] = low
            active[r, chunk(k)] = gelu.astype(BF)
            slope[r, chunk(k)] = (up * (normal + gate * density)).astype(BF)
            if arriving:
                total[...] = dot(low, down_w[chunk(k)]) + (total[...] if k else 0.0)
            else:
                branch += dot(low, down_w[chunk(k)])
        if not arriving:
            total[...] = branch
        post_norm(r, attended, total[...], 1, scaled_second, out)

    def feed_norm_back(m, grad):
        r = micro_rows(m)
        through = norm_back(r, grad, 1, scaled_second)
        branch_second[r] = through.astype(BF)
        total[...] = through

    def feed_back(m):
        r = micro_rows(m)
        through = total[...]
        for k in range(CHUNKS):
            hidden_grad = dot_right(branch_second[r], down_w[chunk(k)])
            gate_grad = (hidden_grad * slope[r, chunk(k)].astype(F32)).astype(BF)
            up_grad = (hidden_grad * active[r, chunk(k)].astype(F32)).astype(BF)
            both_grad[r, chunk(k)] = gate_grad
            both_grad[r, upper(k)] = up_grad
            through += dot_right(gate_grad, gated_w[:, chunk(k)]) + dot_right(up_grad, gated_w[:, upper(k)])
        total[...] = through

    def attend_back(m, grad):
        r = micro_rows(m)
        through = norm_back(r, grad, 0, scaled_first)
        branch_first[r] = through.astype(BF)
        total[...] = through
        mixed_grad[...] = dot_right(branch_first[r], mixing_w[...]).astype(BF)
        for j in range(BLOCKS):
            b = m * BLOCKS + j
            at = block_rows(b)

            def pair(p, b=b, j=j, at=at):
                lanes = [pl.ds(n * D + p * BLOCK, BLOCK) for n in range(3)]
                queries, keys, values = [joint_rows[at, n] for n in lanes]
                above = stacked(mixed_grad[j * BLOCK : (j + 1) * BLOCK, p * BLOCK : (p + 1) * BLOCK])
                soft = probs[b * PAIRS + p]
                probs_grad = dot_right(above, values)
                yield
                values_grad = dot_left(soft.astype(BF), above)
                score_grad = soft * (probs_grad - jnp.sum(probs_grad * soft, axis=-1, keepdims=True))
                score_grad = score_grad.astype(BF)
                yield
                queries_grad = SCALE * dot(beside(score_grad), stacked(keys))
                keys_grad = SCALE * dot_left(score_grad, stacked(queries))
                yield
                for n, grad_part in zip(lanes, (queries_grad, keys_grad, values_grad)):
                    joint_rows[at, n] = grad_part.astype(BF)

            in_step([pair(p) for p in range(PAIRS)])
            grad_rows = total[j * BLOCK : (j + 1) * BLOCK, :] + dot_right(joint_rows[at], joint_w[...])

            @pl.when(plane == 0)
            def _(at=at, grad_rows=grad_rows):
                back[at] = grad_rows.astype(BF)

            @pl.when(plane == 1)
            def _(b=b, at=at, grad_rows=grad_rows):
                back[at] = (grad_rows + columns[at, :1] * back[at].astype(F32)).astype(BF)
                behind(b).start()


    wait_weights(0)

    @pl.when(plane == 0)
    def _():
        for copy in input_loads():
            copy.wait()

    def forward_step(step, carry):
        feeding = jnp.where(plane == 0, lax.div(step, MICRO), lax.rem(step, 2))
        m = jnp.where(plane == 0, lax.rem(step, MICRO), lax.div(step, 2))

        @pl.when(feeding == 0)
        def _():
            attend(m)

        @pl.when(feeding == 1)
        def _():
            @pl.when(m == 0)
            def _():
                feed(0, True)

            @pl.when(m > 0)
            def _():
                feed(m, False)

            @pl.when(plane == 0)
            def _():
                for j in range(BLOCKS):
                    ahead(m * BLOCKS + j).start()

        return carry

    lax.fori_loop(0, 2 * MICRO, forward_step, 0)

    @pl.when(plane == 1)
    def _():
        remote(out.at[front], swapped, swap_send, swap_recv, peer).start()

    def pairs(n, height):
        tile = tile_of(n)
        row = jnp.where(tile < 4, lax.rem(tile, 2) * D, tile * PIECE)
        return pl.ds(pl.multiple_of(row, PIECE), height)

    def half_tile(n, which):
        return staged.at[lax.rem(n, 2), pl.ds(pl.multiple_of(which * PIECE, PIECE), PIECE)]

    def keep(n, source, height):
        return pltpu.make_async_copy(source, mine_out.at[pairs(n, height)], keep_sem.at[lax.rem(n, 2)])

    def give(n, source, height):
        unit = jnp.where(n < 4, lax.rem(tile_of(n), 2), n - 2)
        return remote(source, landed_out.at[pairs(n, height)], give_send.at[lax.rem(n, 2)], give_recv.at[unit], partner)

    def wide(k):
        return pl.ds(pl.multiple_of(k * D, D), D)

    def tile_of(n):
        return n + (n == 1).astype(jnp.int32) - (n == 2).astype(jnp.int32)

    def each_part(n, kept, given):
        tile = tile_of(n)

        @pl.when((tile < 4) & (lax.div(tile, 2) == core))
        def _():
            kept(keep(n, staged.at[lax.rem(n, 2)], D))

        @pl.when((tile < 4) & (lax.div(tile, 2) != core))
        def _():
            given(give(n, staged.at[lax.rem(n, 2)], D))

        @pl.when(tile >= 4)
        def _():
            kept(keep(n, half_tile(n, core), PIECE))
            given(give(n, half_tile(n, 1 - core), PIECE))

    def finish(n):
        each_part(n, lambda copy: copy.wait(), lambda copy: copy.wait_send())

    def launch(n, value):
        staged[lax.rem(n, 2)] = value.astype(BF)
        each_part(n, lambda copy: copy.start(), lambda copy: copy.start())

    def down_tile(n):
        launch(n, dot_left(hidden[:, wide(tile_of(n))], branch_second[...]))

    def first_tiles():
        down_tile(jnp.int32(0))
        down_tile(jnp.int32(1))

    @pl.when(plane == 1)
    def _():
        for copy in token_loads():
            copy.wait()

    def backward_step(m, carry):
        r = micro_rows(m)

        @pl.when(plane == 0)
        def _():
            for j in range(BLOCKS):
                behind(m * BLOCKS + j).wait_recv()

        @pl.when(plane == 1)
        def _():
            upstream[r] = (columns[r, :1] * upstream[r].astype(F32)).astype(BF)

        feed_norm_back(m, upstream[r].astype(F32))

        @pl.when((plane == 0) & (m == MICRO - 1))
        def _():
            first_tiles()

        feed_back(m)

        @pl.when((plane == 1) | (m < MICRO - 1))
        def _():
            attend_back(m, total[...].astype(BF).astype(F32))

        return carry

    lax.fori_loop(0, MICRO, backward_step, 0)

    def last_attend_back():
        attend_back(MICRO - 1, total[...].astype(BF).astype(F32))
        remote(back.at[rear], swapped, swap_send, swap_recv, peer).start()

    def task(i):
        n = i + 3

        @pl.when(i == 0)
        def _():
            down_tile(n)
            finish(n - 1)

        @pl.when((i > 0) & (i < 9))
        def _():
            launch(n, dot_left(attended[...], both_grad[:, wide(n - 4)]))
            finish(n - 1)

        @pl.when((i == 9) & (plane == 0))
        def _():
            last_attend_back()

        @pl.when((i >= 10) & (i < 13))
        def _():
            launch(n - 1, dot_left(rows[...], joint_rows[:, wide(n - 13)]))
            finish(n - 2)

        @pl.when(i == 13)
        def _():
            launch(n - 1, dot_left(mixed[...], branch_first[...]))
            finish(n - 2)

        @pl.when(i == 14)
        def _():
            finish(n - 2)

    signal_near(ready_sem)
    @pl.when(plane == 1)
    def _():
        first_tiles()

    finish(jnp.int32(0))
    down_tile(jnp.int32(2))
    finish(jnp.int32(1))
    half = lines // 2
    mid = half - 1
    lower = z < half
    depth = jnp.where(lower, z, lines - 1 - z)
    inward = (jnp.where(lower, dp + 2, dp - 2), section)
    outward = (jnp.where(lower, dp - 2, dp + 2), section)
    my_side, other_side = y * SIDE, (1 - y) * SIDE
    pause = max(0, LAG * (2 * lines - 1) - (RING - 2))

    def window(ref, row, column, height):
        return ref.at[pl.ds(pl.multiple_of(row, 16), height), pl.ds(pl.multiple_of(column * WIDTH, WIDTH), WIDTH)]

    def slot(b):
        return lax.rem(b, RING)

    def grown(b, row=0, height=PIECE):
        return window(gated_w, row, slot(b), height)

    def sums(b, row=0, height=PIECE):
        return window(gated_w, PIECE + row, slot(b), height)

    def landed(b):
        return window(down_w, lax.rem(b, 8) * PIECE, 0, PIECE)

    def from_side(b):
        return window(down_w, lax.div(slot(b), 2) * PIECE + lax.rem(b, 2) * SIDE, 1, SIDE)

    def from_inner(n, b):
        return window(active, (2 * n + lax.div(slot(b), 8)) * SIDE, lax.rem(b, 8), SIDE)

    def from_low(b):
        return window(slope, lax.div(slot(b), 8) * RAIL, lax.rem(b, 8), RAIL)

    def from_high(b):
        return high.at[slot(b)]

    def from_root(b):
        return window(slope, 2 * RAIL, lax.rem(lax.div(b, 2), 8), RAIL)

    def from_pair(ref, b):
        row = pl.multiple_of(lax.div(b, 2) * PIECE, PIECE)
        return ref.at[pl.ds(row, PIECE), pl.ds(pl.multiple_of(lax.rem(b, 2) * WIDTH, WIDTH), WIDTH)]

    def load_own(b):
        return pltpu.make_async_copy(from_pair(mine_out, b), grown(b), own_sem.at[lax.rem(b, AHEAD + 1)])

    def load_other(b):
        return pltpu.make_async_copy(from_pair(landed_out, b), landed(b), other_sem.at[lax.rem(b, AHEAD + 1)])

    def store(b):
        return pltpu.make_async_copy(sums(b), pieces_out.at[b], store_sem.at[slot(b)])

    def root_of(b):
        odd = lax.rem(b, 2)
        return jnp.where(b < PIECES // 2, odd * (lines - 1), mid + odd)

    def release_grown(b):
        root = root_of(b)
        settled(grown(b, other_side, SIDE), side_send.at[slot(b)])
        settled(grown(b, my_side, SIDE), inner_send.at[slot(b)])

        @pl.when(z != root)
        def _():
            settled(grown(b, 2 * SIDE, RAIL), up_send.at[slot(b)])

        @pl.when(z == root)
        def _():
            settled(grown(b, 2 * SIDE, RAIL), up_send.at[slot(b)])

    def release_sums(b):
        root = root_of(b)
        store(b).wait()
        settled(sums(b, my_side, SIDE), back_send.at[slot(b)])

        @pl.when(depth > 0)
        def _():
            settled(sums(b, my_side, SIDE), line_send.at[slot(b)])

        @pl.when(has_low & (z <= root))
        def _():
            settled(sums(b, 2 * SIDE, RAIL), low_send.at[slot(b)])

        @pl.when(has_high & (z >= root))
        def _():
            settled(sums(b, 2 * SIDE, RAIL), high_send.at[slot(b)])

    def load(b):
        @pl.when((b < 8) & (lax.rem(b, 4) == 0))
        def _():
            settled(landed_out.at[pl.ds(0, D)], give_recv.at[lax.div(b, 4)])

        @pl.when((b >= 8) & (lax.rem(b, 2) == 0))
        def _():
            settled(landed_out.at[pl.ds(0, PIECE)], give_recv.at[lax.div(b, 2) - 2])

        load_own(b).start()
        load_other(b).start()

    def add(into, first, *others):
        value = first[...].astype(F32)
        for other in others:
            value = value + other[...].astype(F32)
        into[...] = value.astype(BF)

    def piece_at(j):
        if pause == 0:
            return j
        return jnp.where(j < RING, j, jnp.where(j < RING + pause, -1, j - pause))

    def when(active_now, b):
        return pl.when(active_now & (b >= 0) & (b < PIECES))

    def small_sum(n, source, arrival):
        settled(small_in.at[arrival], small_recv.at[arrival])
        small[n] = small[source] + small_in[arrival]

    def small_step(i):
        @pl.when(i == 14)
        def _():
            remote(small.at[0], small_in.at[0], small_send.at[0], small_recv.at[0], partner).start()

        @pl.when(i == 16)
        def _():
            small_sum(1, 0, 0)
            remote(small.at[1], small_in.at[1], small_send.at[1], small_recv.at[1], across).start()

        @pl.when(i == 18 + 2 * depth)
        def _():
            small_sum(2, 1, 1)

            @pl.when(depth > 0)
            def _():
                small_sum(3, 2, 2)

            @pl.when(depth == 0)
            def _():
                small[3] = small[2]

            into = jnp.where(depth == mid, 3, 2)
            remote(small.at[3], small_in.at[into], small_send.at[2], small_recv.at[into], inward).start()

        @pl.when(i == 20 + 2 * (2 * mid - depth))
        def _():
            @pl.when(depth == mid)
            def _():
                small_sum(4, 3, 3)

            @pl.when(depth < mid)
            def _():
                settled(small.at[4], small_recv.at[4])

            @pl.when(depth > 0)
            def _():
                remote(small.at[4], small.at[4], small_send.at[3], small_recv.at[4], outward).start()

            remote(small.at[4], small_in.at[4], small_send.at[4], small_recv.at[5], peer).start()

    def writes(which):
        pairs = [
            [(out.at[front], first_out), (swapped, second_out), (back.at[front], input_out), (upstream.at[front], middle_out)],
            [(rows.at[rear], first_out), (out.at[rear], second_out), (swapped, input_out), (back.at[rear], middle_out)],
        ][which]
        return [pltpu.make_async_copy(a, b, out_sem.at[n]) for n, (a, b) in enumerate(pairs)]

    def small_writes():
        pairs = ((small.at[4], small_out), (small_in.at[4], other_out))
        return [pltpu.make_async_copy(a, b, out_sem.at[4 + n]) for n, (a, b) in enumerate(pairs)]

    def output_step(i):
        @pl.when(i == 20)
        def _():
            remote(out.at[front], swapped, swap_send, swap_recv, peer).wait_recv()
            for which in range(2):
                @pl.when(plane == which)
                def _(which=which):
                    for copy in writes(which):
                        copy.start()

        @pl.when(i == 24 + 4 * mid)
        def _():
            small_finish()
            for copy in small_writes():
                copy.start()

    def small_finish():
        settled(small_in.at[4], small_recv.at[5])
        settled(small.at[0], small_send.at[0])
        settled(small.at[1], small_send.at[1])
        settled(small.at[3], small_send.at[2])
        settled(small.at[4], small_send.at[4])

        @pl.when(depth > 0)
        def _():
            settled(small.at[4], small_send.at[3])

    def step(i, carry):
        small_step(i)
        output_step(i)

        b1 = piece_at(i - LAG * (1 + depth))

        @when(True, b1)
        def _():
            settled(from_side(b1), side_recv.at[slot(b1)])

            @pl.when(depth == 0)
            def _():
                add(grown(b1, my_side, SIDE), grown(b1, my_side, SIDE), from_side(b1))

            @pl.when(depth > 0)
            def _():
                settled(from_inner(0, b1), inner_recv.at[0, slot(b1)])
                add(grown(b1, my_side, SIDE), grown(b1, my_side, SIDE), from_side(b1), from_inner(0, b1))

            into = (depth == mid).astype(jnp.int32)
            remote(grown(b1, my_side, SIDE), from_inner(into, b1), inner_send.at[slot(b1)], inner_recv.at[into, slot(b1)], inward).start()

        b2 = piece_at(i - LAG * (2 + mid + mid - depth))

        @when(True, b2)
        def _():
            @pl.when(depth == mid)
            def _():
                settled(from_inner(1, b2), inner_recv.at[1, slot(b2)])
                add(sums(b2, my_side, SIDE), grown(b2, my_side, SIDE), from_inner(1, b2))

            @pl.when(depth < mid)
            def _():
                settled(sums(b2, my_side, SIDE), inner_recv.at[1, slot(b2)])

            part = sums(b2, my_side, SIDE)

            @pl.when(depth > 0)
            def _():
                remote(part, part, line_send.at[slot(b2)], inner_recv.at[1, slot(b2)], outward).start()

            remote(part, part, back_send.at[slot(b2)], back_recv.at[slot(b2)], across).start()

        b3 = piece_at(i - LAG * (3 + mid + mid - depth))

        @when(True, b3)
        def _():
            settled(sums(b3, other_side, SIDE), back_recv.at[slot(b3)])

        for early in (True, False):
            for odd in (0, 1):
                root = (odd * (lines - 1)) if early else mid + odd
                height = max(root, lines - 1 - root)
                distance = jnp.abs(z - root)

                def matches(b, root=root, odd=odd):
                    return (root_of(b) == root) & (lax.rem(b + 2 * PIECES, 2) == odd)

                hop = jnp.where(z < root, z, jnp.where(z > root, lines - 1 - z, height))
                c1 = piece_at(i - LAG * hop)

                @when((z != root) & (hop > 0) & matches(c1), c1)
                def _(root=root, c1=c1):
                    part = grown(c1, 2 * SIDE, RAIL)

                    @pl.when(z < root)
                    def _():
                        settled(from_low(c1), low_recv.at[slot(c1)])
                        add(part, part, from_low(c1))
                        remote(part, from_low(c1), up_send.at[slot(c1)], low_recv.at[slot(c1)], above).start()

                    @pl.when(z > root)
                    def _():
                        settled(from_high(c1), high_recv.at[slot(c1)])
                        add(part, part, from_high(c1))
                        remote(part, from_high(c1), up_send.at[slot(c1)], high_recv.at[slot(c1)], below).start()

                @when((z == root) & matches(c1), c1)
                def _(root=root, c1=c1):
                    part = grown(c1, 2 * SIDE, RAIL)
                    others = []
                    if root > 0:
                        settled(from_low(c1), low_recv.at[slot(c1)])
                        others.append(from_low(c1))
                    if root < lines - 1:
                        settled(from_high(c1), high_recv.at[slot(c1)])
                        others.append(from_high(c1))
                    add(part, part, *others)
                    remote(part, from_root(c1), up_send.at[slot(c1)], root_recv.at[slot(c1)], across).start()

                c2 = piece_at(i - LAG * (height + 1 + distance))

                @when(matches(c2), c2)
                def _(root=root, c2=c2):
                    part = sums(c2, 2 * SIDE, RAIL)

                    @pl.when(z == root)
                    def _():
                        settled(from_root(c2), root_recv.at[slot(c2)])
                        add(part, grown(c2, 2 * SIDE, RAIL), from_root(c2))

                    @pl.when(z != root)
                    def _():
                        settled(part, root_recv.at[slot(c2)])

                    @pl.when(has_low & (z <= root))
                    def _():
                        remote(part, part, low_send.at[slot(c2)], root_recv.at[slot(c2)], below).start()

                    @pl.when(has_high & (z >= root))
                    def _():
                        remote(part, part, high_send.at[slot(c2)], root_recv.at[slot(c2)], above).start()

        b6 = piece_at(i - LAG * (2 * lines - 2))

        @when(True, b6)
        def _():
            release_grown(b6)

        b4 = piece_at(i - LAG * (2 * lines - 1))

        @when(True, b4)
        def _():
            store(b4).start()

        b0 = piece_at(i)

        @when(True, b0)
        def _():
            @pl.when(b0 >= RING)
            def _():
                release_sums(b0 - RING)

            load_own(b0).wait()
            load_other(b0).wait()
            add(grown(b0), grown(b0), landed(b0))
            remote(grown(b0, other_side, SIDE), from_side(b0), side_send.at[slot(b0)], side_recv.at[slot(b0)], across).start()
            part, root = grown(b0, 2 * SIDE, RAIL), root_of(b0)

            @pl.when((z == 0) & (root != 0))
            def _():
                remote(part, from_low(b0), up_send.at[slot(b0)], low_recv.at[slot(b0)], above).start()

            @pl.when((z == lines - 1) & (root != lines - 1))
            def _():
                remote(part, from_high(b0), up_send.at[slot(b0)], high_recv.at[slot(b0)], below).start()

        task(i)
        b5 = piece_at(i + AHEAD)

        @when(i > 0, b5)
        def _():
            load(b5)

        return carry

    def first_load(b, carry):
        load(b)
        return carry

    lax.fori_loop(0, AHEAD + 1, first_load, 0)
    pl.semaphore_wait(ready_sem, near)
    lax.fori_loop(0, PIECES + pause + LAG * (2 * lines - 1), step, 0)
    def release_last(b, carry):
        release_sums(b)
        return carry

    lax.fori_loop(PIECES - RING, PIECES, release_last, 0)

    for copy in small_writes():
        copy.wait()

    for which in range(2):
        @pl.when(plane == which)
        def _(which=which):
            for copy in writes(which):
                copy.wait()

    remote(out.at[front], swapped, swap_send, swap_recv, peer).wait_send()
    for b in range(TOKENS // BLOCK):
        @pl.when(plane == 0)
        def _(b=b):
            ahead(b).wait_send()

        @pl.when(plane == 1)
        def _(b=b):
            behind(b).wait_send()

    for n, (source, place, _, _) in enumerate(norm_copies):
        remote(source, place, norm_send.at[n], norm_recv.at[n], partner).wait_send()
    wait_weights_sent(0)
    wait_weights_sent(1)


def run_layer(lines, inputs, first, second, segments, joint, mixing, gated, down, gain, bias):
    sems = lambda *s: pltpu.SemaphoreType.DMA(s)
    half = TOKENS // 2
    copies = 2 + 3 * CHUNKS
    ring = sems(RING)
    any_spec, vmem = pl.BlockSpec(memory_space=pl.ANY), pl.BlockSpec(memory_space=pltpu.VMEM)
    rows_out = jax.ShapeDtypeStruct((half, D), BF)
    pieces = jax.ShapeDtypeStruct((PIECES, PIECE, WIDTH), BF)
    paired = jax.ShapeDtypeStruct((PIECES // 2 * PIECE, 2 * WIDTH), BF)
    block = jax.ShapeDtypeStruct((SMALL, D), F32)
    tokens, hiddens = pltpu.VMEM((TOKENS, D), BF), pltpu.VMEM((TOKENS, FF), BF)
    return pl.pallas_call(
        functools.partial(layer_kernel, lines),
        out_shape=[rows_out] * 4 + [paired] * 2 + [pieces] + [block] * 2,
        in_specs=[any_spec] * 3 + [vmem] + [any_spec] * 6,
        out_specs=[any_spec] * 9,
        scratch_shapes=[
            pltpu.VMEM((D, 3 * D), BF), pltpu.VMEM((D, D), BF), pltpu.VMEM((D, 2 * FF), BF), pltpu.VMEM((FF, D), BF),
            pltpu.VMEM((2, 2, 1, D), F32),
            tokens, tokens, tokens, pltpu.VMEM((half, D), BF), tokens, tokens,
            pltpu.VMEM((TOKENS, 3 * D), BF),
            pltpu.VMEM((TOKENS // BLOCK * PAIRS, 2 * BLOCK, BLOCK), F32),
            tokens, hiddens, hiddens, hiddens, pltpu.VMEM((TOKENS, 2 * FF), BF),
            tokens, tokens, pltpu.VMEM((TOKENS, D), F32), pltpu.VMEM((TOKENS, D), F32),
            pltpu.VMEM((TOKENS // BLOCK, BLOCK, BLOCK), F32), pltpu.VMEM((TOKENS, BLOCK), F32),
            pltpu.VMEM((ROWS, D), F32), pltpu.VMEM((5, SMALL, D), F32), pltpu.VMEM((5, SMALL, D), F32),
            pltpu.VMEM((ROWS, D), BF), pltpu.VMEM((2, D, D), BF), pltpu.VMEM((RING, RAIL, WIDTH), BF),
            sems(6), sems(copies), sems(copies), sems(copies), sems(2), sems(2), sems(2),
            sems(4), sems(4), sems(4), sems(4), pltpu.SemaphoreType.DMA, pltpu.SemaphoreType.DMA, sems(6),
            sems(2), sems(2), sems(TILES - 2), pltpu.SemaphoreType.REGULAR,
            sems(AHEAD + 1), sems(AHEAD + 1), ring, sems(5), sems(6), ring, ring, ring, sems(2, RING),
            ring, ring, ring, ring, ring, ring, ring, ring, ring,
        ],
        compiler_params=pltpu.CompilerParams(collective_id=2, has_side_effects=True, vmem_limit_bytes=62 * 2**20),
    )(inputs, first, second, segments, joint, mixing, gated, down, gain, bias)


def place_kernel(
    pieces_ref, small_ref, other_ref, first_ref, second_ref, input_ref, middle_ref,
    first_out, second_out, input_out, middle_out, joint_out, mixing_out, gated_out, down_out, gain_out, bias_out, stats_out,
    held, wide, passed, load_sem, store_sem, pass_sem,
):
    section = lax.axis_index("section")
    plane, core = lax.div(section, 2), lax.rem(section, 2)
    loads = [pltpu.make_async_copy(pieces_ref.at[p], held.at[p], load_sem.at[p]) for p in range(PIECES)]
    for load in loads:
        load.start()
    pairs = ((first_ref, first_out), (second_ref, second_out), (input_ref, input_out), (middle_ref, middle_out))
    takes = [pltpu.make_async_copy(a, passed.at[n], pass_sem.at[n]) for n, (a, _) in enumerate(pairs)]
    passes = [pltpu.make_async_copy(passed.at[n], b, pass_sem.at[4 + n]) for n, (_, b) in enumerate(pairs)]
    for copy in takes:
        copy.start()

    def place(piece):
        if piece < 8:
            return down_out.at[pl.ds(piece // 2 * PIECE, PIECE), pl.ds(piece % 2 * WIDTH, WIDTH)]
        if piece < 24:
            return gated_out.at[:, pl.ds((piece - 8) * WIDTH, WIDTH)]
        if piece < 30:
            return joint_out.at[:, pl.ds((piece - 24) * WIDTH, WIDTH)]
        return mixing_out.at[:, pl.ds((piece - 30) * WIDTH, WIDTH)]

    stores = [pltpu.make_async_copy(wide.at[p % SLOTS], place(p), store_sem.at[p % SLOTS]) for p in range(PIECES)]
    for p in range(PIECES):
        loads[p].wait()
        if p >= SLOTS:
            stores[p - SLOTS].wait()
        wide[p % SLOTS] = held[p].astype(F32)
        stores[p].start()

    for take, copy in zip(takes, passes):
        take.wait()
        copy.start()

    gain_out[...] = small_ref[pl.ds(2 * core, 1), :]
    bias_out[...] = small_ref[pl.ds(2 * core + 1, 1), :]
    count = small_ref[8:9, :1] * D
    row = lax.broadcasted_iota(jnp.int32, (2, 4), 0)
    lane = lax.broadcasted_iota(jnp.int32, (2, 4), 1)
    stats = jnp.zeros((2, 4), F32)
    for n in range(4):
        for at, source in ((2 * plane, small_ref), (2 - 2 * plane, other_ref)):
            value = jnp.sum(source[4 + n : 5 + n, :], axis=1, keepdims=True) / count
            stats = jnp.where((row == n // 2) & (lane == at + n % 2), jnp.sqrt(value), stats)
    stats_out[...] = stats
    for p in range(PIECES - SLOTS, PIECES):
        stores[p].wait()
    for copy in passes:
        copy.wait()


def place_results(pieces, small, other, *rows):
    any_spec, vmem = pl.BlockSpec(memory_space=pl.ANY), pl.BlockSpec(memory_space=pltpu.VMEM)
    shapes = ((HALF, 3 * D), (HALF, D), (HALF, 2 * FF), (FF // 2, D), (1, D), (1, D), (2, 4))
    return pl.pallas_call(
        place_kernel,
        out_shape=[jax.ShapeDtypeStruct(r.shape, BF) for r in rows] + [jax.ShapeDtypeStruct(s, F32) for s in shapes],
        in_specs=[any_spec, vmem, vmem] + [any_spec] * 4,
        out_specs=[any_spec] * 8 + [vmem] * 3,
        scratch_shapes=[
            pltpu.VMEM((PIECES, PIECE, WIDTH), BF), pltpu.VMEM((SLOTS, PIECE, WIDTH), F32),
            pltpu.VMEM((4,) + rows[0].shape, BF),
            pltpu.SemaphoreType.DMA((PIECES,)), pltpu.SemaphoreType.DMA((SLOTS,)), pltpu.SemaphoreType.DMA((8,)),
        ],
        compiler_params=pltpu.CompilerParams(vmem_limit_bytes=61 * 2**20),
    )(pieces, small, other, *rows)


def per_device(
    inputs, cotangent_first, cotangent_second, segment_ids,
    joint_projection, mixing_weight, gated_weight, down_weight, norm_gain, norm_bias,
):
    segments = segment_ids.reshape(-1, BLOCK)
    *rows, _, _, pieces, small, other = run_layer(
        lax.axis_size("dp") // 2, inputs, cotangent_first, cotangent_second, segments,
        joint_projection, mixing_weight, gated_weight, down_weight, norm_gain, norm_bias,
    )
    return tuple(place_results(pieces, small, other, *rows))


def solution(mesh):
    tokens, rows = P("dp", None), P("section", None)
    return jax.shard_map(
        per_device,
        mesh=mesh,
        in_specs=(tokens, tokens, tokens, P("dp"), rows, rows, rows, rows, rows, rows),
        out_specs=(P(("dp", "section"), None),) * 4 + (rows,) * 6 + (P(),),
        check_vma=False,
    )
```

```python
import functools

import jax
import jax.numpy as jnp
from jax import lax
from jax.experimental import pallas as pl
from jax.experimental.pallas import tpu as pltpu
from jax.sharding import PartitionSpec as P

D = 768
HEADS = 12
HEAD = D // HEADS
FF = 3072
BLOCK = 128
HALF = D // 2
PAIRS = HEADS // 2
TOKENS = 512
MICRO = 2
ROWS = TOKENS // MICRO
CHUNK = 1024
PART = 512
CHUNKS = FF // CHUNK
SMALL = 16
PIECES = 32
PIECE = 384
SIDE = 112
RAIL = 160
WIDTH = 384
AHEAD = 3
LAG = 2
RING = 16
BLOCKS = ROWS // BLOCK
TILES = 16
SLOTS = 8

EPSILON = 1e-05
FAR = 1e30
ROOT_HALF = 0.7071067811865476
ROOT_TWO_PI = 2.5066282746310002
SCALE = HEAD**-0.5

MESH = pl.DeviceIdType.MESH
BF = jnp.bfloat16
F32 = jnp.float32


def alibi_slopes():
    closest = 1 << HEADS.bit_length() - 1
    first_slope = 2.0 ** (-8.0 / closest)
    slopes = [first_slope ** (power_index + 1) for power_index in range(closest)]
    double_slope = 2.0 ** (-8.0 / (2 * closest))
    extra_slopes = [double_slope ** (power_index + 1) for power_index in range(2 * closest)]
    return slopes + extra_slopes[0::2][: HEADS - closest]


SLOPES = alibi_slopes()


def dot(a, b):
    return jnp.dot(a, b, preferred_element_type=F32)


def dot_right(a, b):
    return lax.dot_general(a, b, (((1,), (1,)), ((), ())), preferred_element_type=F32)


def dot_left(a, b):
    return lax.dot_general(a, b, (((0,), (0,)), ((), ())), preferred_element_type=F32)


def lane_mean(x):
    return jnp.sum(x, axis=-1, keepdims=True) * (1.0 / D)


def remote(src, dst, send, recv, device):
    return pltpu.make_async_remote_copy(
        src_ref=src, dst_ref=dst, send_sem=send, recv_sem=recv, device_id=device, device_id_type=MESH
    )


def settled(ref, sem):
    pltpu.make_async_copy(ref, ref, sem).wait()


def layer_kernel(
    lines,
    inputs_ref, first_ref, second_ref, segments_ref, joint_ref, mixing_ref, gated_ref, down_ref, gain_ref, bias_ref,
    first_out, second_out, input_out, middle_out, mine_out, landed_out, pieces_out, small_out, other_out,
    joint_w, mixing_w, gated_w, down_w, norms,
    rows, attended, out, swapped, upstream, back,
    joint_rows, probs, mixed, hidden, active, slope, both_grad,
    branch_first, branch_second, scaled_first, scaled_second, spread, columns,
    total, small, small_in, mixed_grad, staged, high,
    load_sem, local_sem, weight_send, weight_recv, norm_sem, norm_send, norm_recv,
    ahead_send, ahead_recv, behind_send, behind_recv, swap_send, swap_recv, out_sem,
    keep_sem, give_send, give_recv, ready_sem,
    own_sem, other_sem, store_sem, small_send, small_recv, side_send, side_recv, inner_send, inner_recv,
    up_send, low_recv, high_recv, root_recv, line_send, back_send, back_recv, low_send, high_send,
):
    dp, section = lax.axis_index("dp"), lax.axis_index("section")
    plane, core = lax.div(section, 2), lax.rem(section, 2)
    partner = (dp, section + 1 - 2 * core)
    peer = (dp, section + 2 - 4 * plane)

    y, z = lax.rem(dp, 2), lax.div(dp, 2)
    across, below, above = (dp + 1 - 2 * y, section), (dp - 2, section), (dp + 2, section)
    has_low, has_high = z > 0, z < lines - 1
    near = 1 + has_low.astype(jnp.int32) + has_high.astype(jnp.int32)

    def signal_near(semaphore):
        pl.semaphore_signal(semaphore, inc=1, device_id=across, device_id_type=MESH)

        @pl.when(has_low)
        def _():
            pl.semaphore_signal(semaphore, inc=1, device_id=below, device_id_type=MESH)

        @pl.when(has_high)
        def _():
            pl.semaphore_signal(semaphore, inc=1, device_id=above, device_id_type=MESH)

    barrier = pltpu.get_barrier_semaphore()
    pl.semaphore_signal(barrier, inc=1, device_id=partner, device_id_type=MESH)
    pl.semaphore_signal(barrier, inc=1, device_id=peer, device_id_type=MESH)
    signal_near(barrier)
    pl.semaphore_wait(barrier, 2 + near)

    mine = pl.ds(pl.multiple_of(core * HALF, HALF), HALF)
    theirs = pl.ds(pl.multiple_of((1 - core) * HALF, HALF), HALF)

    def micro_rows(m):
        return pl.ds(pl.multiple_of(m * ROWS, ROWS), ROWS)

    def token_loads():
        copies = []
        for m in range(2):
            there = pl.ds(pl.multiple_of((2 * m + core) * (TOKENS // 2), TOKENS // 2), TOKENS // 2)
            here = pl.ds(m * (TOKENS // 2), TOKENS // 2)
            copies.append(pltpu.make_async_copy(first_ref.at[there], back.at[here], load_sem.at[2 * m]))
            copies.append(pltpu.make_async_copy(second_ref.at[there], upstream.at[here], load_sem.at[2 * m + 1]))
        return copies

    def input_loads():
        copies = []
        for m in range(2):
            there = pl.ds(pl.multiple_of((2 * m + core) * (TOKENS // 2), TOKENS // 2), TOKENS // 2)
            here = pl.ds(m * (TOKENS // 2), TOKENS // 2)
            copies.append(pltpu.make_async_copy(inputs_ref.at[there], rows.at[here], load_sem.at[4 + m]))
        return copies

    def chunk(k):
        return pl.ds(pl.multiple_of(k * CHUNK, CHUNK), CHUNK)

    def upper(k):
        return pl.ds(pl.multiple_of(FF + k * CHUNK, CHUNK), CHUNK)

    def weight_copies(which):
        if which == 0:
            return [(joint_ref, joint_w.at[mine], joint_w.at[theirs], 0), (mixing_ref, mixing_w.at[mine], mixing_w.at[theirs], 1)]
        copies = []
        for k in range(CHUNKS):
            for n, columns_at in enumerate((chunk(k), upper(k))):
                copies.append((gated_ref.at[:, columns_at], gated_w.at[mine, columns_at], gated_w.at[theirs, columns_at], 2 + 2 * k + n))
            here = pl.ds(pl.multiple_of(core * (FF // 2) + k * PART, PART), PART)
            there = pl.ds(pl.multiple_of((1 - core) * (FF // 2) + k * PART, PART), PART)
            copies.append((down_ref.at[pl.ds(k * PART, PART)], down_w.at[here], down_w.at[there], 2 + 2 * CHUNKS + k))
        return copies

    def start_weights(which):
        for source, place, _, n in weight_copies(which):
            remote(source, place, weight_send.at[n], weight_recv.at[n], partner).start()
            pltpu.make_async_copy(source, place, local_sem.at[n]).start()

    def wait_weights(which):
        for source, place, other, n in weight_copies(which):
            pltpu.make_async_copy(source, place, local_sem.at[n]).wait()
            settled(other, weight_recv.at[n])

    def wait_chunk(k):
        for source, place, other, n in weight_copies(1)[3 * k : 3 * k + 2]:
            pltpu.make_async_copy(source, place, local_sem.at[n]).wait()
            settled(other, weight_recv.at[n])
        for part in (2 * k, 2 * k + 1):
            source, _, _, n = weight_copies(1)[3 * (part % CHUNKS) + 2]
            place = down_w.at[pl.ds(part * PART, PART)]

            @pl.when(core == part // CHUNKS)
            def _():
                pltpu.make_async_copy(source, place, local_sem.at[n]).wait()

            @pl.when(core != part // CHUNKS)
            def _():
                settled(place, weight_recv.at[n])

    def wait_weights_sent(which):
        for source, place, _, n in weight_copies(which):
            remote(source, place, weight_send.at[n], weight_recv.at[n], partner).wait_send()

    norm_copies = []
    for n, source in enumerate((gain_ref, bias_ref)):
        norm_copies.append((source, norms.at[n, core], norms.at[n, 1 - core], n))
    for source, place, _, n in norm_copies:
        remote(source, place, norm_send.at[n], norm_recv.at[n], partner).start()
        pltpu.make_async_copy(source, place, norm_sem.at[n]).start()
    start_weights(0)

    @pl.when(plane == 0)
    def _():
        for copy in input_loads():
            copy.start()

    @pl.when(plane == 1)
    def _():
        for copy in token_loads():
            copy.start()

    start_weights(1)

    first = lax.broadcasted_iota(jnp.int32, (BLOCK, BLOCK), 0)
    second = lax.broadcasted_iota(jnp.int32, (BLOCK, BLOCK), 1)
    distance = jnp.abs(first - second).astype(F32)
    half_blocks = TOKENS // (2 * BLOCK)
    for b in range(TOKENS // BLOCK):
        at = (2 * (b // half_blocks) + core) * half_blocks + b % half_blocks
        along = jnp.broadcast_to(segments_ref[pl.ds(at, 1), :].astype(F32), (BLOCK, BLOCK))
        down = along.T
        spread[b] = jnp.where(along == down, distance, FAR)
        columns[pl.ds(b * BLOCK, BLOCK), :] = jnp.where(down >= 0.0, 1.0, 0.0)
    small[0] = jnp.zeros_like(small[0])
    small[0, 8:9, :BLOCK] = jnp.sum(columns[...], axis=0, keepdims=True)

    lane = lax.broadcasted_iota(jnp.int32, (1, BLOCK), 1)
    low_lanes = jnp.where(lane < HEAD, 1.0, 0.0).astype(BF)
    high_lanes = jnp.where(lane < HEAD, 0.0, 1.0).astype(BF)

    def stacked(x):
        return jnp.concatenate([x * low_lanes, x * high_lanes], axis=0)

    def beside(x):
        return jnp.concatenate([x[:BLOCK], x[BLOCK:]], axis=1)

    for source, place, other, n in norm_copies:
        pltpu.make_async_copy(source, place, norm_sem.at[n]).wait()
        settled(other, norm_recv.at[n])

    def add_small(row, value):
        small[0, row : row + 1, :] += value

    def keep_column(r, at, value):
        columns[r] = jnp.where(lane == at, value, columns[r])

    def column(value):
        return jnp.sum(value, axis=0, keepdims=True)

    def post_norm(r, source, branch, kind, scaled_ref, result_ref):
        before = source[r].astype(F32)
        ok = columns[r, :1]
        add_small(4 + kind, column(ok * (before * before)))
        add_small(6 + kind, column(ok * (branch * branch)))
        summed = before + branch
        center = summed - lane_mean(summed)
        inverse = lax.rsqrt(lane_mean(center * center) + EPSILON)
        scaled = center * inverse
        scaled_ref[r] = scaled
        keep_column(r, 1 + kind, inverse)
        result_ref[r] = (scaled * norms[0, kind] + norms[1, kind]).astype(BF)

    def norm_back(r, grad, kind, scaled_ref):
        scaled = scaled_ref[r]
        add_small(2 * kind, column(grad * scaled))
        add_small(2 * kind + 1, column(grad))
        inner = grad * norms[0, kind]
        return columns[r, 1 + kind : 2 + kind] * (inner - lane_mean(inner) - scaled * lane_mean(inner * scaled))

    def in_step(units):
        units = list(units)
        while units:
            units = [u for u in units if next(u, units) is not units]

    def block_rows(b):
        return pl.ds(pl.multiple_of(b * BLOCK, BLOCK), BLOCK)

    def ahead(b):
        r = block_rows(b)
        return remote(out.at[r], rows.at[r], ahead_send.at[b], ahead_recv.at[b], peer)

    def behind(b):
        r = block_rows(b)
        return remote(back.at[r], upstream.at[r], behind_send.at[b], behind_recv.at[b], peer)

    front, rear = pl.ds(0, TOKENS // 2), pl.ds(TOKENS // 2, TOKENS // 2)

    def attend(m):
        r = micro_rows(m)
        for j in range(BLOCKS):
            b = m * BLOCKS + j

            @pl.when(plane == 1)
            def _(b=b):
                ahead(b).wait_recv()

            at = block_rows(b)
            joint_rows[at] = dot(rows[at], joint_w[...]).astype(BF)
            far = spread[b]

            def pair(p, b=b, at=at, far=far):
                queries, keys, values = [joint_rows[at, pl.ds(n * D + p * BLOCK, BLOCK)] for n in range(3)]
                raw = dot_right(stacked(queries), keys)
                yield
                parts = []
                for e in range(2):
                    scores = raw[e * BLOCK : (e + 1) * BLOCK] * SCALE - SLOPES[2 * p + e] * far
                    weights = jnp.exp(scores - jnp.max(scores, axis=-1, keepdims=True))
                    parts.append(weights * (1.0 / jnp.sum(weights, axis=-1, keepdims=True)))
                soft = jnp.concatenate(parts, axis=0)
                probs[b * PAIRS + p] = soft
                yield
                mixed[at, pl.ds(p * BLOCK, BLOCK)] = dot(beside(soft.astype(BF)), stacked(values)).astype(BF)

            in_step([pair(p) for p in range(PAIRS)])
        branch = dot(mixed[r], mixing_w[...])
        post_norm(r, rows, branch, 0, scaled_first, attended)

    def feed(m, arriving):
        r = micro_rows(m)
        branch = 0.0
        for k in range(CHUNKS):
            if arriving:
                wait_chunk(k)
            gate = dot(attended[r], gated_w[:, chunk(k)])
            up = dot(attended[r], gated_w[:, upper(k)])
            normal = 0.5 + 0.5 * lax.erf(gate * ROOT_HALF)
            density = jnp.exp(-0.5 * gate * gate) * (1.0 / ROOT_TWO_PI)
            gelu = gate * normal
            low = (gelu * up).astype(BF)
            hidden[r, chunk(k)] = low
            active[r, chunk(k)] = gelu.astype(BF)
            slope[r, chunk(k)] = (up * (normal + gate * density)).astype(BF)
            if arriving:
                total[...] = dot(low, down_w[chunk(k)]) + (total[...] if k else 0.0)
            else:
                branch += dot(low, down_w[chunk(k)])
        if not arriving:
            total[...] = branch
        post_norm(r, attended, total[...], 1, scaled_second, out)

    def feed_norm_back(m, grad):
        r = micro_rows(m)
        through = norm_back(r, grad, 1, scaled_second)
        branch_second[r] = through.astype(BF)
        total[...] = through

    def feed_back(m):
        r = micro_rows(m)
        through = total[...]
        for k in range(CHUNKS):
            hidden_grad = dot_right(branch_second[r], down_w[chunk(k)])
            gate_grad = (hidden_grad * slope[r, chunk(k)].astype(F32)).astype(BF)
            up_grad = (hidden_grad * active[r, chunk(k)].astype(F32)).astype(BF)
            both_grad[r, chunk(k)] = gate_grad
            both_grad[r, upper(k)] = up_grad
            through += dot_right(gate_grad, gated_w[:, chunk(k)]) + dot_right(up_grad, gated_w[:, upper(k)])
        total[...] = through

    def attend_back(m, grad):
        r = micro_rows(m)
        through = norm_back(r, grad, 0, scaled_first)
        branch_first[r] = through.astype(BF)
        total[...] = through
        mixed_grad[...] = dot_right(branch_first[r], mixing_w[...]).astype(BF)
        for j in range(BLOCKS):
            b = m * BLOCKS + j
            at = block_rows(b)

            def pair(p, b=b, j=j, at=at):
                lanes = [pl.ds(n * D + p * BLOCK, BLOCK) for n in range(3)]
                queries, keys, values = [joint_rows[at, n] for n in lanes]
                above = stacked(mixed_grad[j * BLOCK : (j + 1) * BLOCK, p * BLOCK : (p + 1) * BLOCK])
                soft = probs[b * PAIRS + p]
                probs_grad = dot_right(above, values)
                yield
                values_grad = dot_left(soft.astype(BF), above)
                score_grad = soft * (probs_grad - jnp.sum(probs_grad * soft, axis=-1, keepdims=True))
                score_grad = score_grad.astype(BF)
                yield
                queries_grad = SCALE * dot(beside(score_grad), stacked(keys))
                keys_grad = SCALE * dot_left(score_grad, stacked(queries))
                yield
                for n, grad_part in zip(lanes, (queries_grad, keys_grad, values_grad)):
                    joint_rows[at, n] = grad_part.astype(BF)

            in_step([pair(p) for p in range(PAIRS)])
            grad_rows = total[j * BLOCK : (j + 1) * BLOCK, :] + dot_right(joint_rows[at], joint_w[...])

            @pl.when(plane == 0)
            def _(at=at, grad_rows=grad_rows):
                back[at] = grad_rows.astype(BF)

            @pl.when(plane == 1)
            def _(b=b, at=at, grad_rows=grad_rows):
                back[at] = (grad_rows + columns[at, :1] * back[at].astype(F32)).astype(BF)
                behind(b).start()


    wait_weights(0)

    @pl.when(plane == 0)
    def _():
        for copy in input_loads():
            copy.wait()

    def forward_step(step, carry):
        feeding = jnp.where(plane == 0, lax.div(step, MICRO), lax.rem(step, 2))
        m = jnp.where(plane == 0, lax.rem(step, MICRO), lax.div(step, 2))

        @pl.when(feeding == 0)
        def _():
            attend(m)

        @pl.when(feeding == 1)
        def _():
            @pl.when(m == 0)
            def _():
                feed(0, True)

            @pl.when(m > 0)
            def _():
                feed(m, False)

            @pl.when(plane == 0)
            def _():
                for j in range(BLOCKS):
                    ahead(m * BLOCKS + j).start()

        return carry

    lax.fori_loop(0, 2 * MICRO, forward_step, 0)

    @pl.when(plane == 1)
    def _():
        remote(out.at[front], swapped, swap_send, swap_recv, peer).start()

    def pairs(n, height):
        tile = tile_of(n)
        row = jnp.where(tile < 4, lax.rem(tile, 2) * D, tile * PIECE)
        return pl.ds(pl.multiple_of(row, PIECE), height)

    def half_tile(n, which):
        return staged.at[lax.rem(n, 2), pl.ds(pl.multiple_of(which * PIECE, PIECE), PIECE)]

    def keep(n, source, height):
        return pltpu.make_async_copy(source, mine_out.at[pairs(n, height)], keep_sem.at[lax.rem(n, 2)])

    def give(n, source, height):
        unit = jnp.where(n < 4, lax.rem(tile_of(n), 2), n - 2)
        return remote(source, landed_out.at[pairs(n, height)], give_send.at[lax.rem(n, 2)], give_recv.at[unit], partner)

    def wide(k):
        return pl.ds(pl.multiple_of(k * D, D), D)

    def tile_of(n):
        return n + (n == 1).astype(jnp.int32) - (n == 2).astype(jnp.int32)

    def each_part(n, kept, given):
        tile = tile_of(n)

        @pl.when((tile < 4) & (lax.div(tile, 2) == core))
        def _():
            kept(keep(n, staged.at[lax.rem(n, 2)], D))

        @pl.when((tile < 4) & (lax.div(tile, 2) != core))
        def _():
            given(give(n, staged.at[lax.rem(n, 2)], D))

        @pl.when(tile >= 4)
        def _():
            kept(keep(n, half_tile(n, core), PIECE))
            given(give(n, half_tile(n, 1 - core), PIECE))

    def finish(n):
        each_part(n, lambda copy: copy.wait(), lambda copy: copy.wait_send())

    def launch(n, value):
        staged[lax.rem(n, 2)] = value.astype(BF)
        each_part(n, lambda copy: copy.start(), lambda copy: copy.start())

    def down_tile(n):
        launch(n, dot_left(hidden[:, wide(tile_of(n))], branch_second[...]))

    def first_tiles():
        down_tile(jnp.int32(0))
        down_tile(jnp.int32(1))

    @pl.when(plane == 1)
    def _():
        for copy in token_loads():
            copy.wait()

    def backward_step(m, carry):
        r = micro_rows(m)

        @pl.when(plane == 0)
        def _():
            for j in range(BLOCKS):
                behind(m * BLOCKS + j).wait_recv()

        @pl.when(plane == 1)
        def _():
            upstream[r] = (columns[r, :1] * upstream[r].astype(F32)).astype(BF)

        feed_norm_back(m, upstream[r].astype(F32))

        @pl.when((plane == 0) & (m == MICRO - 1))
        def _():
            first_tiles()

        feed_back(m)

        @pl.when((plane == 1) | (m < MICRO - 1))
        def _():
            attend_back(m, total[...].astype(BF).astype(F32))

        return carry

    lax.fori_loop(0, MICRO, backward_step, 0)

    def last_attend_back():
        attend_back(MICRO - 1, total[...].astype(BF).astype(F32))
        remote(back.at[rear], swapped, swap_send, swap_recv, peer).start()

    def task(i):
        n = i + 3

        @pl.when(i == 0)
        def _():
            down_tile(n)
            finish(n - 1)

        @pl.when((i > 0) & (i < 9))
        def _():
            launch(n, dot_left(attended[...], both_grad[:, wide(n - 4)]))
            finish(n - 1)

        @pl.when((i == 9) & (plane == 0))
        def _():
            last_attend_back()

        @pl.when((i >= 10) & (i < 13))
        def _():
            launch(n - 1, dot_left(rows[...], joint_rows[:, wide(n - 13)]))
            finish(n - 2)

        @pl.when(i == 13)
        def _():
            launch(n - 1, dot_left(mixed[...], branch_first[...]))
            finish(n - 2)

        @pl.when(i == 14)
        def _():
            finish(n - 2)

    signal_near(ready_sem)
    @pl.when(plane == 1)
    def _():
        first_tiles()

    finish(jnp.int32(0))
    down_tile(jnp.int32(2))
    finish(jnp.int32(1))
    half = lines // 2
    mid = half - 1
    lower = z < half
    depth = jnp.where(lower, z, lines - 1 - z)
    inward = (jnp.where(lower, dp + 2, dp - 2), section)
    outward = (jnp.where(lower, dp - 2, dp + 2), section)
    my_side, other_side = y * SIDE, (1 - y) * SIDE
    pause = max(0, LAG * (2 * lines - 1) - (RING - 2))

    def window(ref, row, column, height):
        return ref.at[pl.ds(pl.multiple_of(row, 16), height), pl.ds(pl.multiple_of(column * WIDTH, WIDTH), WIDTH)]

    def slot(b):
        return lax.rem(b, RING)

    def grown(b, row=0, height=PIECE):
        return window(gated_w, row, slot(b), height)

    def sums(b, row=0, height=PIECE):
        return window(gated_w, PIECE + row, slot(b), height)

    def landed(b):
        return window(down_w, lax.rem(b, 8) * PIECE, 0, PIECE)

    def from_side(b):
        return window(down_w, lax.div(slot(b), 2) * PIECE + lax.rem(b, 2) * SIDE, 1, SIDE)

    def from_inner(n, b):
        return window(active, (2 * n + lax.div(slot(b), 8)) * SIDE, lax.rem(b, 8), SIDE)

    def from_low(b):
        return window(slope, lax.div(slot(b), 8) * RAIL, lax.rem(b, 8), RAIL)

    def from_high(b):
        return high.at[slot(b)]

    def from_root(b):
        return window(slope, 2 * RAIL, lax.rem(lax.div(b, 2), 8), RAIL)

    def from_pair(ref, b):
        row = pl.multiple_of(lax.div(b, 2) * PIECE, PIECE)
        return ref.at[pl.ds(row, PIECE), pl.ds(pl.multiple_of(lax.rem(b, 2) * WIDTH, WIDTH), WIDTH)]

    def load_own(b):
        return pltpu.make_async_copy(from_pair(mine_out, b), grown(b), own_sem.at[lax.rem(b, AHEAD + 1)])

    def load_other(b):
        return pltpu.make_async_copy(from_pair(landed_out, b), landed(b), other_sem.at[lax.rem(b, AHEAD + 1)])

    def store(b):
        return pltpu.make_async_copy(sums(b), pieces_out.at[b], store_sem.at[slot(b)])

    def root_of(b):
        odd = lax.rem(b, 2)
        return jnp.where(lax.rem(b, 4) < 2, odd * (lines - 1), mid + odd)

    def release_grown(b):
        root = root_of(b)
        settled(grown(b, other_side, SIDE), side_send.at[slot(b)])
        settled(grown(b, my_side, SIDE), inner_send.at[slot(b)])

        @pl.when(z != root)
        def _():
            settled(grown(b, 2 * SIDE, RAIL), up_send.at[slot(b)])

        @pl.when(z == root)
        def _():
            settled(grown(b, 2 * SIDE, RAIL), up_send.at[slot(b)])

    def release_sums(b):
        root = root_of(b)
        store(b).wait()
        settled(sums(b, my_side, SIDE), back_send.at[slot(b)])

        @pl.when(depth > 0)
        def _():
            settled(sums(b, my_side, SIDE), line_send.at[slot(b)])

        @pl.when(has_low & (z <= root))
        def _():
            settled(sums(b, 2 * SIDE, RAIL), low_send.at[slot(b)])

        @pl.when(has_high & (z >= root))
        def _():
            settled(sums(b, 2 * SIDE, RAIL), high_send.at[slot(b)])

    def load(b):
        @pl.when((b < 8) & (lax.rem(b, 4) == 0))
        def _():
            settled(landed_out.at[pl.ds(0, D)], give_recv.at[lax.div(b, 4)])

        @pl.when((b >= 8) & (lax.rem(b, 2) == 0))
        def _():
            settled(landed_out.at[pl.ds(0, PIECE)], give_recv.at[lax.div(b, 2) - 2])

        load_own(b).start()
        load_other(b).start()

    def add(into, first, *others):
        value = first[...].astype(F32)
        for other in others:
            value = value + other[...].astype(F32)
        into[...] = value.astype(BF)

    def piece_at(j):
        if pause == 0:
            return j
        return jnp.where(j < RING, j, jnp.where(j < RING + pause, -1, j - pause))

    def when(active_now, b):
        return pl.when(active_now & (b >= 0) & (b < PIECES))

    def small_sum(n, source, arrival):
        settled(small_in.at[arrival], small_recv.at[arrival])
        small[n] = small[source] + small_in[arrival]

    def small_step(i):
        @pl.when(i == 14)
        def _():
            remote(small.at[0], small_in.at[0], small_send.at[0], small_recv.at[0], partner).start()

        @pl.when(i == 16)
        def _():
            small_sum(1, 0, 0)
            remote(small.at[1], small_in.at[1], small_send.at[1], small_recv.at[1], across).start()

        @pl.when(i == 18 + 2 * depth)
        def _():
            small_sum(2, 1, 1)

            @pl.when(depth > 0)
            def _():
                small_sum(3, 2, 2)

            @pl.when(depth == 0)
            def _():
                small[3] = small[2]

            into = jnp.where(depth == mid, 3, 2)
            remote(small.at[3], small_in.at[into], small_send.at[2], small_recv.at[into], inward).start()

        @pl.when(i == 20 + 2 * (2 * mid - depth))
        def _():
            @pl.when(depth == mid)
            def _():
                small_sum(4, 3, 3)

            @pl.when(depth < mid)
            def _():
                settled(small.at[4], small_recv.at[4])

            @pl.when(depth > 0)
            def _():
                remote(small.at[4], small.at[4], small_send.at[3], small_recv.at[4], outward).start()

            remote(small.at[4], small_in.at[4], small_send.at[4], small_recv.at[5], peer).start()

    def writes(which):
        pairs = [
            [(out.at[front], first_out), (swapped, second_out), (back.at[front], input_out), (upstream.at[front], middle_out)],
            [(rows.at[rear], first_out), (out.at[rear], second_out), (swapped, input_out), (back.at[rear], middle_out)],
        ][which]
        return [pltpu.make_async_copy(a, b, out_sem.at[n]) for n, (a, b) in enumerate(pairs)]

    def small_writes():
        pairs = ((small.at[4], small_out), (small_in.at[4], other_out))
        return [pltpu.make_async_copy(a, b, out_sem.at[4 + n]) for n, (a, b) in enumerate(pairs)]

    def output_step(i):
        @pl.when(i == 20)
        def _():
            remote(out.at[front], swapped, swap_send, swap_recv, peer).wait_recv()
            for which in range(2):
                @pl.when(plane == which)
                def _(which=which):
                    for copy in writes(which):
                        copy.start()

        @pl.when(i == 24 + 4 * mid)
        def _():
            small_finish()
            for copy in small_writes():
                copy.start()

    def small_finish():
        settled(small_in.at[4], small_recv.at[5])
        settled(small.at[0], small_send.at[0])
        settled(small.at[1], small_send.at[1])
        settled(small.at[3], small_send.at[2])
        settled(small.at[4], small_send.at[4])

        @pl.when(depth > 0)
        def _():
            settled(small.at[4], small_send.at[3])

    def step(i, carry):
        small_step(i)
        output_step(i)

        b1 = piece_at(i - LAG * (1 + depth))

        @when(True, b1)
        def _():
            settled(from_side(b1), side_recv.at[slot(b1)])

            @pl.when(depth == 0)
            def _():
                add(grown(b1, my_side, SIDE), grown(b1, my_side, SIDE), from_side(b1))

            @pl.when(depth > 0)
            def _():
                settled(from_inner(0, b1), inner_recv.at[0, slot(b1)])
                add(grown(b1, my_side, SIDE), grown(b1, my_side, SIDE), from_side(b1), from_inner(0, b1))

            into = (depth == mid).astype(jnp.int32)
            remote(grown(b1, my_side, SIDE), from_inner(into, b1), inner_send.at[slot(b1)], inner_recv.at[into, slot(b1)], inward).start()

        b2 = piece_at(i - LAG * (2 + mid + mid - depth))

        @when(True, b2)
        def _():
            @pl.when(depth == mid)
            def _():
                settled(from_inner(1, b2), inner_recv.at[1, slot(b2)])
                add(sums(b2, my_side, SIDE), grown(b2, my_side, SIDE), from_inner(1, b2))

            @pl.when(depth < mid)
            def _():
                settled(sums(b2, my_side, SIDE), inner_recv.at[1, slot(b2)])

            part = sums(b2, my_side, SIDE)

            @pl.when(depth > 0)
            def _():
                remote(part, part, line_send.at[slot(b2)], inner_recv.at[1, slot(b2)], outward).start()

            remote(part, part, back_send.at[slot(b2)], back_recv.at[slot(b2)], across).start()

        b3 = piece_at(i - LAG * (3 + mid + mid - depth))

        @when(True, b3)
        def _():
            settled(sums(b3, other_side, SIDE), back_recv.at[slot(b3)])

        for early in (True, False):
            for odd in (0, 1):
                root = (odd * (lines - 1)) if early else mid + odd
                height = max(root, lines - 1 - root)
                distance = jnp.abs(z - root)

                def matches(b, root=root, odd=odd):
                    return (root_of(b) == root) & (lax.rem(b + 2 * PIECES, 2) == odd)

                hop = jnp.where(z < root, z, jnp.where(z > root, lines - 1 - z, height))
                c1 = piece_at(i - LAG * hop)

                @when((z != root) & (hop > 0) & matches(c1), c1)
                def _(root=root, c1=c1):
                    part = grown(c1, 2 * SIDE, RAIL)

                    @pl.when(z < root)
                    def _():
                        settled(from_low(c1), low_recv.at[slot(c1)])
                        add(part, part, from_low(c1))
                        remote(part, from_low(c1), up_send.at[slot(c1)], low_recv.at[slot(c1)], above).start()

                    @pl.when(z > root)
                    def _():
                        settled(from_high(c1), high_recv.at[slot(c1)])
                        add(part, part, from_high(c1))
                        remote(part, from_high(c1), up_send.at[slot(c1)], high_recv.at[slot(c1)], below).start()

                @when((z == root) & matches(c1), c1)
                def _(root=root, c1=c1):
                    part = grown(c1, 2 * SIDE, RAIL)
                    others = []
                    if root > 0:
                        settled(from_low(c1), low_recv.at[slot(c1)])
                        others.append(from_low(c1))
                    if root < lines - 1:
                        settled(from_high(c1), high_recv.at[slot(c1)])
                        others.append(from_high(c1))
                    add(part, part, *others)
                    remote(part, from_root(c1), up_send.at[slot(c1)], root_recv.at[slot(c1)], across).start()

                c2 = piece_at(i - LAG * (height + 1 + distance))

                @when(matches(c2), c2)
                def _(root=root, c2=c2):
                    part = sums(c2, 2 * SIDE, RAIL)

                    @pl.when(z == root)
                    def _():
                        settled(from_root(c2), root_recv.at[slot(c2)])
                        add(part, grown(c2, 2 * SIDE, RAIL), from_root(c2))

                    @pl.when(z != root)
                    def _():
                        settled(part, root_recv.at[slot(c2)])

                    @pl.when(has_low & (z <= root))
                    def _():
                        remote(part, part, low_send.at[slot(c2)], root_recv.at[slot(c2)], below).start()

                    @pl.when(has_high & (z >= root))
                    def _():
                        remote(part, part, high_send.at[slot(c2)], root_recv.at[slot(c2)], above).start()

        b6 = piece_at(i - LAG * (2 * lines - 2))

        @when(True, b6)
        def _():
            release_grown(b6)

        b4 = piece_at(i - LAG * (2 * lines - 1))

        @when(True, b4)
        def _():
            store(b4).start()

        b0 = piece_at(i)

        @when(True, b0)
        def _():
            @pl.when(b0 >= RING)
            def _():
                release_sums(b0 - RING)

            load_own(b0).wait()
            load_other(b0).wait()
            add(grown(b0), grown(b0), landed(b0))
            remote(grown(b0, other_side, SIDE), from_side(b0), side_send.at[slot(b0)], side_recv.at[slot(b0)], across).start()
            part, root = grown(b0, 2 * SIDE, RAIL), root_of(b0)

            @pl.when((z == 0) & (root != 0))
            def _():
                remote(part, from_low(b0), up_send.at[slot(b0)], low_recv.at[slot(b0)], above).start()

            @pl.when((z == lines - 1) & (root != lines - 1))
            def _():
                remote(part, from_high(b0), up_send.at[slot(b0)], high_recv.at[slot(b0)], below).start()

        task(i)
        b5 = piece_at(i + AHEAD)

        @when(i > 0, b5)
        def _():
            load(b5)

        return carry

    def first_load(b, carry):
        load(b)
        return carry

    lax.fori_loop(0, AHEAD + 1, first_load, 0)
    pl.semaphore_wait(ready_sem, near)
    lax.fori_loop(0, PIECES + pause + LAG * (2 * lines - 1), step, 0)
    def release_last(b, carry):
        release_sums(b)
        return carry

    lax.fori_loop(PIECES - RING, PIECES, release_last, 0)

    for copy in small_writes():
        copy.wait()

    for which in range(2):
        @pl.when(plane == which)
        def _(which=which):
            for copy in writes(which):
                copy.wait()

    remote(out.at[front], swapped, swap_send, swap_recv, peer).wait_send()
    for b in range(TOKENS // BLOCK):
        @pl.when(plane == 0)
        def _(b=b):
            ahead(b).wait_send()

        @pl.when(plane == 1)
        def _(b=b):
            behind(b).wait_send()

    for n, (source, place, _, _) in enumerate(norm_copies):
        remote(source, place, norm_send.at[n], norm_recv.at[n], partner).wait_send()
    wait_weights_sent(0)
    wait_weights_sent(1)


def run_layer(lines, inputs, first, second, segments, joint, mixing, gated, down, gain, bias):
    sems = lambda *s: pltpu.SemaphoreType.DMA(s)
    half = TOKENS // 2
    copies = 2 + 3 * CHUNKS
    ring = sems(RING)
    any_spec, vmem = pl.BlockSpec(memory_space=pl.ANY), pl.BlockSpec(memory_space=pltpu.VMEM)
    rows_out = jax.ShapeDtypeStruct((half, D), BF)
    pieces = jax.ShapeDtypeStruct((PIECES, PIECE, WIDTH), BF)
    paired = jax.ShapeDtypeStruct((PIECES // 2 * PIECE, 2 * WIDTH), BF)
    block = jax.ShapeDtypeStruct((SMALL, D), F32)
    tokens, hiddens = pltpu.VMEM((TOKENS, D), BF), pltpu.VMEM((TOKENS, FF), BF)
    return pl.pallas_call(
        functools.partial(layer_kernel, lines),
        out_shape=[rows_out] * 4 + [paired] * 2 + [pieces] + [block] * 2,
        in_specs=[any_spec] * 3 + [vmem] + [any_spec] * 6,
        out_specs=[any_spec] * 9,
        scratch_shapes=[
            pltpu.VMEM((D, 3 * D), BF), pltpu.VMEM((D, D), BF), pltpu.VMEM((D, 2 * FF), BF), pltpu.VMEM((FF, D), BF),
            pltpu.VMEM((2, 2, 1, D), F32),
            tokens, tokens, tokens, pltpu.VMEM((half, D), BF), tokens, tokens,
            pltpu.VMEM((TOKENS, 3 * D), BF),
            pltpu.VMEM((TOKENS // BLOCK * PAIRS, 2 * BLOCK, BLOCK), F32),
            tokens, hiddens, hiddens, hiddens, pltpu.VMEM((TOKENS, 2 * FF), BF),
            tokens, tokens, pltpu.VMEM((TOKENS, D), F32), pltpu.VMEM((TOKENS, D), F32),
            pltpu.VMEM((TOKENS // BLOCK, BLOCK, BLOCK), F32), pltpu.VMEM((TOKENS, BLOCK), F32),
            pltpu.VMEM((ROWS, D), F32), pltpu.VMEM((5, SMALL, D), F32), pltpu.VMEM((5, SMALL, D), F32),
            pltpu.VMEM((ROWS, D), BF), pltpu.VMEM((2, D, D), BF), pltpu.VMEM((RING, RAIL, WIDTH), BF),
            sems(6), sems(copies), sems(copies), sems(copies), sems(2), sems(2), sems(2),
            sems(4), sems(4), sems(4), sems(4), pltpu.SemaphoreType.DMA, pltpu.SemaphoreType.DMA, sems(6),
            sems(2), sems(2), sems(TILES - 2), pltpu.SemaphoreType.REGULAR,
            sems(AHEAD + 1), sems(AHEAD + 1), ring, sems(5), sems(6), ring, ring, ring, sems(2, RING),
            ring, ring, ring, ring, ring, ring, ring, ring, ring,
        ],
        compiler_params=pltpu.CompilerParams(collective_id=2, has_side_effects=True, vmem_limit_bytes=62 * 2**20),
    )(inputs, first, second, segments, joint, mixing, gated, down, gain, bias)


def place_kernel(
    pieces_ref, small_ref, other_ref, first_ref, second_ref, input_ref, middle_ref,
    first_out, second_out, input_out, middle_out, joint_out, mixing_out, gated_out, down_out, gain_out, bias_out, stats_out,
    held, wide, passed, load_sem, store_sem, pass_sem,
):
    section = lax.axis_index("section")
    plane, core = lax.div(section, 2), lax.rem(section, 2)
    loads = [pltpu.make_async_copy(pieces_ref.at[p], held.at[p], load_sem.at[p]) for p in range(PIECES)]
    for load in loads:
        load.start()
    pairs = ((first_ref, first_out), (second_ref, second_out), (input_ref, input_out), (middle_ref, middle_out))
    takes = [pltpu.make_async_copy(a, passed.at[n], pass_sem.at[n]) for n, (a, _) in enumerate(pairs)]
    passes = [pltpu.make_async_copy(passed.at[n], b, pass_sem.at[4 + n]) for n, (_, b) in enumerate(pairs)]
    for copy in takes:
        copy.start()

    def place(piece):
        if piece < 8:
            return down_out.at[pl.ds(piece // 2 * PIECE, PIECE), pl.ds(piece % 2 * WIDTH, WIDTH)]
        if piece < 24:
            return gated_out.at[:, pl.ds((piece - 8) * WIDTH, WIDTH)]
        if piece < 30:
            return joint_out.at[:, pl.ds((piece - 24) * WIDTH, WIDTH)]
        return mixing_out.at[:, pl.ds((piece - 30) * WIDTH, WIDTH)]

    stores = [pltpu.make_async_copy(wide.at[p % SLOTS], place(p), store_sem.at[p % SLOTS]) for p in range(PIECES)]
    for p in range(PIECES):
        loads[p].wait()
        if p >= SLOTS:
            stores[p - SLOTS].wait()
        wide[p % SLOTS] = held[p].astype(F32)
        stores[p].start()

    for take, copy in zip(takes, passes):
        take.wait()
        copy.start()

    gain_out[...] = small_ref[pl.ds(2 * core, 1), :]
    bias_out[...] = small_ref[pl.ds(2 * core + 1, 1), :]
    count = small_ref[8:9, :1] * D
    row = lax.broadcasted_iota(jnp.int32, (2, 4), 0)
    lane = lax.broadcasted_iota(jnp.int32, (2, 4), 1)
    stats = jnp.zeros((2, 4), F32)
    for n in range(4):
        for at, source in ((2 * plane, small_ref), (2 - 2 * plane, other_ref)):
            value = jnp.sum(source[4 + n : 5 + n, :], axis=1, keepdims=True) / count
            stats = jnp.where((row == n // 2) & (lane == at + n % 2), jnp.sqrt(value), stats)
    stats_out[...] = stats
    for p in range(PIECES - SLOTS, PIECES):
        stores[p].wait()
    for copy in passes:
        copy.wait()


def place_results(pieces, small, other, *rows):
    any_spec, vmem = pl.BlockSpec(memory_space=pl.ANY), pl.BlockSpec(memory_space=pltpu.VMEM)
    shapes = ((HALF, 3 * D), (HALF, D), (HALF, 2 * FF), (FF // 2, D), (1, D), (1, D), (2, 4))
    return pl.pallas_call(
        place_kernel,
        out_shape=[jax.ShapeDtypeStruct(r.shape, BF) for r in rows] + [jax.ShapeDtypeStruct(s, F32) for s in shapes],
        in_specs=[any_spec, vmem, vmem] + [any_spec] * 4,
        out_specs=[any_spec] * 8 + [vmem] * 3,
        scratch_shapes=[
            pltpu.VMEM((PIECES, PIECE, WIDTH), BF), pltpu.VMEM((SLOTS, PIECE, WIDTH), F32),
            pltpu.VMEM((4,) + rows[0].shape, BF),
            pltpu.SemaphoreType.DMA((PIECES,)), pltpu.SemaphoreType.DMA((SLOTS,)), pltpu.SemaphoreType.DMA((8,)),
        ],
        compiler_params=pltpu.CompilerParams(vmem_limit_bytes=61 * 2**20),
    )(pieces, small, other, *rows)


def per_device(
    inputs, cotangent_first, cotangent_second, segment_ids,
    joint_projection, mixing_weight, gated_weight, down_weight, norm_gain, norm_bias,
):
    segments = segment_ids.reshape(-1, BLOCK)
    *rows, _, _, pieces, small, other = run_layer(
        lax.axis_size("dp") // 2, inputs, cotangent_first, cotangent_second, segments,
        joint_projection, mixing_weight, gated_weight, down_weight, norm_gain, norm_bias,
    )
    return tuple(place_results(pieces, small, other, *rows))


def solution(mesh):
    tokens, rows = P("dp", None), P("section", None)
    return jax.shard_map(
        per_device,
        mesh=mesh,
        in_specs=(tokens, tokens, tokens, P("dp"), rows, rows, rows, rows, rows, rows),
        out_specs=(P(("dp", "section"), None),) * 4 + (rows,) * 6 + (P(),),
        check_vma=False,
    )
```
